32 devices in a mesh: frm: 8 (over z, core), col: 4 (over y, x).
Axes of the slice: x: 2, y: 2, z: 4, core: 2. Of those that a mesh axis runs over, the one named last changes fastest.
Arguments:
- video: bfloat16 [64, 8, 128, 512], P('frm', None, 'col'), may hold values from -6 to 6
- norm_gain: float32 [512], replicated, may hold values from 0.25 to 1.75
- w_query: bfloat16 [512, 512], replicated, may hold values from -1 to 1
- w_key: bfloat16 [512, 512], replicated, may hold values from -1 to 1
- w_value: bfloat16 [512, 512], replicated, may hold values from -0.25 to 0.25
- w_out: bfloat16 [512, 512], replicated, may hold values from -0.25 to 0.25
- w_time: bfloat16 [3, 512, 512], replicated, may hold values from -0.15625 to 0.15625
- w_depth: float32 [3, 3, 512], replicated, may hold values from -2 to 2
Outputs:
- encoded: bfloat16 [32, 8, 128, 512], P('frm', None, 'col')
The draws below stay inside these ranges and needn't reach their ends.
All inputs are finite; a program needn't handle non-finite values.
Results may differ from the reference program's by a relative error of at most 0.012.
The reference program's roundings to bfloat16 on the way (of `normed`, `queries`, `key_proj`, `values`, `weights`, `attended`, `mixed_rows` and `activated`) count: a program that leaves them out, or rounds other values in their place, can miss the bound.
Values may be sent and summed in bfloat16 or wider, within the bound.
No kernel may reach another device: no remote copies, remote signals or barrier semaphores. Data moves between devices by JAX's collectives and lax.ppermute only.
A program may use at most 64 MiB of HBM per device.

```python
import math
import jax
import jax.numpy as jnp
from jax import lax

CHAN = 512
FRAMES = 64
VIDEOS = 1
FRAMES_OUT = 32
HEIGHT = 8
WIDTH = 128


def pair_weights(key):
    base = jax.random.fold_in(key, 7)
    first_key, second_key = jax.random.split(base, 2)
    scale = CHAN ** (-0.5)
    first = jnp.clip(jax.random.normal(first_key, (CHAN, CHAN), jnp.float32), -6.0, 6.0) * scale
    second = jnp.clip(jax.random.normal(second_key, (CHAN, CHAN), jnp.float32), -6.0, 6.0) * scale
    return (first, second)


def draw_w_query(key, part):
    return pair_weights(key)[0].astype(jnp.bfloat16)


def draw_w_key(key, part):
    return pair_weights(key)[1].astype(jnp.bfloat16)


def level_of(own_key, dims, pieces, low, high):
    loudness = 1.0
    for position, parts in pieces:
        heights = jax.random.uniform(jax.random.fold_in(jax.random.fold_in(own_key, 6), position), (parts,), jnp.float32, low / len(pieces), high / len(pieces))
        loudness = loudness * jnp.repeat(jnp.exp(heights), dims[position] // parts).reshape((-1,) + (1,) * (len(dims) - 1 - position))
    return loudness


def centred(stream_key, shape, width, bound, pieces=(), dtype=jnp.bfloat16):
    level = level_of(stream_key, shape, pieces, -0.22, 0.18) if pieces else 1.0
    entries = jax.random.normal(stream_key, shape, jnp.float32) * width * level
    return jnp.minimum(jnp.maximum(entries, -bound), bound).astype(dtype)


def setup_inputs(seed: int = 0) -> dict:
    streams_of = jax.random.split(jax.random.key(seed), 9)
    video = centred(streams_of[0], (VIDEOS * FRAMES, HEIGHT, WIDTH, CHAN), 1.0, 6.0, ((0, 8), (2, 4)))
    norm_gain = jnp.clip(1.0 + 0.15 * jax.random.normal(streams_of[1], (CHAN,), jnp.float32), 0.25, 1.75)
    w_query = draw_w_query(jax.random.fold_in(streams_of[8], 71), 0)
    w_key = draw_w_key(jax.random.fold_in(streams_of[8], 71), 0)
    w_value = centred(streams_of[4], (CHAN, CHAN), CHAN ** -0.5, 0.25)
    w_out = centred(streams_of[5], (CHAN, CHAN), CHAN ** -0.5, 0.25)
    w_time = centred(streams_of[6], (3, CHAN, CHAN), (3 * CHAN) ** -0.5, 0.15625)
    w_depth = centred(streams_of[7], (3, 3, CHAN), 9 ** -0.5, 2.0, (), jnp.float32)
    return dict(video=video, norm_gain=norm_gain, w_query=w_query, w_key=w_key, w_value=w_value, w_out=w_out, w_time=w_time, w_depth=w_depth)


epsilon = 1e-06

def attend_row(row_slab, norm_gain, w_query, w_key, w_value, w_out):
    channels = row_slab.shape[-1]
    widened = row_slab.reshape(-1, channels).astype(jnp.float32)
    normed = (widened * lax.rsqrt(lax.optimization_barrier(jnp.mean(widened * widened, axis=-1, keepdims=True)) + epsilon) * norm_gain).astype(jnp.bfloat16)
    grid_shape = (VIDEOS, FRAMES, -1, channels)
    queries = jnp.dot(normed, w_query, preferred_element_type=jnp.float32).astype(jnp.bfloat16).reshape(grid_shape)
    key_proj = jnp.dot(normed, w_key, preferred_element_type=jnp.float32).astype(jnp.bfloat16).reshape(grid_shape)
    values = jnp.dot(normed, w_value, preferred_element_type=jnp.float32).astype(jnp.bfloat16).reshape(grid_shape)
    scores = jnp.einsum('bqpc,bkpc->bpqk', queries.astype(jnp.float32), key_proj.astype(jnp.float32)) / math.sqrt(channels)
    causal = jnp.arange(FRAMES)[:, None] >= jnp.arange(FRAMES)[None, :]
    scores = jnp.where(causal, scores, -1e+30)
    raised = jnp.exp(scores - lax.optimization_barrier(jnp.max(scores, axis=-1, keepdims=True)))
    weights = (raised / lax.optimization_barrier(jnp.sum(raised, axis=-1, keepdims=True))).astype(jnp.bfloat16)
    attended = jnp.einsum('bpqk,bkpc->bqpc', weights.astype(jnp.float32), values.astype(jnp.float32)).astype(jnp.bfloat16)
    projected = jnp.dot(attended.reshape(-1, channels), w_out, preferred_element_type=jnp.float32)
    return (widened + projected).astype(jnp.bfloat16).reshape(row_slab.shape)

def time_conv(prior_frames, even_frames, odd_frames, w_time):
    channels = even_frames.shape[-1]
    summed = jnp.dot(prior_frames.reshape(-1, channels), w_time[0], preferred_element_type=jnp.float32)
    summed = summed + jnp.dot(even_frames.reshape(-1, channels), w_time[1], preferred_element_type=jnp.float32)
    summed = summed + jnp.dot(odd_frames.reshape(-1, channels), w_time[2], preferred_element_type=jnp.float32)
    return jax.nn.silu(summed).astype(jnp.bfloat16).reshape(even_frames.shape)

def reference(video, norm_gain, w_query, w_key, w_value, w_out, w_time, w_depth):
    channels = video.shape[-1]
    rows_first = jnp.moveaxis(video, 1, 0)

    def per_row(row_slab):
        mixed_rows = attend_row(row_slab, norm_gain, w_query, w_key, w_value, w_out)
        grouped = mixed_rows.reshape(VIDEOS, FRAMES, -1, channels)
        even_frames = grouped[:, 0::2]
        odd_frames = grouped[:, 1::2]
        prior_frames = jnp.concatenate([grouped[:, :1], odd_frames[:, :-1]], axis=1)
        return time_conv(prior_frames, even_frames, odd_frames, w_time).reshape(VIDEOS * FRAMES_OUT, -1, channels)
    activated = jnp.moveaxis(lax.map(per_row, rows_first), 0, 1)

    def per_frame(frame):
        rows = frame.shape[0]
        cols = frame.shape[1]
        padded = jnp.pad(frame.astype(jnp.float32), ((1, 1), (1, 1), (0, 0)))
        summed = jnp.zeros(frame.shape, jnp.float32)
        for row_step in range(3):
            for col_step in range(3):
                summed = summed + padded[row_step:row_step + rows, col_step:col_step + cols] * w_depth[row_step, col_step]
        return summed.astype(jnp.bfloat16)
    return lax.map(per_frame, activated)
```

```python
import functools
import math

import jax
import jax.numpy as jnp
from jax import lax
from jax.experimental import pallas as pl
from jax.experimental.pallas import tpu as pltpu
from jax.sharding import PartitionSpec as P

epsilon = 1e-06
GROUP = 8
MEMORY = 56 * 1024 * 1024


def attend_group(x, gain, w_query, w_key, w_value, w_out, w_time, frames):
    channels = x.shape[-1]
    rows = frames * GROUP
    x = x.reshape(rows, channels)
    normed = (x * lax.rsqrt(jnp.mean(x * x, axis=-1, keepdims=True) + epsilon) * gain).astype(jnp.bfloat16)

    def project(weight):
        return jnp.dot(normed, weight[...], preferred_element_type=jnp.float32).astype(jnp.bfloat16)

    queries, key_proj, values = project(w_query), project(w_key), project(w_value)
    blocks = 2
    height = rows // blocks
    mixed = []
    for block in range(blocks):
        begin = block * height
        span = begin + height
        scores = lax.dot_general(
            queries[begin:span],
            key_proj[:span],
            (((1,), (1,)), ((), ())),
            preferred_element_type=jnp.float32,
        ) * (1.0 / math.sqrt(channels))
        to_row = lax.broadcasted_iota(jnp.int32, scores.shape, 0) + begin
        from_row = lax.broadcasted_iota(jnp.int32, scores.shape, 1)
        allowed = (from_row <= to_row) & (lax.rem(from_row, GROUP) == lax.rem(to_row, GROUP))
        scores = jnp.where(allowed, scores, -1e30)
        raised = jnp.exp(scores - jnp.max(scores, axis=-1, keepdims=True))
        weights = (raised / jnp.sum(raised, axis=-1, keepdims=True)).astype(jnp.bfloat16)
        attended = jnp.dot(weights, values[:span], preferred_element_type=jnp.float32).astype(jnp.bfloat16)
        projected = jnp.dot(attended, w_out[...], preferred_element_type=jnp.float32)
        mixed.append(x[begin:span] + projected)
    mixed = jnp.concatenate(mixed, axis=0).reshape(frames // 2, 2, GROUP, channels)
    even = mixed[:, 0]
    odd = mixed[:, 1]
    prior = jnp.concatenate([even[:1], odd[:-1]], axis=0)
    summed = jnp.zeros((rows // 2, channels), jnp.float32)
    for tap, part in enumerate((prior, even, odd)):
        part = part.reshape(rows // 2, channels).astype(jnp.bfloat16)
        summed = summed + jnp.dot(part, w_time[tap], preferred_element_type=jnp.float32)
    return (summed / (1.0 + jnp.exp(-summed))).reshape(frames // 2, GROUP, channels)


def attend_kernel(count, *refs):
    pieces = refs[:count]
    gain, w_query, w_key, w_value, w_out, w_time = refs[count : count + 6]
    results = refs[count + 6 : 2 * count + 6]
    band, done, sems = refs[2 * count + 6 :]
    me = lax.axis_index("frm")
    span = pieces[0].shape[0]
    made = results[0].shape[0]
    copies = [
        pltpu.make_async_copy(pieces[k], band.at[pl.ds((me ^ k) * span, span)], sems.at[k]) for k in range(count)
    ]
    for copy in copies:
        copy.start()
    for copy in copies:
        copy.wait()
    frames, cols, channels = band.shape
    x = band[...].astype(jnp.float32)
    parts = [
        attend_group(x[:, g : g + GROUP], gain[...], w_query, w_key, w_value, w_out, w_time, frames)
        for g in range(0, cols, GROUP)
    ]
    done[...] = jnp.concatenate(parts, axis=1).astype(jnp.bfloat16)
    copies = [
        pltpu.make_async_copy(done.at[pl.ds((me ^ k) * made, made)], results[k], sems.at[k]) for k in range(count)
    ]
    for copy in copies:
        copy.start()
    for copy in copies:
        copy.wait()


def attend(pieces, norm_gain, w_query, w_key, w_value, w_out, w_time):
    count = len(pieces)
    span, cols, channels = pieces[0].shape
    frames = span * count
    made = span // 2
    anywhere = pl.BlockSpec(memory_space=pl.ANY)
    inside = pl.BlockSpec(memory_space=pltpu.VMEM)
    rows = frames * cols
    return pl.pallas_call(
        functools.partial(attend_kernel, count),
        out_shape=[jax.ShapeDtypeStruct((made, cols, channels), jnp.bfloat16)] * count,
        in_specs=[anywhere] * count + [inside] * 6,
        out_specs=[anywhere] * count,
        scratch_shapes=[
            pltpu.VMEM((frames, cols, channels), jnp.bfloat16),
            pltpu.VMEM((frames // 2, cols, channels), jnp.bfloat16),
            pltpu.SemaphoreType.DMA((count,)),
        ],
        compiler_params=pltpu.CompilerParams(vmem_limit_bytes=MEMORY),
        cost_estimate=pl.CostEstimate(
            flops=rows * channels * (channels * 11 + GROUP * frames * 4),
            bytes_accessed=rows * channels * 3 + channels * channels * 14,
            transcendentals=rows * frames,
        ),
        name="attend",
    )(*pieces, norm_gain[None], w_query, w_key, w_value, w_out, w_time)


def filter_kernel(count, *refs):
    outer = refs[:count]
    inner = refs[count : 2 * count]
    left, right, w_depth, out, outer_rows, inner_rows, sems = refs[2 * count :]
    me = lax.axis_index("frm")
    copies = []
    for k in range(count):
        copies.append(pltpu.make_async_copy(outer[k], outer_rows.at[me ^ k], sems.at[2 * k]))
        copies.append(pltpu.make_async_copy(inner[k], inner_rows.at[me ^ k], sems.at[2 * k + 1]))
    for copy in copies:
        copy.start()
    for copy in copies:
        copy.wait()
    frames, height, cols, channels = out.shape
    edge = outer_rows.shape[2] // 2
    lanes = 128

    def one_part(step, carry):
        part = pl.ds(pl.multiple_of(step * lanes, lanes), lanes)
        for frame in range(frames):
            taps = [[w_depth[a, b, part] for b in range(3)] for a in range(3)]

            def filtered(row):
                rim = outer_rows[row, frame, :, part].astype(jnp.float32)
                core = inner_rows[row, frame, :, part].astype(jnp.float32)
                mid = jnp.concatenate([rim[:edge], core, rim[edge:]], axis=0)
                place = lax.broadcasted_iota(jnp.int32, mid.shape, 0)
                low = left[me ^ row, frame, part].astype(jnp.float32)[None]
                high = right[me ^ row, frame, part].astype(jnp.float32)[None]
                before = jnp.where(place == 0, low, pltpu.roll(mid, 1, 0))
                after = jnp.where(place == cols - 1, high, pltpu.roll(mid, cols - 1, 0))
                return [
                    before * taps[a][0][None] + mid * taps[a][1][None] + after * taps[a][2][None] for a in range(3)
                ]

            above = None
            here = filtered(0)
            for row in range(height):
                below = filtered(row + 1) if row + 1 < height else None
                total = here[1]
                if above is not None:
                    total = total + above[0]
                if below is not None:
                    total = total + below[2]
                out[frame, row, :, part] = total.astype(jnp.bfloat16)
                above, here = here, below
        return carry

    lax.fori_loop(0, channels // lanes, one_part, 0)


def depth_filter(outer, inner, left, right, w_depth):
    count = len(outer)
    frames, width, channels = outer[0].shape
    cols = 2 * width
    anywhere = pl.BlockSpec(memory_space=pl.ANY)
    inside = pl.BlockSpec(memory_space=pltpu.VMEM)
    size = frames * count * cols * channels
    return pl.pallas_call(
        functools.partial(filter_kernel, count),
        out_shape=jax.ShapeDtypeStruct((frames, count, cols, channels), jnp.bfloat16),
        in_specs=[anywhere] * (2 * count) + [inside] * 3,
        out_specs=inside,
        scratch_shapes=[
            pltpu.VMEM((count, frames, width, channels), jnp.bfloat16),
            pltpu.VMEM((count, frames, width, channels), jnp.bfloat16),
            pltpu.SemaphoreType.DMA((2 * count,)),
        ],
        compiler_params=pltpu.CompilerParams(vmem_limit_bytes=MEMORY),
        cost_estimate=pl.CostEstimate(flops=18 * size, bytes_accessed=4 * size, transcendentals=0),
        name="depth_filter",
    )(*outer, *inner, left, right, w_depth)


def swap(block, k, count):
    if k == 0:
        return block
    return lax.ppermute(block, "frm", [(i, i ^ k) for i in range(count)])


def local(video, norm_gain, w_query, w_key, w_value, w_out, w_time, w_depth):
    count = lax.axis_size("frm")
    me = lax.axis_index("frm")
    frames, height, cols, channels = video.shape
    assert height == count and count & (count - 1) == 0
    edge = cols // 4
    weights = (norm_gain, w_query, w_key, w_value, w_out, w_time)
    order = sorted(range(count), key=lambda k: -k)

    def forward(cut):
        return {k: swap(cut(lax.dynamic_index_in_dim(video, me ^ k, 1, keepdims=False)), k, count) for k in order}

    def back(pieces):
        results = attend([pieces[k] for k in range(count)], *weights)
        return {k: swap(results[k], k, count) for k in order}

    outer = forward(lambda row: jnp.concatenate([row[:, :edge], row[:, cols - edge :]], axis=1))
    inner = forward(lambda row: row[:, edge : cols - edge])
    outer = back(outer)
    outer = [outer[k] for k in range(count)]
    line = lax.axis_size("col")
    upward = [(i, i + 1) for i in range(line - 1)]
    left = lax.ppermute(jnp.stack([piece[:, 2 * edge - 1] for piece in outer]), "col", upward)
    right = lax.ppermute(jnp.stack([piece[:, 0] for piece in outer]), "col", [(b, a) for a, b in upward])
    inner = back(inner)
    inner = [inner[k] for k in range(count)]
    return depth_filter(outer, inner, left, right, w_depth)


def solution(mesh):
    return jax.shard_map(
        local,
        mesh=mesh,
        in_specs=(P("frm", None, "col", None), P(), P(), P(), P(), P(), P(), P()),
        out_specs=P("frm", None, "col", None),
        check_vma=False,
    )
```

```python
import functools
import math

import jax
import jax.numpy as jnp
from jax import lax
from jax.experimental import pallas as pl
from jax.experimental.pallas import tpu as pltpu
from jax.sharding import PartitionSpec as P

epsilon = 1e-06
GROUP = 8
BLOCKS = 2
MIB = 1024 * 1024
ANYWHERE = pl.BlockSpec(memory_space=pl.ANY)
INSIDE = pl.BlockSpec(memory_space=pltpu.VMEM)


def place():
    me = lax.axis_index("frm")
    return me // 2, me % 2


def gather_kernel(pairs_of, n_in, *refs):
    *arrays, sems = refs
    pairs = pairs_of(arrays[:n_in], arrays[n_in:])
    copies = [pltpu.make_async_copy(source, target, sems.at[i]) for i, (source, target) in enumerate(pairs)]
    for copy in copies:
        copy.start()
    for copy in copies:
        copy.wait()


def gather(pairs_of, n_pairs, arrays, shapes, name):
    size = sum(math.prod(shape) for shape in shapes)
    return pl.pallas_call(
        functools.partial(gather_kernel, pairs_of, len(arrays)),
        out_shape=[jax.ShapeDtypeStruct(shape, jnp.bfloat16) for shape in shapes],
        in_specs=[ANYWHERE] * len(arrays),
        out_specs=[INSIDE] * len(shapes),
        scratch_shapes=[pltpu.SemaphoreType.DMA((n_pairs,))],
        compiler_params=pltpu.CompilerParams(vmem_limit_bytes=4 * MIB),
        cost_estimate=pl.CostEstimate(flops=0, bytes_accessed=4 * size, transcendentals=0),
        name=name,
    )(*arrays)


def cut_kernel(order, rim, video, *refs):
    *results, held, sems = refs
    if not rim:
        results = results[:-1] + [results[-1].at[k] for k in range(len(results) - 1)]
    row_of = order(lax.axis_index("frm"))
    edge = held.shape[2] // 4
    copies = [pltpu.make_async_copy(video.at[:, row], held.at[i], sems.at[i]) for i, row in enumerate(row_of)]
    for copy in copies:
        copy.start()
    for i, (copy, result) in enumerate(zip(copies, results)):
        copy.wait()
        row = held[i].astype(jnp.float32)
        if rim:
            row = jnp.concatenate([row[:, :edge], row[:, 3 * edge :]], axis=1)
        else:
            row = row[:, edge : 3 * edge]
        result[...] = row.astype(jnp.bfloat16)


def cut(order, rim, video, name):
    span, height, cols, channels = video.shape
    shape = (span, cols // 2, channels)
    shapes = [shape] * height if rim else [shape] * (height // 2) + [(height // 2, *shape)]
    return pl.pallas_call(
        functools.partial(cut_kernel, order, rim),
        out_shape=[jax.ShapeDtypeStruct(shape, jnp.bfloat16) for shape in shapes],
        in_specs=[ANYWHERE],
        out_specs=[INSIDE] * len(shapes),
        scratch_shapes=[
            pltpu.VMEM((height, span, cols, channels), jnp.bfloat16),
            pltpu.SemaphoreType.DMA((height,)),
        ],
        compiler_params=pltpu.CompilerParams(vmem_limit_bytes=10 * MIB),
        cost_estimate=pl.CostEstimate(flops=0, bytes_accessed=3 * video.size, transcendentals=0),
        name=name,
    )(video)


def stacked(x):
    return jnp.stack([x[:, g : g + GROUP] for g in range(0, x.shape[1], GROUP)])


def attend_frames(x, gain, bias, weights, ready):
    w_query, w_key, w_value, w_out, w_time = weights
    groups, frames, _, channels = x.shape
    rows = frames * GROUP
    x = x.reshape(groups * rows, channels)
    normed = (x * lax.rsqrt(jnp.mean(x * x, axis=-1, keepdims=True) + epsilon) * gain).astype(jnp.bfloat16)

    def project(index):
        ready(index)
        return jnp.dot(normed, weights[index][...], preferred_element_type=jnp.float32).astype(jnp.bfloat16)

    queries, key_proj, values = project(0), project(1), project(2)
    height = rows // BLOCKS
    attended = []
    for group in range(groups):
        first = group * rows
        for block in range(BLOCKS):
            begin = block * height
            span = begin + height
            scores = lax.dot_general(
                queries[first + begin : first + span],
                key_proj[first : first + span],
                (((1,), (1,)), ((), ())),
                preferred_element_type=jnp.float32,
            )
            scores = scores * (1.0 / math.sqrt(channels)) + bias[begin:span, :span]
            raised = jnp.exp(scores - jnp.max(scores, axis=-1, keepdims=True))
            shares = (raised * (1.0 / jnp.sum(raised, axis=-1, keepdims=True))).astype(jnp.bfloat16)
            attended.append(
                jnp.dot(shares, values[first : first + span], preferred_element_type=jnp.float32).astype(jnp.bfloat16)
            )
    ready(3)
    mixed = x + jnp.dot(jnp.concatenate(attended, axis=0), w_out[...], preferred_element_type=jnp.float32)
    mixed = mixed.reshape(groups, frames // 2, 2, GROUP, channels)
    even = mixed[:, :, 0]
    odd = mixed[:, :, 1]
    prior = jnp.concatenate([even[:, :1], odd[:, :-1]], axis=1)
    ready(4)
    summed = None
    for tap, part in enumerate((prior, even, odd)):
        part = part.reshape(groups * rows // 2, channels).astype(jnp.bfloat16)
        term = jnp.dot(part, w_time[tap], preferred_element_type=jnp.float32)
        summed = term if summed is None else summed + term
    return (summed / (1.0 + jnp.exp(-summed))).reshape(groups, frames // 2, GROUP, channels)


def attend_kernel(inward, n_in, chips, with_tail, *refs):
    pieces = refs[:n_in]
    gain = refs[n_in]
    sources = refs[n_in + 1 : n_in + 6]
    rest = refs[n_in + 6 :]
    if with_tail:
        tail, out, band, bias, *held, sems, weight_sems, tail_sem = rest
    else:
        results = rest[:chips]
        low, high, band, out, bias, *held, sems, weight_sems = rest[chips:]
    fetches = [pltpu.make_async_copy(s, h, weight_sems.at[i]) for i, (s, h) in enumerate(zip(sources, held))]
    waited = set()

    def ready(index):
        if index not in waited:
            waited.add(index)
            fetches[index].wait()

    copies = [
        pltpu.make_async_copy(piece, band.at[pl.ds(first, piece.shape[0])], sems.at[i])
        for i, (piece, first) in enumerate(inward(pieces))
    ]
    for copy in copies + fetches:
        copy.start()
    count, block, _ = out.shape
    frames, cols, channels = band.shape
    body = frames * cols // (2 * count)
    if with_tail:
        tail_copy = pltpu.make_async_copy(tail, out.at[:, pl.ds(body, block - body)], tail_sem)
        tail_copy.start()
    to_row = lax.broadcasted_iota(jnp.int32, bias.shape, 0)
    from_row = lax.broadcasted_iota(jnp.int32, bias.shape, 1)
    allowed = (from_row <= to_row) & (lax.rem(from_row, GROUP) == lax.rem(to_row, GROUP))
    bias[...] = jnp.where(allowed, 0.0, -1e30)
    for copy in copies:
        copy.wait()
    made = attend_frames(stacked(band[...].astype(jnp.float32)), gain[...], bias, held, ready)
    made = jnp.concatenate([made[g] for g in range(cols // GROUP)], axis=1)
    out[:, :body] = made.astype(jnp.bfloat16).reshape(count, body, channels)
    if with_tail:
        tail_copy.wait()
    else:
        chip = lax.axis_index("frm") // 2
        copies = [
            pltpu.make_async_copy(out.at[pl.ds(2 * (chip ^ k), 2)], result, sems.at[k])
            for k, result in enumerate(results)
        ]
        for copy in copies:
            copy.start()
        low[...] = made[:, 0].astype(jnp.bfloat16)
        high[...] = made[:, cols - 1].astype(jnp.bfloat16)
        for copy in copies:
            copy.wait()


def attend(inward, n_copies, pieces, weights, count, frames, name, tail=None):
    cols, channels = pieces[0].shape[-2:]
    rows = frames * cols
    body = rows // (2 * count)
    norm_gain, *matrices = weights
    with_tail = tail is not None
    chips = count // 2
    shapes = (
        [(count, body + tail.shape[1], channels)]
        if with_tail
        else [(2, body, channels)] * chips + [(frames // 2, channels)] * 2
    )
    return pl.pallas_call(
        functools.partial(attend_kernel, inward, len(pieces), chips, with_tail),
        out_shape=[jax.ShapeDtypeStruct(shape, jnp.bfloat16) for shape in shapes],
        in_specs=[ANYWHERE] * len(pieces) + [INSIDE] + [ANYWHERE] * (5 + with_tail),
        out_specs=[INSIDE] if with_tail else [ANYWHERE] * chips + [INSIDE] * 2,
        scratch_shapes=[
            pltpu.VMEM((frames, cols, channels), jnp.bfloat16),
            *([] if with_tail else [pltpu.VMEM((count, body, channels), jnp.bfloat16)]),
            pltpu.VMEM((frames * GROUP, frames * GROUP), jnp.float32),
            *[pltpu.VMEM(matrix.shape, jnp.bfloat16) for matrix in matrices],
            pltpu.SemaphoreType.DMA((n_copies,)),
            pltpu.SemaphoreType.DMA((5,)),
            *([pltpu.SemaphoreType.DMA(())] if with_tail else []),
        ],
        compiler_params=pltpu.CompilerParams(vmem_limit_bytes=20 * MIB),
        cost_estimate=pl.CostEstimate(
            flops=rows * channels * (channels * 11 + GROUP * frames * 4),
            bytes_accessed=rows * channels * 3 + channels * channels * 14,
            transcendentals=rows * frames,
        ),
        name=name,
    )(*pieces, norm_gain[None], *matrices, *([tail] if with_tail else []))


def filter_kernel(chips, *refs):
    pieces = refs[:chips]
    other, inner, w_depth, out, outer, sems = refs[chips:]
    me = lax.axis_index("frm")
    chip, core = me // 2, me % 2
    copies = []
    for k in range(chips):
        row = 2 * (chip ^ k)
        copies.append(pltpu.make_async_copy(pieces[k].at[core], outer.at[row + core], sems.at[2 * k]))
        copies.append(pltpu.make_async_copy(other.at[k], outer.at[row + 1 - core], sems.at[2 * k + 1]))
    for copy in copies:
        copy.start()
    for copy in copies:
        copy.wait()
    frames, height, cols, channels = out.shape
    width = cols // 2
    edge = width // 2
    body = frames * width
    lanes = 128

    def one_part(step, carry):
        part = pl.ds(pl.multiple_of(step * lanes, lanes), lanes)
        taps = [[w_depth[a, b, part] for b in range(3)] for a in range(3)]
        for frame in range(frames):
            begin = frame * width

            def filtered(row):
                rim = outer[row, begin : begin + width, part].astype(jnp.float32)
                core = inner[row, begin : begin + width, part].astype(jnp.float32)
                mid = jnp.concatenate([rim[:edge], core, rim[edge:]], axis=0)
                spot = lax.broadcasted_iota(jnp.int32, mid.shape, 0)
                low = inner[row, body + frame, part].astype(jnp.float32)[None]
                high = inner[row, body + frames + frame, part].astype(jnp.float32)[None]
                before = jnp.where(spot == 0, low, pltpu.roll(mid, 1, 0))
                after = jnp.where(spot == cols - 1, high, pltpu.roll(mid, cols - 1, 0))
                return [
                    before * taps[a][0][None] + mid * taps[a][1][None] + after * taps[a][2][None] for a in range(3)
                ]

            above = None
            here = filtered(0)
            for row in range(height):
                below = filtered(row + 1) if row + 1 < height else None
                total = here[1]
                if above is not None:
                    total = total + above[0]
                if below is not None:
                    total = total + below[2]
                out[frame, row, :, part] = total.astype(jnp.bfloat16)
                above, here = here, below
        return carry

    lax.fori_loop(0, channels // lanes, one_part, 0)


def depth_filter(outer, other, inner, w_depth, frames, cols):
    chips, body, channels = other.shape
    height = 2 * chips
    size = frames * height * cols * channels
    return pl.pallas_call(
        functools.partial(filter_kernel, chips),
        out_shape=jax.ShapeDtypeStruct((frames, height, cols, channels), jnp.bfloat16),
        in_specs=[ANYWHERE] * (chips + 1) + [INSIDE] * 2,
        out_specs=INSIDE,
        scratch_shapes=[
            pltpu.VMEM((height, body, channels), jnp.bfloat16),
            pltpu.SemaphoreType.DMA((height,)),
        ],
        compiler_params=pltpu.CompilerParams(vmem_limit_bytes=8 * MIB),
        cost_estimate=pl.CostEstimate(flops=18 * size, bytes_accessed=4 * size, transcendentals=0),
        name="depth_filter",
    )(*outer, other, inner, w_depth)


def local(video, norm_gain, w_query, w_key, w_value, w_out, w_time, w_depth):
    count = lax.axis_size("frm")
    chips = count // 2
    span, height, cols, channels = video.shape
    assert height == count and count & (count - 1) == 0
    made = span // 2
    frames = span * count
    edge = cols // 4
    width = 2 * edge
    weights = (norm_gain, w_query, w_key, w_value, w_out, w_time)

    def swap(block, k):
        return lax.ppermute(block, "frm", [(i, i ^ k) for i in range(count)]) if k else block

    early = [k for k in (1, 3) if k < count]
    late = [k for k in (2,) if k < count]
    order = early + [k for k in range(count - 1, 0, -1) if k not in early + late] + late + [0]
    outer = [swap(piece, k) for k, piece in zip(order, cut(lambda me: [me ^ k for k in order], True, video, "cut_outer"))]

    video, outer[0] = lax.optimization_barrier((video, outer[0]))
    far = list(range(chips - 1, 0, -1))
    nearest = list(range(chips))
    *own, other = cut(
        lambda me: [me ^ (2 * k) for k in nearest] + [me ^ (2 * k) ^ 1 for k in nearest], False, video, "cut_inner"
    )
    other = swap(other, 1)

    def pack_inner(ins, outs):
        pairs = []
        for i, k in enumerate(far):
            pairs.append((ins[i], outs[i].at[pl.ds(0, span)]))
            pairs.append((ins[-1].at[k], outs[i].at[pl.ds(span, span)]))
        return pairs

    packed = gather(
        pack_inner,
        2 * len(far),
        [*[own[k] for k in far], other],
        [(2 * span, width, channels)] * len(far),
        "pack_inner",
    )
    outer, packed = lax.optimization_barrier((outer, packed))
    inner = [swap(piece, 2 * k) for k, piece in zip(far, packed)]

    def outer_in(pieces):
        me = lax.axis_index("frm")
        return [(piece, (me ^ k) * span) for k, piece in zip(order, pieces)]

    def inner_in(pieces):
        me = lax.axis_index("frm")
        chip, core = me // 2, me % 2
        pairs = []
        for k, piece in zip(far, pieces):
            pairs.append((piece.at[pl.ds(0, span)], (2 * (chip ^ k) + core) * span))
            pairs.append((piece.at[pl.ds(span, span)], (2 * (chip ^ k) + 1 - core) * span))
        pairs.append((pieces[-2], me * span))
        pairs.append((pieces[-1].at[0], (me ^ 1) * span))
        return pairs

    *outer, low, high = attend(outer_in, count, outer, weights, count, frames, "attend_outer")
    outer = [swap(piece, 2 * k) for k, piece in enumerate(outer)]
    line = lax.axis_size("col")
    upward = [(i, i + 1) for i in range(line - 1)]
    left = lax.ppermute(high, "col", upward).reshape(count, made, channels)
    right = lax.ppermute(low, "col", [(b, a) for a, b in upward]).reshape(count, made, channels)
    spare = -2 * made % 16
    tail = jnp.concatenate([left, right, jnp.zeros((count, spare, channels), jnp.bfloat16)], axis=1)
    (inner,) = attend(inner_in, count, [*inner, own[0], other], weights, count, frames, "attend_inner", tail)
    *outer, inner = lax.optimization_barrier((*outer, inner))

    def pack_back(ins, outs):
        chip, core = place()
        return [(piece.at[1 - core], outs[0].at[k]) for k, piece in enumerate(ins)]

    outer_other = swap(gather(pack_back, chips, outer, [(chips, *outer[0].shape[1:])], "pack_back")[0], 1)
    inner = lax.all_to_all(inner, "frm", split_axis=0, concat_axis=0, tiled=True)
    return depth_filter(outer, outer_other, inner, w_depth, made, cols)


def solution(mesh):
    return jax.shard_map(
        local,
        mesh=mesh,
        in_specs=(P("frm", None, "col", None), P(), P(), P(), P(), P(), P(), P()),
        out_specs=P("frm", None, "col", None),
        check_vma=False,
    )
```

```python
import functools
import math

import jax
import jax.numpy as jnp
from jax import lax
from jax.experimental import pallas as pl
from jax.experimental.pallas import tpu as pltpu
from jax.sharding import PartitionSpec as P

epsilon = 1e-06
GROUP = 8
BLOCKS = 2
MIB = 1024 * 1024
ANYWHERE = pl.BlockSpec(memory_space=pl.ANY)
INSIDE = pl.BlockSpec(memory_space=pltpu.VMEM)


def place():
    me = lax.axis_index("frm")
    return me // 2, me % 2


def gather_kernel(pairs_of, n_in, *refs):
    *arrays, sems = refs
    pairs = pairs_of(arrays[:n_in], arrays[n_in:])
    copies = [pltpu.make_async_copy(source, target, sems.at[i]) for i, (source, target) in enumerate(pairs)]
    for copy in copies:
        copy.start()
    for copy in copies:
        copy.wait()


def gather(pairs_of, n_pairs, arrays, shapes, name):
    size = sum(math.prod(shape) for shape in shapes)
    return pl.pallas_call(
        functools.partial(gather_kernel, pairs_of, len(arrays)),
        out_shape=[jax.ShapeDtypeStruct(shape, jnp.bfloat16) for shape in shapes],
        in_specs=[ANYWHERE] * len(arrays),
        out_specs=[INSIDE] * len(shapes),
        scratch_shapes=[pltpu.SemaphoreType.DMA((n_pairs,))],
        compiler_params=pltpu.CompilerParams(vmem_limit_bytes=4 * MIB),
        cost_estimate=pl.CostEstimate(flops=0, bytes_accessed=4 * size, transcendentals=0),
        name=name,
    )(*arrays)


def cut_kernel(rows_of, video, *refs):
    *results, held, sems = refs
    span, height, cols = held.shape[1], held.shape[0], held.shape[2]
    edge = cols // 4
    copies = [pltpu.make_async_copy(video.at[:, row], held.at[row], sems.at[row]) for row in range(height)]
    for copy in copies:
        copy.start()
    for copy in copies:
        copy.wait()
    half = len(results) // 2
    own, other = rows_of(lax.axis_index("frm"))
    for rim in (True, False):
        *singles, stack = results[:half] if rim else results[half:]
        targets = singles + [stack.at[k] for k in range(stack.shape[0])]
        for row, target in zip(own + other, targets):
            values = held[row].astype(jnp.float32)
            if rim:
                values = jnp.concatenate([values[:, :edge], values[:, 3 * edge :]], axis=1)
            else:
                values = values[:, edge : 3 * edge]
            target[...] = values.astype(jnp.bfloat16)


def cut(rows_of, chips, video):
    span, height, cols, channels = video.shape
    shape = (span, cols // 2, channels)
    shapes = ([shape] * chips + [(chips, *shape)]) * 2
    return pl.pallas_call(
        functools.partial(cut_kernel, rows_of),
        out_shape=[jax.ShapeDtypeStruct(shape, jnp.bfloat16) for shape in shapes],
        in_specs=[ANYWHERE],
        out_specs=[INSIDE] * len(shapes),
        scratch_shapes=[
            pltpu.VMEM((height, span, cols, channels), jnp.bfloat16),
            pltpu.SemaphoreType.DMA((height,)),
        ],
        compiler_params=pltpu.CompilerParams(vmem_limit_bytes=12 * MIB),
        cost_estimate=pl.CostEstimate(flops=0, bytes_accessed=3 * video.size, transcendentals=0),
        name="cut",
    )(video)


def stacked(x):
    return jnp.stack([x[:, g : g + GROUP] for g in range(0, x.shape[1], GROUP)])


def attend_frames(x, gain, bias, weights, ready):
    w_query, w_key, w_value, w_out, w_time = weights
    groups, frames, _, channels = x.shape
    rows = frames * GROUP
    x = x.reshape(groups * rows, channels)
    normed = (x * lax.rsqrt(jnp.mean(x * x, axis=-1, keepdims=True) + epsilon) * gain).astype(jnp.bfloat16)

    def project(index):
        ready(index)
        return jnp.dot(normed, weights[index][...], preferred_element_type=jnp.float32).astype(jnp.bfloat16)

    queries, key_proj, values = project(0), project(1), project(2)
    height = rows // BLOCKS
    attended = []
    for group in range(groups):
        first = group * rows
        for block in range(BLOCKS):
            begin = block * height
            span = begin + height
            scores = lax.dot_general(
                queries[first + begin : first + span],
                key_proj[first : first + span],
                (((1,), (1,)), ((), ())),
                preferred_element_type=jnp.float32,
            )
            scores = scores * (1.0 / math.sqrt(channels)) + bias[begin:span, :span]
            raised = jnp.exp(scores - jnp.max(scores, axis=-1, keepdims=True))
            shares = (raised * (1.0 / jnp.sum(raised, axis=-1, keepdims=True))).astype(jnp.bfloat16)
            attended.append(
                jnp.dot(shares, values[first : first + span], preferred_element_type=jnp.float32).astype(jnp.bfloat16)
            )
    ready(3)
    mixed = x + jnp.dot(jnp.concatenate(attended, axis=0), w_out[...], preferred_element_type=jnp.float32)
    mixed = mixed.reshape(groups, frames // 2, 2, GROUP, channels)
    even = mixed[:, :, 0]
    odd = mixed[:, :, 1]
    prior = jnp.concatenate([even[:, :1], odd[:, :-1]], axis=1)
    ready(4)
    summed = None
    for tap, part in enumerate((prior, even, odd)):
        part = part.reshape(groups * rows // 2, channels).astype(jnp.bfloat16)
        term = jnp.dot(part, w_time[tap], preferred_element_type=jnp.float32)
        summed = term if summed is None else summed + term
    return (summed / (1.0 + jnp.exp(-summed))).reshape(groups, frames // 2, GROUP, channels)


def attend_kernel(inward, n_in, n_out, *refs):
    pieces = refs[:n_in]
    gain = refs[n_in]
    sources = refs[n_in + 1 : n_in + 6]
    results = refs[n_in + 6 : n_in + 6 + n_out]
    band, done, bias, *held, sems, weight_sems = refs[n_in + 6 + n_out :]
    fetches = [pltpu.make_async_copy(s, h, weight_sems.at[i]) for i, (s, h) in enumerate(zip(sources, held))]
    waited = set()

    def ready(index):
        if index not in waited:
            waited.add(index)
            fetches[index].wait()

    copies = [
        pltpu.make_async_copy(piece, band.at[pl.ds(first, piece.shape[0])], sems.at[i])
        for i, (piece, first) in enumerate(inward(pieces))
    ]
    for copy in copies + fetches:
        copy.start()
    to_row = lax.broadcasted_iota(jnp.int32, bias.shape, 0)
    from_row = lax.broadcasted_iota(jnp.int32, bias.shape, 1)
    allowed = (from_row <= to_row) & (lax.rem(from_row, GROUP) == lax.rem(to_row, GROUP))
    bias[...] = jnp.where(allowed, 0.0, -1e30)
    for copy in copies:
        copy.wait()
    made = attend_frames(stacked(band[...].astype(jnp.float32)), gain[...], bias, held, ready)
    done[...] = jnp.concatenate([made[g] for g in range(made.shape[0])], axis=1).astype(jnp.bfloat16)
    chip, _ = place()
    copies = [
        pltpu.make_async_copy(
            done if n_out == 1 else done.at[pl.ds((chip ^ k) * result.shape[0], result.shape[0])], result, sems.at[k]
        )
        for k, result in enumerate(results)
    ]
    for copy in copies:
        copy.start()
    for copy in copies:
        copy.wait()


def attend(inward, n_copies, pieces, weights, frames, n_out, name):
    cols, channels = pieces[0].shape[-2:]
    rows = frames * cols
    made = frames // 2
    norm_gain, *matrices = weights
    return pl.pallas_call(
        functools.partial(attend_kernel, inward, len(pieces), n_out),
        out_shape=[jax.ShapeDtypeStruct((made // n_out, cols, channels), jnp.bfloat16)] * n_out,
        in_specs=[ANYWHERE] * len(pieces) + [INSIDE] + [ANYWHERE] * 5,
        out_specs=[ANYWHERE] * n_out,
        scratch_shapes=[
            pltpu.VMEM((frames, cols, channels), jnp.bfloat16),
            pltpu.VMEM((made, cols, channels), jnp.bfloat16),
            pltpu.VMEM((frames * GROUP, frames * GROUP), jnp.float32),
            *[pltpu.VMEM(matrix.shape, jnp.bfloat16) for matrix in matrices],
            pltpu.SemaphoreType.DMA((n_copies,)),
            pltpu.SemaphoreType.DMA((5,)),
        ],
        compiler_params=pltpu.CompilerParams(vmem_limit_bytes=20 * MIB),
        cost_estimate=pl.CostEstimate(
            flops=rows * channels * (channels * 11 + GROUP * frames * 4),
            bytes_accessed=rows * channels * 3 + channels * channels * 14,
            transcendentals=rows * frames,
        ),
        name=name,
    )(*pieces, norm_gain[None], *matrices)


def rim_kernel(chips, *refs):
    mine = refs[:chips]
    other, left, right = refs[chips:]
    _, core = place()
    made, cols, _ = other.shape[1:]
    for k in range(chips):
        own = mine[k][pl.ds(core * made, made)]
        for slot, part in ((2 * k, own), (2 * k + 1, other[k])):
            left[slot] = part[:, 0]
            right[slot] = part[:, cols - 1]


def rim(mine, other):
    chips, made, _, channels = other.shape
    return pl.pallas_call(
        functools.partial(rim_kernel, chips),
        out_shape=[jax.ShapeDtypeStruct((2 * chips, made, channels), jnp.bfloat16)] * 2,
        in_specs=[INSIDE] * (chips + 1),
        out_specs=[INSIDE] * 2,
        compiler_params=pltpu.CompilerParams(vmem_limit_bytes=4 * MIB),
        name="rim",
    )(*mine, other)


def filter_kernel(chips, *refs):
    pieces = refs[:chips]
    other, inner, left, right, w_depth, out, outer, sems = refs[chips:]
    chip, core = place()
    made = other.shape[1]
    copies = []
    for k in range(chips):
        row = 2 * (chip ^ k)
        copies.append(
            pltpu.make_async_copy(pieces[k].at[pl.ds(core * made, made)], outer.at[row + core], sems.at[2 * k])
        )
        copies.append(pltpu.make_async_copy(other.at[k], outer.at[row + 1 - core], sems.at[2 * k + 1]))
    for copy in copies:
        copy.start()
    for copy in copies:
        copy.wait()
    frames, height, cols, channels = out.shape
    edge = cols // 4
    lanes = 128

    def one_part(step, carry):
        part = pl.ds(pl.multiple_of(step * lanes, lanes), lanes)
        taps = [[w_depth[a, b, part] for b in range(3)] for a in range(3)]
        for frame in range(frames):

            def filtered(row):
                sides = outer[row, frame, :, part].astype(jnp.float32)
                between = inner[row, frame, :, part].astype(jnp.float32)
                mid = jnp.concatenate([sides[:edge], between, sides[edge:]], axis=0)
                spot = lax.broadcasted_iota(jnp.int32, mid.shape, 0)
                slot = 2 * (chip ^ (row // 2)) + (core ^ (row % 2))
                low = left[slot, frame, part].astype(jnp.float32)[None]
                high = right[slot, frame, part].astype(jnp.float32)[None]
                before = jnp.where(spot == 0, low, pltpu.roll(mid, 1, 0))
                after = jnp.where(spot == cols - 1, high, pltpu.roll(mid, cols - 1, 0))
                return [
                    before * taps[a][0][None] + mid * taps[a][1][None] + after * taps[a][2][None] for a in range(3)
                ]

            above = None
            here = filtered(0)
            for row in range(height):
                below = filtered(row + 1) if row + 1 < height else None
                total = here[1]
                if above is not None:
                    total = total + above[0]
                if below is not None:
                    total = total + below[2]
                out[frame, row, :, part] = total.astype(jnp.bfloat16)
                above, here = here, below
        return carry

    lax.fori_loop(0, channels // lanes, one_part, 0)


def depth_filter(outer, other, inner, left, right, w_depth):
    height, frames, width, channels = inner.shape
    cols = 2 * width
    size = frames * height * cols * channels
    return pl.pallas_call(
        functools.partial(filter_kernel, len(outer)),
        out_shape=jax.ShapeDtypeStruct((frames, height, cols, channels), jnp.bfloat16),
        in_specs=[ANYWHERE] * (len(outer) + 1) + [INSIDE] * 4,
        out_specs=INSIDE,
        scratch_shapes=[
            pltpu.VMEM((height, frames, width, channels), jnp.bfloat16),
            pltpu.SemaphoreType.DMA((height,)),
        ],
        compiler_params=pltpu.CompilerParams(vmem_limit_bytes=8 * MIB),
        cost_estimate=pl.CostEstimate(flops=18 * size, bytes_accessed=4 * size, transcendentals=0),
        name="depth_filter",
    )(*outer, other, inner, left, right, w_depth)


def local(video, norm_gain, w_query, w_key, w_value, w_out, w_time, w_depth):
    count = lax.axis_size("frm")
    chips = count // 2
    span, height, cols, channels = video.shape
    assert height == count and chips & (chips - 1) == 0 and chips > 1
    made = span // 2
    frames = span * count
    width = cols // 2
    weights = (norm_gain, w_query, w_key, w_value, w_out, w_time)

    def swap(block, k):
        return lax.ppermute(block, "frm", [(i, i ^ k) for i in range(count)]) if k else block

    far = list(range(chips - 1, 0, -1))
    hops = [2 * k for k in [*far, 0]]
    pieces = cut(lambda me: ([me ^ k for k in hops], [me ^ k ^ 1 for k in hops]), chips, video)
    *outer, outer_stack = pieces[: chips + 1]
    *inner, inner_stack = pieces[chips + 1 :]

    def joined(ins, outs):
        *owns, other = ins
        pairs = []
        for i, own in enumerate(owns):
            pairs.append((own, outs[i].at[pl.ds(0, span)]))
            pairs.append((other.at[i], outs[i].at[pl.ds(span, span)]))
        return pairs

    def join(owns, other, name):
        return gather(joined, 2 * len(far), [*owns[:-1], other], [(2 * span, width, channels)] * len(far), name)

    outer_other = swap(outer_stack, 1)
    outer_far = join(outer, outer_other, "join_outer")
    *outer_far, inner_stack = lax.optimization_barrier((*outer_far, inner_stack))
    outer_far = [swap(piece, k) for k, piece in zip(hops, outer_far)]
    inner_other = swap(inner_stack, 1)
    inner_far = join(inner, inner_other, "join_inner")
    outer_far[0], *inner_far = lax.optimization_barrier((outer_far[0], *inner_far))
    inner_far = [swap(piece, k) for k, piece in zip(hops, inner_far)]

    def inward(pieces):
        me = lax.axis_index("frm")
        *pieces, own, other = pieces
        pairs = []
        for k, piece in zip(hops, pieces):
            pairs.append((piece.at[pl.ds(0, span)], (me ^ k) * span))
            pairs.append((piece.at[pl.ds(span, span)], (me ^ k ^ 1) * span))
        return pairs + [(own, me * span), (other.at[len(far)], (me ^ 1) * span)]

    outer = attend(inward, count, [*outer_far, outer[-1], outer_other], weights, frames, chips, "attend_outer")
    outer = [swap(piece, 2 * k) for k, piece in enumerate(outer)]
    (inner,) = attend(inward, count, [*inner_far, inner[-1], inner_other], weights, frames, 1, "attend_inner")
    *outer, inner = lax.optimization_barrier((*outer, inner))

    def halves(ins, outs):
        _, core = place()
        return [(piece.at[pl.ds((1 - core) * made, made)], outs[0].at[k]) for k, piece in enumerate(ins)]

    outer_other = swap(gather(halves, chips, outer, [(chips, made, width, channels)], "halves")[0], 1)
    inner = lax.all_to_all(
        inner.reshape(count, made, width, channels), "frm", split_axis=0, concat_axis=0, tiled=True
    )
    low_side, high_side = rim(outer, outer_other)
    line = lax.axis_size("col")
    upward = [(i, i + 1) for i in range(line - 1)]
    left = lax.ppermute(high_side, "col", upward)
    right = lax.ppermute(low_side, "col", [(b, a) for a, b in upward])
    return depth_filter(outer, outer_other, inner, left, right, w_depth)


def solution(mesh):
    return jax.shard_map(
        local,
        mesh=mesh,
        in_specs=(P("frm", None, "col", None), P(), P(), P(), P(), P(), P(), P()),
        out_specs=P("frm", None, "col", None),
        check_vma=False,
    )
```

```python
import functools
import math

import jax
import jax.numpy as jnp
from jax import lax
from jax.experimental import pallas as pl
from jax.experimental.pallas import tpu as pltpu
from jax.sharding import PartitionSpec as P

epsilon = 1e-06
GROUP = 8
BLOCKS = 2
NORM_ROWS = 64
SOFT_ROWS = 32
MIB = 1024 * 1024
ANYWHERE = pl.BlockSpec(memory_space=pl.ANY)
INSIDE = pl.BlockSpec(memory_space=pltpu.VMEM)


def place():
    me = lax.axis_index("frm")
    return me // 2, me % 2


def gather_kernel(pairs_of, n_in, *refs):
    *arrays, sems = refs
    pairs = pairs_of(arrays[:n_in], arrays[n_in:])
    copies = [pltpu.make_async_copy(source, target, sems.at[i]) for i, (source, target) in enumerate(pairs)]
    for copy in copies:
        copy.start()
    for copy in copies:
        copy.wait()


def gather(pairs_of, n_pairs, arrays, shapes, name):
    size = sum(math.prod(shape) for shape in shapes)
    return pl.pallas_call(
        functools.partial(gather_kernel, pairs_of, len(arrays)),
        out_shape=[jax.ShapeDtypeStruct(shape, jnp.bfloat16) for shape in shapes],
        in_specs=[ANYWHERE] * len(arrays),
        out_specs=[INSIDE] * len(shapes),
        scratch_shapes=[pltpu.SemaphoreType.DMA((n_pairs,))],
        compiler_params=pltpu.CompilerParams(vmem_limit_bytes=4 * MIB),
        cost_estimate=pl.CostEstimate(flops=0, bytes_accessed=4 * size, transcendentals=0),
        name=name,
    )(*arrays)


def cut_kernel(rows_of, video, *refs):
    *results, held, sems = refs
    span, height, cols = held.shape[1], held.shape[0], held.shape[2]
    edge = cols // 4
    copies = [pltpu.make_async_copy(video.at[:, row], held.at[row], sems.at[row]) for row in range(height)]
    for copy in copies:
        copy.start()
    for copy in copies:
        copy.wait()
    half = len(results) // 2
    own, other = rows_of(lax.axis_index("frm"))
    for rim in (True, False):
        *singles, stack = results[:half] if rim else results[half:]
        targets = singles + [stack.at[k] for k in range(stack.shape[0])]
        for row, target in zip(own + other, targets):
            values = held[row].astype(jnp.float32)
            if rim:
                values = jnp.concatenate([values[:, :edge], values[:, 3 * edge :]], axis=1)
            else:
                values = values[:, edge : 3 * edge]
            target[...] = values.astype(jnp.bfloat16)


def cut(rows_of, chips, video):
    span, height, cols, channels = video.shape
    shape = (span, cols // 2, channels)
    shapes = ([shape] * chips + [(chips, *shape)]) * 2
    return pl.pallas_call(
        functools.partial(cut_kernel, rows_of),
        out_shape=[jax.ShapeDtypeStruct(shape, jnp.bfloat16) for shape in shapes],
        in_specs=[ANYWHERE],
        out_specs=[INSIDE] * len(shapes),
        scratch_shapes=[
            pltpu.VMEM((height, span, cols, channels), jnp.bfloat16),
            pltpu.SemaphoreType.DMA((height,)),
        ],
        compiler_params=pltpu.CompilerParams(vmem_limit_bytes=12 * MIB),
        cost_estimate=pl.CostEstimate(flops=0, bytes_accessed=3 * video.size, transcendentals=0),
        name="cut",
    )(video)


def attend_frames(band, gain, bias, weights, ready, normed, projected, attended, mixed):
    w_out, w_time = weights[3:]
    frames, cols, channels = band.shape
    groups = cols // GROUP
    rows = frames * GROUP
    tile = NORM_ROWS // GROUP
    for first in range(0, frames, tile):
        wide = band[first : first + tile].astype(jnp.float32)
        for group in range(groups):
            x = wide[:, group * GROUP : (group + 1) * GROUP].reshape(NORM_ROWS, channels)
            x = x * lax.rsqrt(jnp.mean(x * x, axis=-1, keepdims=True) + epsilon) * gain
            begin = group * rows + first * GROUP
            normed[begin : begin + NORM_ROWS] = x.astype(jnp.bfloat16)
    for index in range(3):
        ready(index)
        projected[index] = jnp.dot(normed[...], weights[index][...], preferred_element_type=jnp.float32).astype(
            jnp.bfloat16
        )
    queries, key_proj, values = projected.at[0], projected.at[1], projected.at[2]
    height = rows // BLOCKS
    power = math.log2(math.e) / math.sqrt(channels)
    for group in range(groups):
        first = group * rows
        for block in range(BLOCKS):
            begin = block * height
            span = begin + height
            scores = lax.dot_general(
                queries[first + begin : first + span],
                key_proj[first : first + span],
                (((1,), (1,)), ((), ())),
                preferred_element_type=jnp.float32,
            )
            shares = []
            for low in range(0, height, SOFT_ROWS):
                part = scores[low : low + SOFT_ROWS] + bias[begin + low : begin + low + SOFT_ROWS, :span]
                raised = jnp.exp2((part - jnp.max(part, axis=-1, keepdims=True)) * power)
                scale = 1.0 / jnp.sum(raised, axis=-1, keepdims=True)
                shares.append((raised * scale).astype(jnp.bfloat16))
            attended[first + begin : first + span] = jnp.dot(
                jnp.concatenate(shares, axis=0), values[first : first + span], preferred_element_type=jnp.float32
            ).astype(jnp.bfloat16)
    ready(3)
    out = jnp.dot(attended[...], w_out[...], preferred_element_type=jnp.float32).reshape(
        groups, frames, GROUP, channels
    )
    for group in range(groups):
        for first in range(0, frames, tile):
            x = band[first : first + tile, group * GROUP : (group + 1) * GROUP].astype(jnp.float32)
            x = x + out[group, first : first + tile]
            mixed[group, first + 1 : first + 1 + tile] = x
            if first == 0:
                mixed[group, 0] = x[0]
    ready(4)
    taps = []
    for tap in range(3):
        parts = []
        for group in range(groups):
            view = mixed[group, tap - tap % 2 : tap - tap % 2 + frames].reshape(frames // 2, 2, GROUP, channels)
            parts.append(view[:, tap % 2].reshape(rows // 2, channels).astype(jnp.bfloat16))
        taps.append(jnp.dot(jnp.concatenate(parts, axis=0), w_time[tap], preferred_element_type=jnp.float32))
    summed = (taps[0] + taps[1]) + taps[2]
    return (summed / (1.0 + jnp.exp(-summed))).reshape(groups, frames // 2, GROUP, channels)


def attend_kernel(inward, n_in, n_out, *refs):
    pieces = refs[:n_in]
    gain = refs[n_in]
    sources = refs[n_in + 1 : n_in + 6]
    results = refs[n_in + 6 : n_in + 6 + n_out]
    band, done, bias, normed, projected, attended, mixed, *held, sems, weight_sems = refs[n_in + 6 + n_out :]
    fetches = [pltpu.make_async_copy(s, h, weight_sems.at[i]) for i, (s, h) in enumerate(zip(sources, held))]
    waited = set()

    def ready(index):
        if index not in waited:
            waited.add(index)
            fetches[index].wait()

    copies = [
        pltpu.make_async_copy(piece, band.at[pl.ds(first, piece.shape[0])], sems.at[i])
        for i, (piece, first) in enumerate(inward(pieces))
    ]
    for copy in copies + fetches:
        copy.start()
    to_row = lax.broadcasted_iota(jnp.int32, bias.shape, 0)
    from_row = lax.broadcasted_iota(jnp.int32, bias.shape, 1)
    allowed = (from_row <= to_row) & (((from_row ^ to_row) & (GROUP - 1)) == 0)
    bias[...] = jnp.where(allowed, 0.0, -1e30)
    for copy in copies:
        copy.wait()
    made = attend_frames(band, gain[...], bias, held, ready, normed, projected, attended, mixed)
    done[...] = jnp.concatenate([made[g] for g in range(made.shape[0])], axis=1).astype(jnp.bfloat16)
    chip, _ = place()
    copies = [
        pltpu.make_async_copy(
            done if n_out == 1 else done.at[pl.ds((chip ^ k) * result.shape[0], result.shape[0])], result, sems.at[k]
        )
        for k, result in enumerate(results)
    ]
    for copy in copies:
        copy.start()
    for copy in copies:
        copy.wait()


def attend(inward, n_copies, pieces, weights, frames, n_out, name):
    cols, channels = pieces[0].shape[-2:]
    rows = frames * cols
    made = frames // 2
    norm_gain, *matrices = weights
    return pl.pallas_call(
        functools.partial(attend_kernel, inward, len(pieces), n_out),
        out_shape=[jax.ShapeDtypeStruct((made // n_out, cols, channels), jnp.bfloat16)] * n_out,
        in_specs=[ANYWHERE] * len(pieces) + [INSIDE] + [ANYWHERE] * 5,
        out_specs=[ANYWHERE] * n_out,
        scratch_shapes=[
            pltpu.VMEM((frames, cols, channels), jnp.bfloat16),
            pltpu.VMEM((made, cols, channels), jnp.bfloat16),
            pltpu.VMEM((frames * GROUP, frames * GROUP), jnp.float32),
            pltpu.VMEM((rows, channels), jnp.bfloat16),
            pltpu.VMEM((3, rows, channels), jnp.bfloat16),
            pltpu.VMEM((rows, channels), jnp.bfloat16),
            pltpu.VMEM((cols // GROUP, frames + 2, GROUP, channels), jnp.float32),
            *[pltpu.VMEM(matrix.shape, jnp.bfloat16) for matrix in matrices],
            pltpu.SemaphoreType.DMA((n_copies,)),
            pltpu.SemaphoreType.DMA((5,)),
        ],
        compiler_params=pltpu.CompilerParams(vmem_limit_bytes=20 * MIB),
        cost_estimate=pl.CostEstimate(
            flops=rows * channels * (channels * 11 + GROUP * frames * 4),
            bytes_accessed=rows * channels * 3 + channels * channels * 14,
            transcendentals=rows * frames,
        ),
        name=name,
    )(*pieces, norm_gain[None], *matrices)


def rim_kernel(chips, *refs):
    mine = refs[:chips]
    other, left, right = refs[chips:]
    _, core = place()
    made, cols, _ = other.shape[1:]
    for k in range(chips):
        own = mine[k][pl.ds(core * made, made)]
        for slot, part in ((2 * k, own), (2 * k + 1, other[k])):
            left[slot] = part[:, 0]
            right[slot] = part[:, cols - 1]


def rim(mine, other):
    chips, made, _, channels = other.shape
    return pl.pallas_call(
        functools.partial(rim_kernel, chips),
        out_shape=[jax.ShapeDtypeStruct((2 * chips, made, channels), jnp.bfloat16)] * 2,
        in_specs=[INSIDE] * (chips + 1),
        out_specs=[INSIDE] * 2,
        compiler_params=pltpu.CompilerParams(vmem_limit_bytes=4 * MIB),
        name="rim",
    )(*mine, other)


def filter_kernel(chips, *refs):
    pieces = refs[:chips]
    other, inner, left, right, w_depth, out, outer, sems = refs[chips:]
    chip, core = place()
    made = other.shape[1]
    copies = []
    for k in range(chips):
        row = 2 * (chip ^ k)
        copies.append(
            pltpu.make_async_copy(pieces[k].at[pl.ds(core * made, made)], outer.at[row + core], sems.at[2 * k])
        )
        copies.append(pltpu.make_async_copy(other.at[k], outer.at[row + 1 - core], sems.at[2 * k + 1]))
    for copy in copies:
        copy.start()
    for copy in copies:
        copy.wait()
    frames, height, cols, channels = out.shape
    edge = cols // 4
    lanes = 128

    def one_part(step, carry):
        part = pl.ds(pl.multiple_of(step * lanes, lanes), lanes)
        taps = [[w_depth[a, b, part] for b in range(3)] for a in range(3)]
        for frame in range(frames):

            def filtered(row):
                sides = outer[row, frame, :, part].astype(jnp.float32)
                between = inner[row, frame, :, part].astype(jnp.float32)
                mid = jnp.concatenate([sides[:edge], between, sides[edge:]], axis=0)
                spot = lax.broadcasted_iota(jnp.int32, mid.shape, 0)
                slot = 2 * (chip ^ (row // 2)) + (core ^ (row % 2))
                low = left[slot, frame, part].astype(jnp.float32)[None]
                high = right[slot, frame, part].astype(jnp.float32)[None]
                before = jnp.where(spot == 0, low, pltpu.roll(mid, 1, 0))
                after = jnp.where(spot == cols - 1, high, pltpu.roll(mid, cols - 1, 0))
                return [
                    before * taps[a][0][None] + mid * taps[a][1][None] + after * taps[a][2][None] for a in range(3)
                ]

            above = None
            here = filtered(0)
            for row in range(height):
                below = filtered(row + 1) if row + 1 < height else None
                total = here[1]
                if above is not None:
                    total = total + above[0]
                if below is not None:
                    total = total + below[2]
                out[frame, row, :, part] = total.astype(jnp.bfloat16)
                above, here = here, below
        return carry

    lax.fori_loop(0, channels // lanes, one_part, 0)


def depth_filter(outer, other, inner, left, right, w_depth):
    height, frames, width, channels = inner.shape
    cols = 2 * width
    size = frames * height * cols * channels
    return pl.pallas_call(
        functools.partial(filter_kernel, len(outer)),
        out_shape=jax.ShapeDtypeStruct((frames, height, cols, channels), jnp.bfloat16),
        in_specs=[ANYWHERE] * (len(outer) + 1) + [INSIDE] * 4,
        out_specs=INSIDE,
        scratch_shapes=[
            pltpu.VMEM((height, frames, width, channels), jnp.bfloat16),
            pltpu.SemaphoreType.DMA((height,)),
        ],
        compiler_params=pltpu.CompilerParams(vmem_limit_bytes=8 * MIB),
        cost_estimate=pl.CostEstimate(flops=18 * size, bytes_accessed=4 * size, transcendentals=0),
        name="depth_filter",
    )(*outer, other, inner, left, right, w_depth)


def local(video, norm_gain, w_query, w_key, w_value, w_out, w_time, w_depth):
    count = lax.axis_size("frm")
    chips = count // 2
    span, height, cols, channels = video.shape
    assert height == count and chips & (chips - 1) == 0 and chips > 1
    made = span // 2
    frames = span * count
    width = cols // 2
    weights = (norm_gain, w_query, w_key, w_value, w_out, w_time)

    def swap(block, k):
        return lax.ppermute(block, "frm", [(i, i ^ k) for i in range(count)]) if k else block

    far = list(range(chips - 1, 0, -1))
    hops = [2 * k for k in [*far, 0]]
    pieces = cut(lambda me: ([me ^ k for k in hops], [me ^ k ^ 1 for k in hops]), chips, video)
    *outer, outer_stack = pieces[: chips + 1]
    *inner, inner_stack = pieces[chips + 1 :]

    def joined(ins, outs):
        *owns, other = ins
        pairs = []
        for i, own in enumerate(owns):
            pairs.append((own, outs[i].at[pl.ds(0, span)]))
            pairs.append((other.at[i], outs[i].at[pl.ds(span, span)]))
        return pairs

    def join(owns, other, name):
        return gather(joined, 2 * len(far), [*owns[:-1], other], [(2 * span, width, channels)] * len(far), name)

    outer_other = swap(outer_stack, 1)
    outer_far = join(outer, outer_other, "join_outer")
    *outer_far, inner_stack = lax.optimization_barrier((*outer_far, inner_stack))
    outer_far = [swap(piece, k) for k, piece in zip(hops, outer_far)]
    inner_other = swap(inner_stack, 1)
    inner_far = join(inner, inner_other, "join_inner")
    outer_far[0], *inner_far = lax.optimization_barrier((outer_far[0], *inner_far))
    inner_far = [swap(piece, k) for k, piece in zip(hops, inner_far)]

    def inward(pieces):
        me = lax.axis_index("frm")
        *pieces, own, other = pieces
        pairs = []
        for k, piece in zip(hops, pieces):
            pairs.append((piece.at[pl.ds(0, span)], (me ^ k) * span))
            pairs.append((piece.at[pl.ds(span, span)], (me ^ k ^ 1) * span))
        return pairs + [(own, me * span), (other.at[len(far)], (me ^ 1) * span)]

    outer = attend(inward, count, [*outer_far, outer[-1], outer_other], weights, frames, chips, "attend_outer")
    outer = [swap(piece, 2 * k) for k, piece in enumerate(outer)]
    (inner,) = attend(inward, count, [*inner_far, inner[-1], inner_other], weights, frames, 1, "attend_inner")
    *outer, inner = lax.optimization_barrier((*outer, inner))

    def halves(ins, outs):
        _, core = place()
        return [(piece.at[pl.ds((1 - core) * made, made)], outs[0].at[k]) for k, piece in enumerate(ins)]

    outer_other = swap(gather(halves, chips, outer, [(chips, made, width, channels)], "halves")[0], 1)
    inner = lax.all_to_all(
        inner.reshape(count, made, width, channels), "frm", split_axis=0, concat_axis=0, tiled=True
    )
    low_side, high_side = rim(outer, outer_other)
    line = lax.axis_size("col")
    upward = [(i, i + 1) for i in range(line - 1)]
    left = lax.ppermute(high_side, "col", upward)
    right = lax.ppermute(low_side, "col", [(b, a) for a, b in upward])
    return depth_filter(outer, outer_other, inner, left, right, w_depth)


def solution(mesh):
    return jax.shard_map(
        local,
        mesh=mesh,
        in_specs=(P("frm", None, "col", None), P(), P(), P(), P(), P(), P(), P()),
        out_specs=P("frm", None, "col", None),
        check_vma=False,
    )
```

```python
import functools
import math

import jax
import jax.numpy as jnp
from jax import lax
from jax.experimental import pallas as pl
from jax.experimental.pallas import tpu as pltpu
from jax.sharding import PartitionSpec as P

epsilon = 1e-06
GROUP = 8
BLOCKS = 2
TILE = 8
SOFT_ROWS = 32
MIB = 1024 * 1024
INSIDE = pl.BlockSpec(memory_space=pltpu.VMEM)


def place():
    me = lax.axis_index("frm")
    return me // 2, me % 2


def gather_kernel(pairs_of, n_in, *refs):
    for source, target in pairs_of(refs[:n_in], refs[n_in:]):
        target[...] = source[...]


def gather(pairs_of, arrays, shapes, name):
    size = sum(math.prod(shape) for shape in shapes)
    return pl.pallas_call(
        functools.partial(gather_kernel, pairs_of, len(arrays)),
        out_shape=[jax.ShapeDtypeStruct(shape, jnp.bfloat16) for shape in shapes],
        in_specs=[INSIDE] * len(arrays),
        out_specs=[INSIDE] * len(shapes),
        compiler_params=pltpu.CompilerParams(vmem_limit_bytes=6 * MIB),
        cost_estimate=pl.CostEstimate(flops=0, bytes_accessed=4 * size, transcendentals=0),
        name=name,
    )(*arrays)


def cut_kernel(rows_of, video, *results):
    edge = video.shape[2] // 4
    half = len(results) // 2
    own, other = rows_of(lax.axis_index("frm"))
    for rim in (True, False):
        *singles, stack = results[:half] if rim else results[half:]
        targets = list(singles) + [stack.at[k] for k in range(stack.shape[0])]
        for row, target in zip(own + other, targets):
            values = video[:, row].astype(jnp.float32)
            if rim:
                values = jnp.concatenate([values[:, :edge], values[:, 3 * edge :]], axis=1)
            else:
                values = values[:, edge : 3 * edge]
            target[...] = values.astype(jnp.bfloat16)


def cut(rows_of, chips, video):
    span, height, cols, channels = video.shape
    shape = (span, cols // 2, channels)
    shapes = ([shape] * chips + [(chips, *shape)]) * 2
    return pl.pallas_call(
        functools.partial(cut_kernel, rows_of),
        out_shape=[jax.ShapeDtypeStruct(shape, jnp.bfloat16) for shape in shapes],
        in_specs=[INSIDE],
        out_specs=[INSIDE] * len(shapes),
        compiler_params=pltpu.CompilerParams(vmem_limit_bytes=12 * MIB),
        cost_estimate=pl.CostEstimate(flops=0, bytes_accessed=3 * video.size, transcendentals=0),
        name="cut",
    )(video)


def attend_frames(pieces, gain, bias, weights, normed, projected, attended, mixed):
    w_query, w_key, w_value, w_out, w_time = weights
    groups, frames, _, channels = mixed.shape
    frames = frames - 2
    rows = frames * GROUP
    for piece, first in pieces:
        wide = piece[...].astype(jnp.float32)
        span = wide.shape[0]
        for group in range(groups):
            x = wide[:, group * GROUP : (group + 1) * GROUP]
            mixed[group, pl.ds(first + 1, span)] = x
            x = x.reshape(span * GROUP, channels)
            x = x * lax.rsqrt(jnp.mean(x * x, axis=-1, keepdims=True) + epsilon) * gain
            begin = pl.multiple_of(group * rows + first * GROUP, span * GROUP)
            normed[pl.ds(begin, span * GROUP)] = x.astype(jnp.bfloat16)
    for index, weight in enumerate((w_query, w_key, w_value)):
        projected[index] = jnp.dot(normed[...], weight[...], preferred_element_type=jnp.float32).astype(jnp.bfloat16)
    queries, key_proj, values = projected.at[0], projected.at[1], projected.at[2]
    height = rows // BLOCKS
    power = math.log2(math.e) / math.sqrt(channels)
    for group in range(groups):
        first = group * rows
        for block in range(BLOCKS):
            begin = block * height
            span = begin + height
            scores = lax.dot_general(
                queries[first + begin : first + span],
                key_proj[first : first + span],
                (((1,), (1,)), ((), ())),
                preferred_element_type=jnp.float32,
            )
            shares = []
            for low in range(0, height, SOFT_ROWS):
                part = scores[low : low + SOFT_ROWS] + bias[begin + low : begin + low + SOFT_ROWS, :span]
                raised = jnp.exp2((part - jnp.max(part, axis=-1, keepdims=True)) * power)
                scale = 1.0 / jnp.sum(raised, axis=-1, keepdims=True)
                shares.append((raised * scale).astype(jnp.bfloat16))
            attended[first + begin : first + span] = jnp.dot(
                jnp.concatenate(shares, axis=0), values[first : first + span], preferred_element_type=jnp.float32
            ).astype(jnp.bfloat16)
    out = jnp.dot(attended[...], w_out[...], preferred_element_type=jnp.float32).reshape(
        groups, frames, GROUP, channels
    )
    for group in range(groups):
        for first in range(0, frames, TILE):
            x = mixed[group, first + 1 : first + 1 + TILE] + out[group, first : first + TILE]
            mixed[group, first + 1 : first + 1 + TILE] = x
            if first == 0:
                mixed[group, 0] = x[0]
    taps = []
    for tap in range(3):
        parts = []
        for group in range(groups):
            view = mixed[group, tap - tap % 2 : tap - tap % 2 + frames].reshape(frames // 2, 2, GROUP, channels)
            parts.append(view[:, tap % 2].reshape(rows // 2, channels).astype(jnp.bfloat16))
        taps.append(jnp.dot(jnp.concatenate(parts, axis=0), w_time[tap], preferred_element_type=jnp.float32))
    summed = (taps[0] + taps[1]) + taps[2]
    return (summed / (1.0 + jnp.exp(-summed))).reshape(groups, frames // 2, GROUP, channels)


def attend_kernel(inward, n_in, n_out, *refs):
    gain, *weights = refs[n_in : n_in + 6]
    results = refs[n_in + 6 : n_in + 6 + n_out]
    bias, normed, projected, attended, mixed, *done = refs[n_in + 6 + n_out :]
    to_row = lax.broadcasted_iota(jnp.int32, bias.shape, 0)
    from_row = lax.broadcasted_iota(jnp.int32, bias.shape, 1)
    allowed = (from_row <= to_row) & (((from_row ^ to_row) & (GROUP - 1)) == 0)
    bias[...] = jnp.where(allowed, 0.0, -1e30)
    made = attend_frames(inward(refs[:n_in]), gain[...], bias, weights, normed, projected, attended, mixed)
    made = jnp.concatenate([made[g] for g in range(made.shape[0])], axis=1).astype(jnp.bfloat16)
    if n_out == 1:
        results[0][...] = made
    else:
        done[0][...] = made
        chip, _ = place()
        for k, result in enumerate(results):
            result[...] = done[0][pl.ds((chip ^ k) * result.shape[0], result.shape[0])]


def attend(inward, pieces, weights, frames, n_out, name):
    cols, channels = pieces[0].shape[-2:]
    rows = frames * cols
    made = frames // 2
    norm_gain, *matrices = weights
    return pl.pallas_call(
        functools.partial(attend_kernel, inward, len(pieces), n_out),
        out_shape=[jax.ShapeDtypeStruct((made // n_out, cols, channels), jnp.bfloat16)] * n_out,
        in_specs=[INSIDE] * (len(pieces) + 6),
        out_specs=[INSIDE] * n_out,
        scratch_shapes=[
            pltpu.VMEM((frames * GROUP, frames * GROUP), jnp.float32),
            pltpu.VMEM((rows, channels), jnp.bfloat16),
            pltpu.VMEM((3, rows, channels), jnp.bfloat16),
            pltpu.VMEM((rows, channels), jnp.bfloat16),
            pltpu.VMEM((cols // GROUP, frames + 2, GROUP, channels), jnp.float32),
            *([pltpu.VMEM((made, cols, channels), jnp.bfloat16)] if n_out > 1 else []),
        ],
        compiler_params=pltpu.CompilerParams(vmem_limit_bytes=24 * MIB),
        cost_estimate=pl.CostEstimate(
            flops=rows * channels * (channels * 11 + GROUP * frames * 4),
            bytes_accessed=rows * channels * 3 + channels * channels * 14,
            transcendentals=rows * frames,
        ),
        name=name,
    )(*pieces, norm_gain[None], *matrices)


def rim_kernel(chips, *refs):
    mine = refs[:chips]
    other, left, right = refs[chips:]
    _, core = place()
    made, cols, _ = other.shape[1:]
    for k in range(chips):
        own = mine[k][pl.ds(core * made, made)]
        for slot, part in ((2 * k, own), (2 * k + 1, other[k])):
            left[slot] = part[:, 0]
            right[slot] = part[:, cols - 1]


def rim(mine, other):
    chips, made, _, channels = other.shape
    return pl.pallas_call(
        functools.partial(rim_kernel, chips),
        out_shape=[jax.ShapeDtypeStruct((2 * chips, made, channels), jnp.bfloat16)] * 2,
        in_specs=[INSIDE] * (chips + 1),
        out_specs=[INSIDE] * 2,
        compiler_params=pltpu.CompilerParams(vmem_limit_bytes=4 * MIB),
        name="rim",
    )(*mine, other)


def filter_kernel(chips, *refs):
    pieces = refs[:chips]
    other, inner, left, right, w_depth, out, outer = refs[chips:]
    chip, core = place()
    made = other.shape[1]
    for k in range(chips):
        row = 2 * (chip ^ k)
        outer[row + core] = pieces[k][pl.ds(core * made, made)]
        outer[row + 1 - core] = other[k]
    frames, height, cols, channels = out.shape
    edge = cols // 4
    lanes = 128

    def one_part(step, carry):
        part = pl.ds(pl.multiple_of(step * lanes, lanes), lanes)
        taps = [[w_depth[a, b, part] for b in range(3)] for a in range(3)]
        for frame in range(frames):

            def filtered(row):
                sides = outer[row, frame, :, part].astype(jnp.float32)
                between = inner[row, frame, :, part].astype(jnp.float32)
                mid = jnp.concatenate([sides[:edge], between, sides[edge:]], axis=0)
                spot = lax.broadcasted_iota(jnp.int32, mid.shape, 0)
                slot = 2 * (chip ^ (row // 2)) + (core ^ (row % 2))
                low = left[slot, frame, part].astype(jnp.float32)[None]
                high = right[slot, frame, part].astype(jnp.float32)[None]
                before = jnp.where(spot == 0, low, pltpu.roll(mid, 1, 0))
                after = jnp.where(spot == cols - 1, high, pltpu.roll(mid, cols - 1, 0))
                return [
                    before * taps[a][0][None] + mid * taps[a][1][None] + after * taps[a][2][None] for a in range(3)
                ]

            above = None
            here = filtered(0)
            for row in range(height):
                below = filtered(row + 1) if row + 1 < height else None
                total = here[1]
                if above is not None:
                    total = total + above[0]
                if below is not None:
                    total = total + below[2]
                out[frame, row, :, part] = total.astype(jnp.bfloat16)
                above, here = here, below
        return carry

    lax.fori_loop(0, channels // lanes, one_part, 0)


def depth_filter(outer, other, inner, left, right, w_depth):
    height, frames, width, channels = inner.shape
    cols = 2 * width
    size = frames * height * cols * channels
    return pl.pallas_call(
        functools.partial(filter_kernel, len(outer)),
        out_shape=jax.ShapeDtypeStruct((frames, height, cols, channels), jnp.bfloat16),
        in_specs=[INSIDE] * (len(outer) + 5),
        out_specs=INSIDE,
        scratch_shapes=[pltpu.VMEM((height, frames, width, channels), jnp.bfloat16)],
        compiler_params=pltpu.CompilerParams(vmem_limit_bytes=8 * MIB),
        cost_estimate=pl.CostEstimate(flops=18 * size, bytes_accessed=4 * size, transcendentals=0),
        name="depth_filter",
    )(*outer, other, inner, left, right, w_depth)


def local(video, norm_gain, w_query, w_key, w_value, w_out, w_time, w_depth):
    count = lax.axis_size("frm")
    chips = count // 2
    span, height, cols, channels = video.shape
    assert height == count and chips & (chips - 1) == 0 and chips > 1
    made = span // 2
    frames = span * count
    width = cols // 2
    weights = (norm_gain, w_query, w_key, w_value, w_out, w_time)

    def swap(block, k):
        return lax.ppermute(block, "frm", [(i, i ^ k) for i in range(count)]) if k else block

    far = list(range(chips - 1, 0, -1))
    hops = [2 * k for k in [*far, 0]]
    pieces = cut(lambda me: ([me ^ k for k in hops], [me ^ k ^ 1 for k in hops]), chips, video)
    *outer, outer_stack = pieces[: chips + 1]
    *inner, inner_stack = pieces[chips + 1 :]

    def joined(ins, outs):
        *owns, other = ins
        pairs = []
        for i, own in enumerate(owns):
            pairs.append((own, outs[i].at[pl.ds(0, span)]))
            pairs.append((other.at[i], outs[i].at[pl.ds(span, span)]))
        return pairs

    def join(owns, other, name):
        return gather(joined, [*owns[:-1], other], [(2 * span, width, channels)] * len(far), name)

    outer_other = swap(outer_stack, 1)
    outer_far = join(outer, outer_other, "join_outer")
    *outer_far, inner_stack = lax.optimization_barrier((*outer_far, inner_stack))
    outer_far = [swap(piece, k) for k, piece in zip(hops, outer_far)]
    inner_other = swap(inner_stack, 1)
    inner_far = join(inner, inner_other, "join_inner")
    outer_far[0], *inner_far = lax.optimization_barrier((outer_far[0], *inner_far))
    inner_far = [swap(piece, k) for k, piece in zip(hops, inner_far)]

    def inward(pieces):
        me = lax.axis_index("frm")
        *pieces, own, other = pieces
        pairs = []
        for k, piece in zip(hops, pieces):
            pairs.append((piece.at[pl.ds(0, span)], (me ^ k) * span))
            pairs.append((piece.at[pl.ds(span, span)], (me ^ k ^ 1) * span))
        return pairs + [(own, me * span), (other.at[len(far)], (me ^ 1) * span)]

    outer = attend(inward, [*outer_far, outer[-1], outer_other], weights, frames, chips, "attend_outer")
    outer = [swap(piece, 2 * k) for k, piece in enumerate(outer)]
    (inner,) = attend(inward, [*inner_far, inner[-1], inner_other], weights, frames, 1, "attend_inner")
    *outer, inner = lax.optimization_barrier((*outer, inner))

    def halves(ins, outs):
        _, core = place()
        return [(piece.at[pl.ds((1 - core) * made, made)], outs[0].at[k]) for k, piece in enumerate(ins)]

    outer_other = swap(gather(halves, outer, [(chips, made, width, channels)], "halves")[0], 1)
    inner = lax.all_to_all(
        inner.reshape(count, made, width, channels), "frm", split_axis=0, concat_axis=0, tiled=True
    )
    low_side, high_side = rim(outer, outer_other)
    line = lax.axis_size("col")
    upward = [(i, i + 1) for i in range(line - 1)]
    left = lax.ppermute(high_side, "col", upward)
    right = lax.ppermute(low_side, "col", [(b, a) for a, b in upward])
    return depth_filter(outer, outer_other, inner, left, right, w_depth)


def solution(mesh):
    return jax.shard_map(
        local,
        mesh=mesh,
        in_specs=(P("frm", None, "col", None), P(), P(), P(), P(), P(), P(), P()),
        out_specs=P("frm", None, "col", None),
        check_vma=False,
    )
```

```python
import functools
import math

import jax
import jax.numpy as jnp
from jax import lax
from jax.experimental import pallas as pl
from jax.experimental.pallas import tpu as pltpu
from jax.sharding import PartitionSpec as P

epsilon = 1e-06
GROUP = 8
BLOCKS = 2
TILE = 8
SOFT_ROWS = 32
MIB = 1024 * 1024
INSIDE = pl.BlockSpec(memory_space=pltpu.VMEM)


def place():
    me = lax.axis_index("frm")
    return me // 2, me % 2


def gather_kernel(pairs_of, n_in, *refs):
    for source, target in pairs_of(refs[:n_in], refs[n_in:]):
        target[...] = source[...]


def gather(pairs_of, arrays, shapes, name):
    size = sum(math.prod(shape) for shape in shapes)
    return pl.pallas_call(
        functools.partial(gather_kernel, pairs_of, len(arrays)),
        out_shape=[jax.ShapeDtypeStruct(shape, jnp.bfloat16) for shape in shapes],
        in_specs=[INSIDE] * len(arrays),
        out_specs=[INSIDE] * len(shapes),
        compiler_params=pltpu.CompilerParams(vmem_limit_bytes=6 * MIB),
        cost_estimate=pl.CostEstimate(flops=0, bytes_accessed=4 * size, transcendentals=0),
        name=name,
    )(*arrays)


def cut_kernel(rows_of, video, *results):
    edge = video.shape[2] // 4
    half = len(results) // 2
    own, other = rows_of(lax.axis_index("frm"))
    for rim in (True, False):
        *singles, stack = results[:half] if rim else results[half:]
        targets = list(singles) + [stack.at[k] for k in range(stack.shape[0])]
        for row, target in zip(own + other, targets):
            values = video[:, row].astype(jnp.float32)
            if rim:
                values = jnp.concatenate([values[:, :edge], values[:, 3 * edge :]], axis=1)
            else:
                values = values[:, edge : 3 * edge]
            target[...] = values.astype(jnp.bfloat16)


def cut(rows_of, chips, video):
    span, height, cols, channels = video.shape
    shape = (span, cols // 2, channels)
    shapes = ([shape] * chips + [(chips, *shape)]) * 2
    return pl.pallas_call(
        functools.partial(cut_kernel, rows_of),
        out_shape=[jax.ShapeDtypeStruct(shape, jnp.bfloat16) for shape in shapes],
        in_specs=[INSIDE],
        out_specs=[INSIDE] * len(shapes),
        compiler_params=pltpu.CompilerParams(vmem_limit_bytes=12 * MIB),
        cost_estimate=pl.CostEstimate(flops=0, bytes_accessed=3 * video.size, transcendentals=0),
        name="cut",
    )(video)


def attend_frames(pieces, gain, bias, weights, normed, projected, attended, mixed):
    w_query, w_key, w_value, w_out, w_time = weights
    groups, frames, _, channels = mixed.shape
    frames = frames - 2
    rows = frames * GROUP
    for piece, first in pieces:
        wide = piece[...].astype(jnp.float32)
        span = wide.shape[0]
        for group in range(groups):
            x = wide[:, group * GROUP : (group + 1) * GROUP]
            mixed[group, pl.ds(first + 1, span)] = x
            x = x.reshape(span * GROUP, channels)
            x = x * lax.rsqrt(jnp.mean(x * x, axis=-1, keepdims=True) + epsilon) * gain
            begin = pl.multiple_of(group * rows + first * GROUP, span * GROUP)
            normed[pl.ds(begin, span * GROUP)] = x.astype(jnp.bfloat16)
    for index, weight in enumerate((w_query, w_key, w_value)):
        projected[index] = jnp.dot(normed[...], weight[...], preferred_element_type=jnp.float32).astype(jnp.bfloat16)
    queries, key_proj, values = projected.at[0], projected.at[1], projected.at[2]
    height = rows // BLOCKS
    power = math.log2(math.e) / math.sqrt(channels)
    for group in range(groups):
        first = group * rows
        for block in range(BLOCKS):
            begin = block * height
            span = begin + height
            scores = lax.dot_general(
                queries[first + begin : first + span],
                key_proj[first : first + span],
                (((1,), (1,)), ((), ())),
                preferred_element_type=jnp.float32,
            )
            shares = []
            for low in range(0, height, SOFT_ROWS):
                part = scores[low : low + SOFT_ROWS] + bias[begin + low : begin + low + SOFT_ROWS, :span]
                raised = jnp.exp2((part - jnp.max(part, axis=-1, keepdims=True)) * power)
                scale = 1.0 / jnp.sum(raised, axis=-1, keepdims=True)
                shares.append((raised * scale).astype(jnp.bfloat16))
            attended[first + begin : first + span] = jnp.dot(
                jnp.concatenate(shares, axis=0), values[first : first + span], preferred_element_type=jnp.float32
            ).astype(jnp.bfloat16)
    out = jnp.dot(attended[...], w_out[...], preferred_element_type=jnp.float32).reshape(
        groups, frames, GROUP, channels
    )
    for group in range(groups):
        for first in range(0, frames, TILE):
            x = mixed[group, first + 1 : first + 1 + TILE] + out[group, first : first + TILE]
            mixed[group, first + 1 : first + 1 + TILE] = x
            if first == 0:
                mixed[group, 0] = x[0]
    taps = []
    for tap in range(3):
        parts = []
        for group in range(groups):
            view = mixed[group, tap - tap % 2 : tap - tap % 2 + frames].reshape(frames // 2, 2, GROUP, channels)
            parts.append(view[:, tap % 2].reshape(rows // 2, channels).astype(jnp.bfloat16))
        taps.append(jnp.dot(jnp.concatenate(parts, axis=0), w_time[tap], preferred_element_type=jnp.float32))
    summed = (taps[0] + taps[1]) + taps[2]
    return (summed / (1.0 + jnp.exp(-summed))).reshape(groups, frames // 2, GROUP, channels)


def attend_kernel(inward, hops, paired, n_in, *refs):
    gain, *weights = refs[n_in : n_in + 6]
    *results, done, bias, normed, projected, attended, mixed = refs[n_in + 6 :]
    to_row = lax.broadcasted_iota(jnp.int32, bias.shape, 0)
    from_row = lax.broadcasted_iota(jnp.int32, bias.shape, 1)
    allowed = (from_row <= to_row) & (((from_row ^ to_row) & (GROUP - 1)) == 0)
    bias[...] = jnp.where(allowed, 0.0, -1e30)
    made = attend_frames(inward(refs[:n_in]), gain[...], bias, weights, normed, projected, attended, mixed)
    done[...] = jnp.concatenate([made[g] for g in range(made.shape[0])], axis=1).astype(jnp.bfloat16)
    me = lax.axis_index("frm")
    for i, (hop, result) in enumerate(zip(hops, results)):
        span = result.shape[0]
        if paired:
            result[...] = done[pl.ds((me ^ hop) // 2 * span, span)]
        else:
            result[...] = done[pl.ds((me ^ hop) * span, span)]
            results[-1][i] = done[pl.ds((me ^ hop ^ 1) * span, span)]


def attend(inward, hops, paired, pieces, weights, frames, name):
    cols, channels = pieces[0].shape[-2:]
    rows = frames * cols
    made = frames // 2
    size = made // (2 * len(hops))
    shapes = [(2 * size if paired else size, cols, channels)] * len(hops)
    if not paired:
        shapes.append((len(hops), size, cols, channels))
    norm_gain, *matrices = weights
    return pl.pallas_call(
        functools.partial(attend_kernel, inward, hops, paired, len(pieces)),
        out_shape=[jax.ShapeDtypeStruct(shape, jnp.bfloat16) for shape in shapes],
        in_specs=[INSIDE] * (len(pieces) + 6),
        out_specs=[INSIDE] * len(shapes),
        scratch_shapes=[
            pltpu.VMEM((made, cols, channels), jnp.bfloat16),
            pltpu.VMEM((frames * GROUP, frames * GROUP), jnp.float32),
            pltpu.VMEM((rows, channels), jnp.bfloat16),
            pltpu.VMEM((3, rows, channels), jnp.bfloat16),
            pltpu.VMEM((rows, channels), jnp.bfloat16),
            pltpu.VMEM((cols // GROUP, frames + 2, GROUP, channels), jnp.float32),
        ],
        compiler_params=pltpu.CompilerParams(vmem_limit_bytes=24 * MIB),
        cost_estimate=pl.CostEstimate(
            flops=rows * channels * (channels * 11 + GROUP * frames * 4),
            bytes_accessed=rows * channels * 3 + channels * channels * 14,
            transcendentals=rows * frames,
        ),
        name=name,
    )(*pieces, norm_gain[None], *matrices)


def outer_rows(hops, pieces, taken):
    _, core = place()
    made = taken.shape[1]
    pairs = []
    for i, (hop, piece) in enumerate(zip(hops, pieces)):
        pairs += [(hop, piece.at[pl.ds(core * made, made)]), (hop + 1, taken.at[i])]
    return pairs


def inner_rows(hops, pieces, taken):
    *far, own = pieces
    pairs = [(hop + j, piece.at[j]) for hop, piece in zip(hops, far) for j in range(2)]
    return pairs + [(0, own), (1, taken.at[2 * len(hops) - 1])]


def rim_kernel(hops, *refs):
    *pieces, taken, left, right = refs
    for k, piece in outer_rows(hops, pieces, taken):
        part = piece[...]
        left[k] = part[:, 0]
        right[k] = part[:, part.shape[1] - 1]


def rim(hops, pieces, taken):
    _, made, _, channels = taken.shape
    return pl.pallas_call(
        functools.partial(rim_kernel, hops),
        out_shape=[jax.ShapeDtypeStruct((2 * len(hops), made, channels), jnp.bfloat16)] * 2,
        in_specs=[INSIDE] * (len(pieces) + 1),
        out_specs=[INSIDE] * 2,
        compiler_params=pltpu.CompilerParams(vmem_limit_bytes=4 * MIB),
        name="rim",
    )(*pieces, taken)


def filter_kernel(hops, *refs):
    count = len(hops)
    taken, left, right, w_depth, out, outer, inner = refs[2 * count :]
    me = lax.axis_index("frm")
    for k, piece in outer_rows(hops, refs[:count], taken):
        outer[me ^ k] = piece[...]
    for k, piece in inner_rows(hops, refs[count : 2 * count], taken):
        inner[me ^ k] = piece[...]
    frames, height, cols, channels = out.shape
    edge = cols // 4
    lanes = 128

    def one_part(step, carry):
        part = pl.ds(pl.multiple_of(step * lanes, lanes), lanes)
        taps = [[w_depth[a, b, part] for b in range(3)] for a in range(3)]
        for frame in range(frames):

            def filtered(row):
                sides = outer[row, frame, :, part].astype(jnp.float32)
                between = inner[row, frame, :, part].astype(jnp.float32)
                mid = jnp.concatenate([sides[:edge], between, sides[edge:]], axis=0)
                spot = lax.broadcasted_iota(jnp.int32, mid.shape, 0)
                low = left[me ^ row, frame, part].astype(jnp.float32)[None]
                high = right[me ^ row, frame, part].astype(jnp.float32)[None]
                before = jnp.where(spot == 0, low, pltpu.roll(mid, 1, 0))
                after = jnp.where(spot == cols - 1, high, pltpu.roll(mid, cols - 1, 0))
                return [
                    before * taps[a][0][None] + mid * taps[a][1][None] + after * taps[a][2][None] for a in range(3)
                ]

            above = None
            here = filtered(0)
            for row in range(height):
                below = filtered(row + 1) if row + 1 < height else None
                total = here[1]
                if above is not None:
                    total = total + above[0]
                if below is not None:
                    total = total + below[2]
                out[frame, row, :, part] = total.astype(jnp.bfloat16)
                above, here = here, below
        return carry

    lax.fori_loop(0, channels // lanes, one_part, 0)


def depth_filter(hops, outer, inner, taken, left, right, w_depth):
    height, frames, channels = left.shape
    width = taken.shape[2]
    cols = 2 * width
    size = frames * height * cols * channels
    return pl.pallas_call(
        functools.partial(filter_kernel, hops),
        out_shape=jax.ShapeDtypeStruct((frames, height, cols, channels), jnp.bfloat16),
        in_specs=[INSIDE] * (2 * len(hops) + 4),
        out_specs=INSIDE,
        scratch_shapes=[pltpu.VMEM((height, frames, width, channels), jnp.bfloat16)] * 2,
        compiler_params=pltpu.CompilerParams(vmem_limit_bytes=10 * MIB),
        cost_estimate=pl.CostEstimate(flops=18 * size, bytes_accessed=4 * size, transcendentals=0),
        name="depth_filter",
    )(*outer, *inner, taken, left, right, w_depth)


def local(video, norm_gain, w_query, w_key, w_value, w_out, w_time, w_depth):
    count = lax.axis_size("frm")
    chips = count // 2
    span, height, cols, channels = video.shape
    assert height == count and chips & (chips - 1) == 0 and chips > 1
    made = span // 2
    frames = span * count
    width = cols // 2
    weights = (norm_gain, w_query, w_key, w_value, w_out, w_time)

    def swap(block, k):
        return lax.ppermute(block, "frm", [(i, i ^ k) for i in range(count)]) if k else block

    far = [chips - 1, *([1] if chips > 2 else []), *range(chips - 2, 1, -1)]
    hops = [2 * k for k in [*far, 0]]
    pieces = cut(lambda me: ([me ^ k for k in hops], [me ^ k ^ 1 for k in hops]), chips, video)
    *outer, outer_stack = pieces[: chips + 1]
    *inner, inner_stack = pieces[chips + 1 :]

    def joined(ins, outs):
        *owns, other = ins
        pairs = []
        for i, own in enumerate(owns):
            pairs.append((own, outs[i].at[pl.ds(0, span)]))
            pairs.append((other.at[i], outs[i].at[pl.ds(span, span)]))
        return pairs

    def join(owns, other, name):
        return gather(joined, [*owns[:-1], other], [(2 * span, width, channels)] * len(far), name)

    outer_other = swap(outer_stack, 1)
    outer_far = join(outer, outer_other, "join_outer")
    *outer_far, inner_stack = lax.optimization_barrier((*outer_far, inner_stack))
    outer_far = [swap(piece, k) for k, piece in zip(hops, outer_far)]
    inner_other = swap(inner_stack, 1)
    inner_far = join(inner, inner_other, "join_inner")
    outer_far[0], *inner_far = lax.optimization_barrier((outer_far[0], *inner_far))
    inner_far = [swap(piece, k) for k, piece in zip(hops, inner_far)]

    def inward(pieces):
        me = lax.axis_index("frm")
        *pieces, own, other = pieces
        pairs = []
        for k, piece in zip(hops, pieces):
            pairs.append((piece.at[pl.ds(0, span)], (me ^ k) * span))
            pairs.append((piece.at[pl.ds(span, span)], (me ^ k ^ 1) * span))
        return pairs + [(own, me * span), (other.at[len(far)], (me ^ 1) * span)]

    outer = attend(inward, hops, True, [*outer_far, outer[-1], outer_other], weights, frames, "attend_outer")
    outer = [swap(piece, k) for k, piece in zip(hops, outer)]
    *keep, give = attend(inward, hops, False, [*inner_far, inner[-1], inner_other], weights, frames, "attend_inner")

    def for_mate(ins, outs):
        _, core = place()
        *pieces, give = ins
        pairs = [(piece.at[pl.ds((1 - core) * made, made)], outs[0].at[i]) for i, piece in enumerate(pieces)]
        return pairs + [(give, outs[0].at[pl.ds(chips, chips)])]

    (stack,) = gather(for_mate, [*outer, give], [(2 * chips, made, width, channels)], "stack_back")
    taken = swap(stack, 1)

    def joined_back(ins, outs):
        *keep, taken = ins
        pairs = []
        for i, own in enumerate(keep):
            pairs += [(own, outs[i].at[0]), (taken.at[chips + i], outs[i].at[1])]
        return pairs

    inner = gather(joined_back, [*keep[:-1], taken], [(2, made, width, channels)] * len(far), "join_back")
    inner = [swap(piece, k) for k, piece in zip(hops, inner)]
    low_side, high_side = rim(hops, outer, taken)
    nearest = far.index(1)
    low_side, high_side, inner[nearest] = lax.optimization_barrier((low_side, high_side, inner[nearest]))
    line = lax.axis_size("col")
    upward = [(i, i + 1) for i in range(line - 1)]
    left = lax.ppermute(high_side, "col", upward)
    right = lax.ppermute(low_side, "col", [(b, a) for a, b in upward])
    return depth_filter(hops, outer, [*inner, keep[-1]], taken, left, right, w_depth)


def solution(mesh):
    return jax.shard_map(
        local,
        mesh=mesh,
        in_specs=(P("frm", None, "col", None), P(), P(), P(), P(), P(), P(), P()),
        out_specs=P("frm", None, "col", None),
        check_vma=False,
    )
```

```python
import functools
import math

import jax
import jax.numpy as jnp
from jax import lax
from jax.experimental import pallas as pl
from jax.experimental.pallas import tpu as pltpu
from jax.sharding import PartitionSpec as P

epsilon = 1e-06
GROUP = 8
BLOCKS = 2
TILE = 8
SOFT_ROWS = 32
MIB = 1024 * 1024
INSIDE = pl.BlockSpec(memory_space=pltpu.VMEM)


def place():
    me = lax.axis_index("frm")
    return me // 2, me % 2


def gather_kernel(pairs_of, n_in, *refs):
    for source, target in pairs_of(refs[:n_in], refs[n_in:]):
        target[...] = source[...]


def gather(pairs_of, arrays, shapes, name):
    size = sum(math.prod(shape) for shape in shapes)
    return pl.pallas_call(
        functools.partial(gather_kernel, pairs_of, len(arrays)),
        out_shape=[jax.ShapeDtypeStruct(shape, jnp.bfloat16) for shape in shapes],
        in_specs=[INSIDE] * len(arrays),
        out_specs=[INSIDE] * len(shapes),
        compiler_params=pltpu.CompilerParams(vmem_limit_bytes=6 * MIB),
        cost_estimate=pl.CostEstimate(flops=0, bytes_accessed=4 * size, transcendentals=0),
        name=name,
    )(*arrays)


def cut_kernel(rows_of, video, *results):
    edge = video.shape[2] // 4
    half = len(results) // 2
    own, other = rows_of(lax.axis_index("frm"))
    for rim in (True, False):
        *singles, stack = results[:half] if rim else results[half:]
        targets = list(singles) + [stack.at[k] for k in range(stack.shape[0])]
        for row, target in zip(own + other, targets):
            values = video[:, row].astype(jnp.float32)
            if rim:
                values = jnp.concatenate([values[:, :edge], values[:, 3 * edge :]], axis=1)
            else:
                values = values[:, edge : 3 * edge]
            target[...] = values.astype(jnp.bfloat16)


def cut(rows_of, chips, video):
    span, height, cols, channels = video.shape
    shape = (span, cols // 2, channels)
    shapes = ([shape] * chips + [(chips, *shape)]) * 2
    return pl.pallas_call(
        functools.partial(cut_kernel, rows_of),
        out_shape=[jax.ShapeDtypeStruct(shape, jnp.bfloat16) for shape in shapes],
        in_specs=[INSIDE],
        out_specs=[INSIDE] * len(shapes),
        compiler_params=pltpu.CompilerParams(vmem_limit_bytes=12 * MIB),
        cost_estimate=pl.CostEstimate(flops=0, bytes_accessed=3 * video.size, transcendentals=0),
        name="cut",
    )(video)


def attend_frames(pieces, gain, bias, weights, normed, projected, attended, mixed):
    w_query, w_key, w_value, w_out, w_time = weights
    groups, frames, _, channels = mixed.shape
    frames = frames - 2
    rows = frames * GROUP
    for piece, first in pieces:
        wide = piece[...].astype(jnp.float32)
        span = wide.shape[0]
        for group in range(groups):
            x = wide[:, group * GROUP : (group + 1) * GROUP]
            mixed[group, pl.ds(first + 1, span)] = x
            x = x.reshape(span * GROUP, channels)
            x = x * lax.rsqrt(jnp.mean(x * x, axis=-1, keepdims=True) + epsilon) * gain
            begin = pl.multiple_of(group * rows + first * GROUP, span * GROUP)
            normed[pl.ds(begin, span * GROUP)] = x.astype(jnp.bfloat16)
    for index, weight in enumerate((w_query, w_key, w_value)):
        projected[index] = jnp.dot(normed[...], weight[...], preferred_element_type=jnp.float32).astype(jnp.bfloat16)
    queries, key_proj, values = projected.at[0], projected.at[1], projected.at[2]
    height = rows // BLOCKS
    power = math.log2(math.e) / math.sqrt(channels)
    for group in range(groups):
        first = group * rows
        for block in range(BLOCKS):
            begin = block * height
            span = begin + height
            scores = lax.dot_general(
                queries[first + begin : first + span],
                key_proj[first : first + span],
                (((1,), (1,)), ((), ())),
                preferred_element_type=jnp.float32,
            )
            shares = []
            for low in range(0, height, SOFT_ROWS):
                part = scores[low : low + SOFT_ROWS] + bias[begin + low : begin + low + SOFT_ROWS, :span]
                raised = jnp.exp2((part - jnp.max(part, axis=-1, keepdims=True)) * power)
                scale = 1.0 / jnp.sum(raised, axis=-1, keepdims=True)
                shares.append((raised * scale).astype(jnp.bfloat16))
            attended[first + begin : first + span] = jnp.dot(
                jnp.concatenate(shares, axis=0), values[first : first + span], preferred_element_type=jnp.float32
            ).astype(jnp.bfloat16)
    out = jnp.dot(attended[...], w_out[...], preferred_element_type=jnp.float32).reshape(
        groups, frames, GROUP, channels
    )
    for group in range(groups):
        for first in range(0, frames, TILE):
            x = mixed[group, first + 1 : first + 1 + TILE] + out[group, first : first + TILE]
            mixed[group, first + 1 : first + 1 + TILE] = x
            if first == 0:
                mixed[group, 0] = x[0]
    taps = []
    for tap in range(3):
        parts = []
        for group in range(groups):
            view = mixed[group, tap - tap % 2 : tap - tap % 2 + frames].reshape(frames // 2, 2, GROUP, channels)
            parts.append(view[:, tap % 2].reshape(rows // 2, channels).astype(jnp.bfloat16))
        taps.append(jnp.dot(jnp.concatenate(parts, axis=0), w_time[tap], preferred_element_type=jnp.float32))
    summed = (taps[0] + taps[1]) + taps[2]
    return (summed / (1.0 + jnp.exp(-summed))).reshape(groups, frames // 2, GROUP, channels)


def attend_kernel(inward, hops, paired, n_in, *refs):
    gain, *weights = refs[n_in : n_in + 6]
    *results, done, bias, normed, projected, attended, mixed = refs[n_in + 6 :]
    to_row = lax.broadcasted_iota(jnp.int32, bias.shape, 0)
    from_row = lax.broadcasted_iota(jnp.int32, bias.shape, 1)
    allowed = (from_row <= to_row) & (((from_row ^ to_row) & (GROUP - 1)) == 0)
    bias[...] = jnp.where(allowed, 0.0, -1e30)
    made = attend_frames(inward(refs[:n_in]), gain[...], bias, weights, normed, projected, attended, mixed)
    done[...] = jnp.concatenate([made[g] for g in range(made.shape[0])], axis=1).astype(jnp.bfloat16)
    me = lax.axis_index("frm")
    for i, (hop, result) in enumerate(zip(hops, results)):
        span = result.shape[0]
        if paired:
            result[...] = done[pl.ds((me ^ hop) // 2 * span, span)]
        else:
            result[...] = done[pl.ds((me ^ hop) * span, span)]
            results[-1][i] = done[pl.ds((me ^ hop ^ 1) * span, span)]


def attend(inward, hops, paired, pieces, weights, frames, name):
    cols, channels = pieces[0].shape[-2:]
    rows = frames * cols
    made = frames // 2
    size = made // (2 * len(hops))
    shapes = [(2 * size if paired else size, cols, channels)] * len(hops)
    if not paired:
        shapes.append((len(hops), size, cols, channels))
    norm_gain, *matrices = weights
    return pl.pallas_call(
        functools.partial(attend_kernel, inward, hops, paired, len(pieces)),
        out_shape=[jax.ShapeDtypeStruct(shape, jnp.bfloat16) for shape in shapes],
        in_specs=[INSIDE] * (len(pieces) + 6),
        out_specs=[INSIDE] * len(shapes),
        scratch_shapes=[
            pltpu.VMEM((made, cols, channels), jnp.bfloat16),
            pltpu.VMEM((frames * GROUP, frames * GROUP), jnp.float32),
            pltpu.VMEM((rows, channels), jnp.bfloat16),
            pltpu.VMEM((3, rows, channels), jnp.bfloat16),
            pltpu.VMEM((rows, channels), jnp.bfloat16),
            pltpu.VMEM((cols // GROUP, frames + 2, GROUP, channels), jnp.float32),
        ],
        compiler_params=pltpu.CompilerParams(vmem_limit_bytes=24 * MIB),
        cost_estimate=pl.CostEstimate(
            flops=rows * channels * (channels * 11 + GROUP * frames * 4),
            bytes_accessed=rows * channels * 3 + channels * channels * 14,
            transcendentals=rows * frames,
        ),
        name=name,
    )(*pieces, norm_gain[None], *matrices)


def outer_rows(hops, pieces, taken):
    _, core = place()
    made = taken.shape[1]
    pairs = []
    for i, (hop, piece) in enumerate(zip(hops, pieces)):
        pairs += [(hop, piece.at[pl.ds(core * made, made)]), (hop + 1, taken.at[i])]
    return pairs


def inner_rows(hops, pieces, taken):
    *far, own = pieces
    pairs = [(hop + j, piece.at[j]) for hop, piece in zip(hops, far) for j in range(2)]
    return pairs + [(0, own), (1, taken.at[2 * len(hops) - 1])]


def rim_kernel(hops, *refs):
    *pieces, taken, left, right = refs
    for k, piece in outer_rows(hops, pieces, taken):
        part = piece[...]
        left[k] = part[:, 0]
        right[k] = part[:, part.shape[1] - 1]


def rim(hops, pieces, taken):
    _, made, _, channels = taken.shape
    return pl.pallas_call(
        functools.partial(rim_kernel, hops),
        out_shape=[jax.ShapeDtypeStruct((2 * len(hops), made, channels), jnp.bfloat16)] * 2,
        in_specs=[INSIDE] * (len(pieces) + 1),
        out_specs=[INSIDE] * 2,
        compiler_params=pltpu.CompilerParams(vmem_limit_bytes=4 * MIB),
        name="rim",
    )(*pieces, taken)


def filter_kernel(hops, *refs):
    count = len(hops)
    taken, left, right, w_depth, out, outer, inner = refs[2 * count :]
    me = lax.axis_index("frm")
    for k, piece in outer_rows(hops, refs[:count], taken):
        outer[me ^ k] = piece[...]
    for k, piece in inner_rows(hops, refs[count : 2 * count], taken):
        inner[me ^ k] = piece[...]
    frames, height, cols, channels = out.shape
    edge = cols // 4
    lanes = 128

    def one_part(step, carry):
        part = pl.ds(pl.multiple_of(step * lanes, lanes), lanes)
        taps = [[w_depth[a, b, part] for b in range(3)] for a in range(3)]
        for frame in range(frames):

            def filtered(row):
                sides = outer[row, frame, :, part].astype(jnp.float32)
                between = inner[row, frame, :, part].astype(jnp.float32)
                mid = jnp.concatenate([sides[:edge], between, sides[edge:]], axis=0)
                spot = lax.broadcasted_iota(jnp.int32, mid.shape, 0)
                low = left[me ^ row, frame, part].astype(jnp.float32)[None]
                high = right[me ^ row, frame, part].astype(jnp.float32)[None]
                before = jnp.where(spot == 0, low, pltpu.roll(mid, 1, 0))
                after = jnp.where(spot == cols - 1, high, pltpu.roll(mid, cols - 1, 0))
                return [
                    before * taps[a][0][None] + mid * taps[a][1][None] + after * taps[a][2][None] for a in range(3)
                ]

            above = None
            here = filtered(0)
            for row in range(height):
                below = filtered(row + 1) if row + 1 < height else None
                total = here[1]
                if above is not None:
                    total = total + above[0]
                if below is not None:
                    total = total + below[2]
                out[frame, row, :, part] = total.astype(jnp.bfloat16)
                above, here = here, below
        return carry

    lax.fori_loop(0, channels // lanes, one_part, 0)


def depth_filter(hops, outer, inner, taken, left, right, w_depth):
    height, frames, channels = left.shape
    width = taken.shape[2]
    cols = 2 * width
    size = frames * height * cols * channels
    return pl.pallas_call(
        functools.partial(filter_kernel, hops),
        out_shape=jax.ShapeDtypeStruct((frames, height, cols, channels), jnp.bfloat16),
        in_specs=[INSIDE] * (2 * len(hops) + 4),
        out_specs=INSIDE,
        scratch_shapes=[pltpu.VMEM((height, frames, width, channels), jnp.bfloat16)] * 2,
        compiler_params=pltpu.CompilerParams(vmem_limit_bytes=10 * MIB),
        cost_estimate=pl.CostEstimate(flops=18 * size, bytes_accessed=4 * size, transcendentals=0),
        name="depth_filter",
    )(*outer, *inner, taken, left, right, w_depth)


def local(video, norm_gain, w_query, w_key, w_value, w_out, w_time, w_depth):
    count = lax.axis_size("frm")
    chips = count // 2
    span, height, cols, channels = video.shape
    assert height == count and chips & (chips - 1) == 0 and chips > 1
    made = span // 2
    frames = span * count
    width = cols // 2
    weights = (norm_gain, w_query, w_key, w_value, w_out, w_time)

    def swap(block, k):
        return lax.ppermute(block, "frm", [(i, i ^ k) for i in range(count)]) if k else block

    far = [chips - 1, *([1] if chips > 2 else []), *range(chips - 2, 1, -1)]
    hops = [2 * k for k in [*far, 0]]
    pieces = cut(lambda me: ([me ^ k for k in hops], [me ^ k ^ 1 for k in hops]), chips, video)
    *outer, outer_stack = pieces[: chips + 1]
    *inner, inner_stack = pieces[chips + 1 :]

    def joined(ins, outs):
        *owns, other = ins
        pairs = []
        for i, own in enumerate(owns):
            pairs.append((own, outs[i].at[pl.ds(0, span)]))
            pairs.append((other.at[i], outs[i].at[pl.ds(span, span)]))
        return pairs

    def join(owns, other, name):
        return gather(joined, [*owns[:-1], other], [(2 * span, width, channels)] * len(far), name)

    outer_other = swap(outer_stack, 1)
    outer_far = join(outer, outer_other, "join_outer")
    *outer_far, inner_stack = lax.optimization_barrier((*outer_far, inner_stack))
    outer_far = [swap(piece, k) for k, piece in zip(hops, outer_far)]
    inner_other = swap(inner_stack, 1)
    inner_far = join(inner, inner_other, "join_inner")
    outer_far[0], *inner_far = lax.optimization_barrier((outer_far[0], *inner_far))
    inner_far = [swap(piece, k) for k, piece in zip(hops, inner_far)]

    def inward(pieces):
        me = lax.axis_index("frm")
        *pieces, own, other = pieces
        pairs = []
        for k, piece in zip(hops, pieces):
            pairs.append((piece.at[pl.ds(0, span)], (me ^ k) * span))
            pairs.append((piece.at[pl.ds(span, span)], (me ^ k ^ 1) * span))
        return pairs + [(own, me * span), (other.at[len(far)], (me ^ 1) * span)]

    outer = list(attend(inward, hops, True, [*outer_far, outer[-1], outer_other], weights, frames, "attend_outer"))
    outer[:2], inner_far[0] = lax.optimization_barrier((outer[:2], inner_far[0]))
    for i in range(2, len(far)):
        outer[i], inner_far[i] = lax.optimization_barrier((outer[i], inner_far[i]))
    outer = [swap(piece, k) for k, piece in zip(hops, outer)]
    *keep, give = attend(inward, hops, False, [*inner_far, inner[-1], inner_other], weights, frames, "attend_inner")

    def for_mate(ins, outs):
        _, core = place()
        *pieces, give = ins
        pairs = [(piece.at[pl.ds((1 - core) * made, made)], outs[0].at[i]) for i, piece in enumerate(pieces)]
        return pairs + [(give, outs[0].at[pl.ds(chips, chips)])]

    (stack,) = gather(for_mate, [*outer, give], [(2 * chips, made, width, channels)], "stack_back")
    taken = swap(stack, 1)

    def joined_back(ins, outs):
        *keep, taken = ins
        pairs = []
        for i, own in enumerate(keep):
            pairs += [(own, outs[i].at[0]), (taken.at[chips + i], outs[i].at[1])]
        return pairs

    inner = gather(joined_back, [*keep[:-1], taken], [(2, made, width, channels)] * len(far), "join_back")
    inner = [swap(piece, k) for k, piece in zip(hops, inner)]
    low_side, high_side = rim(hops, outer, taken)
    nearest = far.index(1)
    low_side, high_side, inner[nearest] = lax.optimization_barrier((low_side, high_side, inner[nearest]))
    line = lax.axis_size("col")
    upward = [(i, i + 1) for i in range(line - 1)]
    left = lax.ppermute(high_side, "col", upward)
    right = lax.ppermute(low_side, "col", [(b, a) for a, b in upward])
    return depth_filter(hops, outer, [*inner, keep[-1]], taken, left, right, w_depth)


def solution(mesh):
    return jax.shard_map(
        local,
        mesh=mesh,
        in_specs=(P("frm", None, "col", None), P(), P(), P(), P(), P(), P(), P()),
        out_specs=P("frm", None, "col", None),
        check_vma=False,
    )
```

```python
import functools
import math

import jax
import jax.numpy as jnp
from jax import lax
from jax.experimental import pallas as pl
from jax.experimental.pallas import tpu as pltpu
from jax.sharding import PartitionSpec as P

epsilon = 1e-06
GROUP = 8
BLOCKS = 2
TILE = 8
SOFT_ROWS = 32
MIB = 1024 * 1024
SMALL = pl.CostEstimate(flops=1, bytes_accessed=1, transcendentals=0)
INSIDE = pl.BlockSpec(memory_space=pltpu.VMEM)


def place():
    me = lax.axis_index("frm")
    return me // 2, me % 2


def gather_kernel(pairs_of, n_in, *refs):
    for source, target in pairs_of(refs[:n_in], refs[n_in:]):
        target[...] = source[...]


def gather(pairs_of, arrays, shapes, name):
    size = sum(math.prod(shape) for shape in shapes)
    return pl.pallas_call(
        functools.partial(gather_kernel, pairs_of, len(arrays)),
        out_shape=[jax.ShapeDtypeStruct(shape, jnp.bfloat16) for shape in shapes],
        in_specs=[INSIDE] * len(arrays),
        out_specs=[INSIDE] * len(shapes),
        compiler_params=pltpu.CompilerParams(vmem_limit_bytes=6 * MIB),
        cost_estimate=SMALL,
        name=name,
    )(*arrays)


def cut_kernel(rows_of, video, *results):
    edge = video.shape[2] // 4
    half = len(results) // 2
    own, other = rows_of(lax.axis_index("frm"))
    for rim in (True, False):
        *singles, stack = results[:half] if rim else results[half:]
        targets = list(singles) + [stack.at[k] for k in range(stack.shape[0])]
        for row, target in zip(own + other, targets):
            values = video[:, row].astype(jnp.float32)
            if rim:
                values = jnp.concatenate([values[:, :edge], values[:, 3 * edge :]], axis=1)
            else:
                values = values[:, edge : 3 * edge]
            target[...] = values.astype(jnp.bfloat16)


def cut(rows_of, chips, video):
    span, height, cols, channels = video.shape
    shape = (span, cols // 2, channels)
    shapes = ([shape] * chips + [(chips, *shape)]) * 2
    return pl.pallas_call(
        functools.partial(cut_kernel, rows_of),
        out_shape=[jax.ShapeDtypeStruct(shape, jnp.bfloat16) for shape in shapes],
        in_specs=[INSIDE],
        out_specs=[INSIDE] * len(shapes),
        compiler_params=pltpu.CompilerParams(vmem_limit_bytes=12 * MIB),
        cost_estimate=SMALL,
        name="cut",
    )(video)


def attend_frames(pieces, gain, bias, weights, normed, projected, attended, mixed):
    w_query, w_key, w_value, w_out, w_time = weights
    groups, frames, _, channels = mixed.shape
    frames = frames - 2
    rows = frames * GROUP
    for piece, first in pieces:
        wide = piece[...].astype(jnp.float32)
        span = wide.shape[0]
        for group in range(groups):
            x = wide[:, group * GROUP : (group + 1) * GROUP]
            mixed[group, pl.ds(first + 1, span)] = x
            x = x.reshape(span * GROUP, channels)
            x = x * lax.rsqrt(jnp.mean(x * x, axis=-1, keepdims=True) + epsilon) * gain
            begin = pl.multiple_of(group * rows + first * GROUP, span * GROUP)
            normed[pl.ds(begin, span * GROUP)] = x.astype(jnp.bfloat16)
    for index, weight in enumerate((w_query, w_key, w_value)):
        projected[index] = jnp.dot(normed[...], weight[...], preferred_element_type=jnp.float32).astype(jnp.bfloat16)
    queries, key_proj, values = projected.at[0], projected.at[1], projected.at[2]
    height = rows // BLOCKS
    power = math.log2(math.e) / math.sqrt(channels)
    for group in range(groups):
        first = group * rows
        for block in range(BLOCKS):
            begin = block * height
            span = begin + height
            scores = lax.dot_general(
                queries[first + begin : first + span],
                key_proj[first : first + span],
                (((1,), (1,)), ((), ())),
                preferred_element_type=jnp.float32,
            )
            shares = []
            for low in range(0, height, SOFT_ROWS):
                part = scores[low : low + SOFT_ROWS] + bias[begin + low : begin + low + SOFT_ROWS, :span]
                raised = jnp.exp2((part - jnp.max(part, axis=-1, keepdims=True)) * power)
                scale = 1.0 / jnp.sum(raised, axis=-1, keepdims=True)
                shares.append((raised * scale).astype(jnp.bfloat16))
            attended[first + begin : first + span] = jnp.dot(
                jnp.concatenate(shares, axis=0), values[first : first + span], preferred_element_type=jnp.float32
            ).astype(jnp.bfloat16)
    out = jnp.dot(attended[...], w_out[...], preferred_element_type=jnp.float32).reshape(
        groups, frames, GROUP, channels
    )
    for group in range(groups):
        for first in range(0, frames, TILE):
            x = mixed[group, first + 1 : first + 1 + TILE] + out[group, first : first + TILE]
            mixed[group, first + 1 : first + 1 + TILE] = x
            if first == 0:
                mixed[group, 0] = x[0]
    taps = []
    for tap in range(3):
        parts = []
        for group in range(groups):
            view = mixed[group, tap - tap % 2 : tap - tap % 2 + frames].reshape(frames // 2, 2, GROUP, channels)
            parts.append(view[:, tap % 2].reshape(rows // 2, channels).astype(jnp.bfloat16))
        taps.append(jnp.dot(jnp.concatenate(parts, axis=0), w_time[tap], preferred_element_type=jnp.float32))
    summed = (taps[0] + taps[1]) + taps[2]
    return (summed / (1.0 + jnp.exp(-summed))).reshape(groups, frames // 2, GROUP, channels)


def attend_kernel(inward, hops, paired, n_in, *refs):
    gain, *weights = refs[n_in : n_in + 6]
    *results, done, bias, normed, projected, attended, mixed = refs[n_in + 6 :]
    to_row = lax.broadcasted_iota(jnp.int32, bias.shape, 0)
    from_row = lax.broadcasted_iota(jnp.int32, bias.shape, 1)
    allowed = (from_row <= to_row) & (((from_row ^ to_row) & (GROUP - 1)) == 0)
    bias[...] = jnp.where(allowed, 0.0, -1e30)
    made = attend_frames(inward(refs[:n_in]), gain[...], bias, weights, normed, projected, attended, mixed)
    done[...] = jnp.concatenate([made[g] for g in range(made.shape[0])], axis=1).astype(jnp.bfloat16)
    me = lax.axis_index("frm")
    for i, (hop, result) in enumerate(zip(hops, results)):
        span = result.shape[0]
        if paired:
            result[...] = done[pl.ds((me ^ hop) // 2 * span, span)]
        else:
            result[...] = done[pl.ds((me ^ hop) * span, span)]
            results[-1][i] = done[pl.ds((me ^ hop ^ 1) * span, span)]


def attend(inward, hops, paired, pieces, weights, frames, name):
    cols, channels = pieces[0].shape[-2:]
    rows = frames * cols
    made = frames // 2
    size = made // (2 * len(hops))
    shapes = [(2 * size if paired else size, cols, channels)] * len(hops)
    if not paired:
        shapes.append((len(hops), size, cols, channels))
    norm_gain, *matrices = weights
    return pl.pallas_call(
        functools.partial(attend_kernel, inward, hops, paired, len(pieces)),
        out_shape=[jax.ShapeDtypeStruct(shape, jnp.bfloat16) for shape in shapes],
        in_specs=[INSIDE] * (len(pieces) + 6),
        out_specs=[INSIDE] * len(shapes),
        scratch_shapes=[
            pltpu.VMEM((made, cols, channels), jnp.bfloat16),
            pltpu.VMEM((frames * GROUP, frames * GROUP), jnp.float32),
            pltpu.VMEM((rows, channels), jnp.bfloat16),
            pltpu.VMEM((3, rows, channels), jnp.bfloat16),
            pltpu.VMEM((rows, channels), jnp.bfloat16),
            pltpu.VMEM((cols // GROUP, frames + 2, GROUP, channels), jnp.float32),
        ],
        compiler_params=pltpu.CompilerParams(vmem_limit_bytes=24 * MIB),
        cost_estimate=SMALL,
        name=name,
    )(*pieces, norm_gain[None], *matrices)


def outer_rows(hops, pieces, taken):
    _, core = place()
    made = taken.shape[1]
    pairs = []
    for i, (hop, piece) in enumerate(zip(hops, pieces)):
        pairs += [(hop, piece.at[pl.ds(core * made, made)]), (hop + 1, taken.at[i])]
    return pairs


def inner_rows(hops, pieces, taken):
    *far, own = pieces
    pairs = [(hop + j, piece.at[j]) for hop, piece in zip(hops, far) for j in range(2)]
    return pairs + [(0, own), (1, taken.at[len(far)])]


def rim_kernel(hops, *refs):
    *pieces, taken, left, right = refs
    for k, piece in outer_rows(hops, pieces, taken):
        part = piece[...]
        left[k] = part[:, 0]
        right[k] = part[:, part.shape[1] - 1]


def rim(hops, pieces, taken):
    _, made, _, channels = taken.shape
    return pl.pallas_call(
        functools.partial(rim_kernel, hops),
        out_shape=[jax.ShapeDtypeStruct((2 * len(hops), made, channels), jnp.bfloat16)] * 2,
        in_specs=[INSIDE] * (len(pieces) + 1),
        out_specs=[INSIDE] * 2,
        compiler_params=pltpu.CompilerParams(vmem_limit_bytes=4 * MIB),
        name="rim",
    )(*pieces, taken)


def filter_kernel(hops, *refs):
    count = len(hops) + 1
    left, right, w_depth, result, outer, inner, out, sems = refs[2 * count :]
    me = lax.axis_index("frm")
    for k, piece in outer_rows(hops, refs[: count - 1], refs[count - 1]):
        outer[me ^ k] = piece[...]
    for k, piece in inner_rows(hops, refs[count : 2 * count - 1], refs[2 * count - 1]):
        inner[me ^ k] = piece[...]
    frames, height, cols, channels = out.shape
    edge = cols // 4
    lanes = 128

    copies = [pltpu.make_async_copy(out.at[frame], result.at[frame], sems.at[frame]) for frame in range(frames)]
    for frame in range(frames):
        for first in range(0, channels, lanes):
            part = pl.ds(first, lanes)
            taps = [[w_depth[a, b, part] for b in range(3)] for a in range(3)]

            def filtered(row):
                sides = outer[row, frame, :, part].astype(jnp.float32)
                between = inner[row, frame, :, part].astype(jnp.float32)
                mid = jnp.concatenate([sides[:edge], between, sides[edge:]], axis=0)
                spot = lax.broadcasted_iota(jnp.int32, mid.shape, 0)
                low = left[me ^ row, frame, part].astype(jnp.float32)[None]
                high = right[me ^ row, frame, part].astype(jnp.float32)[None]
                before = jnp.where(spot == 0, low, pltpu.roll(mid, 1, 0))
                after = jnp.where(spot == cols - 1, high, pltpu.roll(mid, cols - 1, 0))
                return [
                    before * taps[a][0][None] + mid * taps[a][1][None] + after * taps[a][2][None] for a in range(3)
                ]

            above = None
            here = filtered(0)
            for row in range(height):
                below = filtered(row + 1) if row + 1 < height else None
                total = here[1]
                if above is not None:
                    total = total + above[0]
                if below is not None:
                    total = total + below[2]
                out[frame, row, :, part] = total.astype(jnp.bfloat16)
                above, here = here, below
        copies[frame].start()
    for copy in copies:
        copy.wait()


def depth_filter(hops, outer, inner, left, right, w_depth):
    height, frames, channels = left.shape
    width = inner[-1].shape[2]
    cols = 2 * width
    size = frames * height * cols * channels
    return pl.pallas_call(
        functools.partial(filter_kernel, hops),
        out_shape=jax.ShapeDtypeStruct((frames, height, cols, channels), jnp.bfloat16),
        in_specs=[INSIDE] * (2 * len(hops) + 5),
        out_specs=pl.BlockSpec(memory_space=pl.ANY),
        scratch_shapes=[
            *[pltpu.VMEM((height, frames, width, channels), jnp.bfloat16)] * 2,
            pltpu.VMEM((frames, height, cols, channels), jnp.bfloat16),
            pltpu.SemaphoreType.DMA((frames,)),
        ],
        compiler_params=pltpu.CompilerParams(vmem_limit_bytes=10 * MIB),
        cost_estimate=SMALL,
        name="depth_filter",
    )(*outer, *inner, left, right, w_depth)


def local(video, norm_gain, w_query, w_key, w_value, w_out, w_time, w_depth):
    count = lax.axis_size("frm")
    chips = count // 2
    span, height, cols, channels = video.shape
    assert height == count and chips & (chips - 1) == 0 and chips > 1
    made = span // 2
    frames = span * count
    width = cols // 2
    weights = (norm_gain, w_query, w_key, w_value, w_out, w_time)

    def swap(block, k):
        return lax.ppermute(block, "frm", [(i, i ^ k) for i in range(count)]) if k else block

    far = [chips - 1, *([1] if chips > 2 else []), *range(chips - 2, 1, -1)]
    hops = [2 * k for k in [*far, 0]]
    pieces = cut(lambda me: ([me ^ k for k in hops], [me ^ k ^ 1 for k in hops]), chips, video)
    *outer, outer_stack = pieces[: chips + 1]
    *inner, inner_stack = pieces[chips + 1 :]

    def joined(ins, outs):
        *owns, other = ins
        pairs = []
        for i, own in enumerate(owns):
            pairs.append((own, outs[i].at[pl.ds(0, span)]))
            pairs.append((other.at[i], outs[i].at[pl.ds(span, span)]))
        return pairs

    def join(owns, other, name):
        return gather(joined, [*owns[:-1], other], [(2 * span, width, channels)] * len(far), name)

    outer_other = swap(outer_stack, 1)
    outer_far = join(outer, outer_other, "join_outer")
    *outer_far, inner_stack = lax.optimization_barrier((*outer_far, inner_stack))
    outer_far = [swap(piece, k) for k, piece in zip(hops, outer_far)]
    nearest = far.index(1)
    inner_other = swap(inner_stack, 1)
    inner_far = join(inner, inner_other, "join_inner")
    outer_far[0], *inner_far = lax.optimization_barrier((outer_far[0], *inner_far))
    inner_far = [swap(piece, k) for k, piece in zip(hops, inner_far)]

    def inward(pieces):
        me = lax.axis_index("frm")
        *pieces, own, other = pieces
        pairs = []
        for k, piece in zip(hops, pieces):
            pairs.append((piece.at[pl.ds(0, span)], (me ^ k) * span))
            pairs.append((piece.at[pl.ds(span, span)], (me ^ k ^ 1) * span))
        return pairs + [(own, me * span), (other.at[len(far)], (me ^ 1) * span)]

    outer = list(attend(inward, hops, True, [*outer_far, outer[-1], outer_other], weights, frames, "attend_outer"))
    outer[:2], inner_far[0] = lax.optimization_barrier((outer[:2], inner_far[0]))
    for i in range(2, len(far)):
        outer[i], inner_far[i] = lax.optimization_barrier((outer[i], inner_far[i]))
    outer = [swap(piece, k) for k, piece in zip(hops, outer)]
    *keep, give = attend(inward, hops, False, [*inner_far, inner[-1], inner_other], weights, frames, "attend_inner")

    outer[:2], give = lax.optimization_barrier((outer[:2], give))
    taken = swap(give, 1)

    def joined_back(ins, outs):
        *keep, taken = ins
        pairs = []
        for i, own in enumerate(keep):
            pairs += [(own, outs[i].at[0]), (taken.at[i], outs[i].at[1])]
        return pairs

    inner = gather(joined_back, [*keep[:-1], taken], [(2, made, width, channels)] * len(far), "join_back")
    inner = [swap(piece, k) for k, piece in zip(hops, inner)]

    def for_mate(ins, outs):
        _, core = place()
        return [(piece.at[pl.ds((1 - core) * made, made)], outs[0].at[i]) for i, piece in enumerate(ins)]

    (stack,) = gather(for_mate, outer, [(chips, made, width, channels)], "stack_back")
    halves = swap(stack, 1)
    low_side, high_side = rim(hops, outer, halves)
    low_side, high_side, inner[nearest] = lax.optimization_barrier((low_side, high_side, inner[nearest]))
    line = lax.axis_size("col")
    upward = [(i, i + 1) for i in range(line - 1)]
    left = lax.ppermute(high_side, "col", upward)
    right = lax.ppermute(low_side, "col", [(b, a) for a, b in upward])
    return depth_filter(hops, [*outer, halves], [*inner, keep[-1], taken], left, right, w_depth)


def solution(mesh):
    return jax.shard_map(
        local,
        mesh=mesh,
        in_specs=(P("frm", None, "col", None), P(), P(), P(), P(), P(), P(), P()),
        out_specs=P("frm", None, "col", None),
        check_vma=False,
    )
```

```python
import functools
import math

import jax
import jax.numpy as jnp
from jax import lax
from jax.experimental import pallas as pl
from jax.experimental.pallas import tpu as pltpu
from jax.sharding import PartitionSpec as P

epsilon = 1e-06
GROUP = 8
BLOCKS = 2
TILE = 8
SOFT_ROWS = 32
MIB = 1024 * 1024
SMALL = pl.CostEstimate(flops=1, bytes_accessed=1, transcendentals=0)
INSIDE = pl.BlockSpec(memory_space=pltpu.VMEM)


def place():
    me = lax.axis_index("frm")
    return me // 2, me % 2


def gather_kernel(pairs_of, n_in, *refs):
    for source, target in pairs_of(refs[:n_in], refs[n_in:]):
        target[...] = source[...]


def gather(pairs_of, arrays, shapes, name):
    size = sum(math.prod(shape) for shape in shapes)
    return pl.pallas_call(
        functools.partial(gather_kernel, pairs_of, len(arrays)),
        out_shape=[jax.ShapeDtypeStruct(shape, jnp.bfloat16) for shape in shapes],
        in_specs=[INSIDE] * len(arrays),
        out_specs=[INSIDE] * len(shapes),
        compiler_params=pltpu.CompilerParams(vmem_limit_bytes=6 * MIB),
        cost_estimate=SMALL,
        name=name,
    )(*arrays)


def cut_kernel(rows_of, video, *results):
    edge = video.shape[2] // 4
    half = len(results) // 2
    own, other = rows_of(lax.axis_index("frm"))
    for rim in (True, False):
        *singles, stack = results[:half] if rim else results[half:]
        targets = list(singles) + [stack.at[k] for k in range(stack.shape[0])]
        for row, target in zip(own + other, targets):
            values = video[:, row].astype(jnp.float32)
            if rim:
                values = jnp.concatenate([values[:, :edge], values[:, 2 * edge :]], axis=1)
            else:
                values = values[:, edge : 2 * edge]
            target[...] = values.astype(jnp.bfloat16)


def cut(rows_of, chips, video):
    span, height, cols, channels = video.shape
    shapes = []
    for width in (cols - cols // 4, cols // 4):
        shapes += [(span, width, channels)] * chips + [(chips, span, width, channels)]
    return pl.pallas_call(
        functools.partial(cut_kernel, rows_of),
        out_shape=[jax.ShapeDtypeStruct(shape, jnp.bfloat16) for shape in shapes],
        in_specs=[INSIDE],
        out_specs=[INSIDE] * len(shapes),
        compiler_params=pltpu.CompilerParams(vmem_limit_bytes=12 * MIB),
        cost_estimate=SMALL,
        name="cut",
    )(video)


def attend_frames(pieces, gain, bias, weights, normed, projected, attended, mixed):
    w_query, w_key, w_value, w_out, w_time = weights
    groups, frames, _, channels = mixed.shape
    frames = frames - 2
    rows = frames * GROUP
    for piece, first in pieces:
        wide = piece[...].astype(jnp.float32)
        span = wide.shape[0]
        for group in range(groups):
            x = wide[:, group * GROUP : (group + 1) * GROUP]
            mixed[group, pl.ds(first + 1, span)] = x
            x = x.reshape(span * GROUP, channels)
            x = x * lax.rsqrt(jnp.mean(x * x, axis=-1, keepdims=True) + epsilon) * gain
            begin = pl.multiple_of(group * rows + first * GROUP, span * GROUP)
            normed[pl.ds(begin, span * GROUP)] = x.astype(jnp.bfloat16)
    for index, weight in enumerate((w_query, w_key, w_value)):
        projected[index] = jnp.dot(normed[...], weight[...], preferred_element_type=jnp.float32).astype(jnp.bfloat16)
    queries, key_proj, values = projected.at[0], projected.at[1], projected.at[2]
    height = rows // BLOCKS
    power = math.log2(math.e) / math.sqrt(channels)
    for group in range(groups):
        first = group * rows
        for block in range(BLOCKS):
            begin = block * height
            span = begin + height
            scores = lax.dot_general(
                queries[first + begin : first + span],
                key_proj[first : first + span],
                (((1,), (1,)), ((), ())),
                preferred_element_type=jnp.float32,
            )
            shares = []
            for low in range(0, height, SOFT_ROWS):
                part = scores[low : low + SOFT_ROWS] + bias[begin + low : begin + low + SOFT_ROWS, :span]
                raised = jnp.exp2((part - jnp.max(part, axis=-1, keepdims=True)) * power)
                scale = 1.0 / jnp.sum(raised, axis=-1, keepdims=True)
                shares.append((raised * scale).astype(jnp.bfloat16))
            attended[first + begin : first + span] = jnp.dot(
                jnp.concatenate(shares, axis=0), values[first : first + span], preferred_element_type=jnp.float32
            ).astype(jnp.bfloat16)
    out = jnp.dot(attended[...], w_out[...], preferred_element_type=jnp.float32).reshape(
        groups, frames, GROUP, channels
    )
    for group in range(groups):
        for first in range(0, frames, TILE):
            x = mixed[group, first + 1 : first + 1 + TILE] + out[group, first : first + TILE]
            mixed[group, first + 1 : first + 1 + TILE] = x
            if first == 0:
                mixed[group, 0] = x[0]
    taps = []
    for tap in range(3):
        parts = []
        for group in range(groups):
            view = mixed[group, tap - tap % 2 : tap - tap % 2 + frames].reshape(frames // 2, 2, GROUP, channels)
            parts.append(view[:, tap % 2].reshape(rows // 2, channels).astype(jnp.bfloat16))
        taps.append(jnp.dot(jnp.concatenate(parts, axis=0), w_time[tap], preferred_element_type=jnp.float32))
    summed = (taps[0] + taps[1]) + taps[2]
    return (summed / (1.0 + jnp.exp(-summed))).reshape(groups, frames // 2, GROUP, channels)


def attend_kernel(inward, hops, paired, n_in, *refs):
    gain, *weights = refs[n_in : n_in + 6]
    *results, done, bias, normed, projected, attended, mixed = refs[n_in + 6 :]
    to_row = lax.broadcasted_iota(jnp.int32, bias.shape, 0)
    from_row = lax.broadcasted_iota(jnp.int32, bias.shape, 1)
    allowed = (from_row <= to_row) & (((from_row ^ to_row) & (GROUP - 1)) == 0)
    bias[...] = jnp.where(allowed, 0.0, -1e30)
    made = attend_frames(inward(refs[:n_in]), gain[...], bias, weights, normed, projected, attended, mixed)
    done[...] = jnp.concatenate([made[g] for g in range(made.shape[0])], axis=1).astype(jnp.bfloat16)
    me = lax.axis_index("frm")
    for i, (hop, result) in enumerate(zip(hops, results)):
        span = result.shape[0]
        if paired:
            result[...] = done[pl.ds((me ^ hop) // 2 * span, span)]
        else:
            result[...] = done[pl.ds((me ^ hop) * span, span)]
            results[-1][i] = done[pl.ds((me ^ hop ^ 1) * span, span)]


def attend(inward, hops, paired, pieces, weights, frames, name):
    cols, channels = pieces[0].shape[-2:]
    rows = frames * cols
    made = frames // 2
    size = made // (2 * len(hops))
    shapes = [(2 * size if paired else size, cols, channels)] * len(hops)
    if not paired:
        shapes.append((len(hops), size, cols, channels))
    norm_gain, *matrices = weights
    return pl.pallas_call(
        functools.partial(attend_kernel, inward, hops, paired, len(pieces)),
        out_shape=[jax.ShapeDtypeStruct(shape, jnp.bfloat16) for shape in shapes],
        in_specs=[INSIDE] * (len(pieces) + 6),
        out_specs=[INSIDE] * len(shapes),
        scratch_shapes=[
            pltpu.VMEM((made, cols, channels), jnp.bfloat16),
            pltpu.VMEM((frames * GROUP, frames * GROUP), jnp.float32),
            pltpu.VMEM((rows, channels), jnp.bfloat16),
            pltpu.VMEM((3, rows, channels), jnp.bfloat16),
            pltpu.VMEM((rows, channels), jnp.bfloat16),
            pltpu.VMEM((cols // GROUP, frames + 2, GROUP, channels), jnp.float32),
        ],
        compiler_params=pltpu.CompilerParams(vmem_limit_bytes=32 * MIB),
        cost_estimate=SMALL,
        name=name,
    )(*pieces, norm_gain[None], *matrices)


def outer_rows(hops, pieces, taken):
    _, core = place()
    made = taken.shape[1]
    pairs = []
    for i, (hop, piece) in enumerate(zip(hops, pieces)):
        pairs += [(hop, piece.at[pl.ds(core * made, made)]), (hop + 1, taken.at[i])]
    return pairs


def inner_rows(hops, pieces, taken):
    *far, own = pieces
    pairs = [(hop + j, piece.at[j]) for hop, piece in zip(hops, far) for j in range(2)]
    return pairs + [(0, own), (1, taken.at[len(far)])]


def rim_kernel(hops, *refs):
    *pieces, taken, left, right = refs
    for k, piece in outer_rows(hops, pieces, taken):
        part = piece[...]
        left[k] = part[:, 0]
        right[k] = part[:, part.shape[1] - 1]


def rim(hops, pieces, taken):
    _, made, _, channels = taken.shape
    return pl.pallas_call(
        functools.partial(rim_kernel, hops),
        out_shape=[jax.ShapeDtypeStruct((2 * len(hops), made, channels), jnp.bfloat16)] * 2,
        in_specs=[INSIDE] * (len(pieces) + 1),
        out_specs=[INSIDE] * 2,
        compiler_params=pltpu.CompilerParams(vmem_limit_bytes=4 * MIB),
        name="rim",
    )(*pieces, taken)


def filter_kernel(hops, *refs):
    count = len(hops) + 1
    left, right, w_depth, result, outer, inner, out, sems = refs[2 * count :]
    me = lax.axis_index("frm")
    for k, piece in outer_rows(hops, refs[: count - 1], refs[count - 1]):
        outer[me ^ k] = piece[...]
    for k, piece in inner_rows(hops, refs[count : 2 * count - 1], refs[2 * count - 1]):
        inner[me ^ k] = piece[...]
    frames, height, cols, channels = out.shape
    edge = cols // 4
    lanes = 128

    copies = [pltpu.make_async_copy(out.at[frame], result.at[frame], sems.at[frame]) for frame in range(frames)]
    for frame in range(frames):
        for first in range(0, channels, lanes):
            part = pl.ds(first, lanes)
            taps = [[w_depth[a, b, part] for b in range(3)] for a in range(3)]

            def filtered(row):
                sides = outer[row, frame, :, part].astype(jnp.float32)
                between = inner[row, frame, :, part].astype(jnp.float32)
                mid = jnp.concatenate([sides[:edge], between, sides[edge:]], axis=0)
                spot = lax.broadcasted_iota(jnp.int32, mid.shape, 0)
                low = left[me ^ row, frame, part].astype(jnp.float32)[None]
                high = right[me ^ row, frame, part].astype(jnp.float32)[None]
                before = jnp.where(spot == 0, low, pltpu.roll(mid, 1, 0))
                after = jnp.where(spot == cols - 1, high, pltpu.roll(mid, cols - 1, 0))
                return [
                    before * taps[a][0][None] + mid * taps[a][1][None] + after * taps[a][2][None] for a in range(3)
                ]

            above = None
            here = filtered(0)
            for row in range(height):
                below = filtered(row + 1) if row + 1 < height else None
                total = here[1]
                if above is not None:
                    total = total + above[0]
                if below is not None:
                    total = total + below[2]
                out[frame, row, :, part] = total.astype(jnp.bfloat16)
                above, here = here, below
        copies[frame].start()
    for copy in copies:
        copy.wait()


def depth_filter(hops, outer, inner, left, right, w_depth):
    height, frames, channels = left.shape
    widths = [pieces[-1].shape[2] for pieces in (outer, inner)]
    cols = sum(widths)
    size = frames * height * cols * channels
    return pl.pallas_call(
        functools.partial(filter_kernel, hops),
        out_shape=jax.ShapeDtypeStruct((frames, height, cols, channels), jnp.bfloat16),
        in_specs=[INSIDE] * (2 * len(hops) + 5),
        out_specs=pl.BlockSpec(memory_space=pl.ANY),
        scratch_shapes=[
            *[pltpu.VMEM((height, frames, width, channels), jnp.bfloat16) for width in widths],
            pltpu.VMEM((frames, height, cols, channels), jnp.bfloat16),
            pltpu.SemaphoreType.DMA((frames,)),
        ],
        compiler_params=pltpu.CompilerParams(vmem_limit_bytes=10 * MIB),
        cost_estimate=SMALL,
        name="depth_filter",
    )(*outer, *inner, left, right, w_depth)


def local(video, norm_gain, w_query, w_key, w_value, w_out, w_time, w_depth):
    count = lax.axis_size("frm")
    chips = count // 2
    span, height, cols, channels = video.shape
    assert height == count and chips & (chips - 1) == 0 and chips > 1
    made = span // 2
    frames = span * count
    weights = (norm_gain, w_query, w_key, w_value, w_out, w_time)

    def swap(block, k):
        return lax.ppermute(block, "frm", [(i, i ^ k) for i in range(count)]) if k else block

    far = [chips - 1, *([1] if chips > 2 else []), *range(chips - 2, 1, -1)]
    hops = [2 * k for k in [*far, 0]]
    pieces = cut(lambda me: ([me ^ k for k in hops], [me ^ k ^ 1 for k in hops]), chips, video)
    *outer, outer_stack = pieces[: chips + 1]
    *inner, inner_stack = pieces[chips + 1 :]

    def joined(ins, outs):
        *owns, other = ins
        pairs = []
        for i, own in enumerate(owns):
            pairs.append((own, outs[i].at[pl.ds(0, span)]))
            pairs.append((other.at[i], outs[i].at[pl.ds(span, span)]))
        return pairs

    def join(owns, other, name):
        return gather(joined, [*owns[:-1], other], [(2 * span, *other.shape[2:])] * len(far), name)

    outer_other = swap(outer_stack, 1)
    outer_far = join(outer, outer_other, "join_outer")
    *outer_far, inner_stack = lax.optimization_barrier((*outer_far, inner_stack))
    outer_far = [swap(piece, k) for k, piece in zip(hops, outer_far)]
    nearest = far.index(1)
    inner_other = swap(inner_stack, 1)
    inner_far = join(inner, inner_other, "join_inner")
    outer_far[0], *inner_far = lax.optimization_barrier((outer_far[0], *inner_far))
    inner_far = [swap(piece, k) for k, piece in zip(hops, inner_far)]

    def inward(pieces):
        me = lax.axis_index("frm")
        *pieces, own, other = pieces
        pairs = []
        for k, piece in zip(hops, pieces):
            pairs.append((piece.at[pl.ds(0, span)], (me ^ k) * span))
            pairs.append((piece.at[pl.ds(span, span)], (me ^ k ^ 1) * span))
        return pairs + [(own, me * span), (other.at[len(far)], (me ^ 1) * span)]

    outer = list(attend(inward, hops, True, [*outer_far, outer[-1], outer_other], weights, frames, "attend_outer"))
    outer[:2], inner_far[:2] = lax.optimization_barrier((outer[:2], inner_far[:2]))
    for i in range(2, len(far)):
        outer[i], inner_far[i] = lax.optimization_barrier((outer[i], inner_far[i]))
    outer = [swap(piece, k) for k, piece in zip(hops, outer)]
    *keep, give = attend(inward, hops, False, [*inner_far, inner[-1], inner_other], weights, frames, "attend_inner")

    outer[:2], give = lax.optimization_barrier((outer[:2], give))
    taken = swap(give, 1)

    def joined_back(ins, outs):
        *keep, taken = ins
        pairs = []
        for i, own in enumerate(keep):
            pairs += [(own, outs[i].at[0]), (taken.at[i], outs[i].at[1])]
        return pairs

    inner = gather(joined_back, [*keep[:-1], taken], [(2, *taken.shape[1:])] * len(far), "join_back")
    inner = [swap(piece, k) for k, piece in zip(hops, inner)]

    def for_mate(ins, outs):
        _, core = place()
        return [(piece.at[pl.ds((1 - core) * made, made)], outs[0].at[i]) for i, piece in enumerate(ins)]

    (stack,) = gather(for_mate, outer, [(chips, made, *outer[0].shape[1:])], "stack_back")
    halves = swap(stack, 1)
    low_side, high_side = rim(hops, outer, halves)
    low_side, high_side, inner[nearest] = lax.optimization_barrier((low_side, high_side, inner[nearest]))
    line = lax.axis_size("col")
    upward = [(i, i + 1) for i in range(line - 1)]
    left = lax.ppermute(high_side, "col", upward)
    right = lax.ppermute(low_side, "col", [(b, a) for a, b in upward])
    return depth_filter(hops, [*outer, halves], [*inner, keep[-1], taken], left, right, w_depth)


def solution(mesh):
    return jax.shard_map(
        local,
        mesh=mesh,
        in_specs=(P("frm", None, "col", None), P(), P(), P(), P(), P(), P(), P()),
        out_specs=P("frm", None, "col", None),
        check_vma=False,
    )
```

```python
import functools
import math

import jax
import jax.numpy as jnp
from jax import lax
from jax.experimental import pallas as pl
from jax.experimental.pallas import tpu as pltpu
from jax.sharding import PartitionSpec as P

epsilon = 1e-06
GROUP = 8
BLOCKS = 2
TILE = 8
SOFT_ROWS = 32
MIB = 1024 * 1024
SMALL = pl.CostEstimate(flops=1, bytes_accessed=1, transcendentals=0)
INSIDE = pl.BlockSpec(memory_space=pltpu.VMEM)


def place():
    me = lax.axis_index("frm")
    return me // 2, me % 2


def gather_kernel(pairs_of, n_in, *refs):
    for source, target in pairs_of(refs[:n_in], refs[n_in:]):
        target[...] = source[...]


def gather(pairs_of, arrays, shapes, name):
    size = sum(math.prod(shape) for shape in shapes)
    return pl.pallas_call(
        functools.partial(gather_kernel, pairs_of, len(arrays)),
        out_shape=[jax.ShapeDtypeStruct(shape, jnp.bfloat16) for shape in shapes],
        in_specs=[INSIDE] * len(arrays),
        out_specs=[INSIDE] * len(shapes),
        compiler_params=pltpu.CompilerParams(vmem_limit_bytes=6 * MIB),
        cost_estimate=SMALL,
        name=name,
    )(*arrays)


def cut_kernel(rows_of, video, *results):
    edge = video.shape[2] // 4
    half = len(results) // 2
    own, other = rows_of(lax.axis_index("frm"))
    for rim in (True, False):
        *singles, stack = results[:half] if rim else results[half:]
        targets = list(singles) + [stack.at[k] for k in range(stack.shape[0])]
        for row, target in zip(own + other, targets):
            values = video[:, row].astype(jnp.float32)
            if rim:
                values = jnp.concatenate([values[:, :edge], values[:, 3 * edge :]], axis=1)
            else:
                values = values[:, edge : 3 * edge]
            target[...] = values.astype(jnp.bfloat16)


def cut(rows_of, chips, video):
    span, height, cols, channels = video.shape
    shape = (span, cols // 2, channels)
    shapes = ([shape] * chips + [(chips, *shape)]) * 2
    return pl.pallas_call(
        functools.partial(cut_kernel, rows_of),
        out_shape=[jax.ShapeDtypeStruct(shape, jnp.bfloat16) for shape in shapes],
        in_specs=[INSIDE],
        out_specs=[INSIDE] * len(shapes),
        compiler_params=pltpu.CompilerParams(vmem_limit_bytes=12 * MIB),
        cost_estimate=SMALL,
        name="cut",
    )(video)


def groups_of(piece):
    wide = piece[...].astype(jnp.float32)
    return [wide[:, begin : begin + GROUP] for begin in range(0, wide.shape[1], GROUP)]


def normalized(x, gain):
    x = x.reshape(-1, x.shape[-1])
    x = x * lax.rsqrt(jnp.mean(x * x, axis=-1, keepdims=True) + epsilon) * gain
    return x.astype(jnp.bfloat16)


def project_kernel(inward, n_early, n_in, *refs):
    gain, w_query, w_key, w_value, out, normed = refs[n_in:]
    at = 0
    for piece, _ in inward(refs[:n_in])[:n_early]:
        for x in groups_of(piece):
            count = x.shape[0] * GROUP
            normed[at : at + count] = normalized(x, gain[...])
            at += count
    for index, weight in enumerate((w_query, w_key, w_value)):
        out[index] = jnp.dot(normed[...], weight[...], preferred_element_type=jnp.float32).astype(jnp.bfloat16)


def project(inward, n_early, pieces, weights, span):
    cols, channels = pieces[0].shape[-2:]
    rows = n_early * span * cols
    norm_gain, *matrices = weights
    return pl.pallas_call(
        functools.partial(project_kernel, inward, n_early, len(pieces)),
        out_shape=jax.ShapeDtypeStruct((3, rows, channels), jnp.bfloat16),
        in_specs=[INSIDE] * (len(pieces) + 4),
        out_specs=INSIDE,
        scratch_shapes=[pltpu.VMEM((rows, channels), jnp.bfloat16)],
        compiler_params=pltpu.CompilerParams(vmem_limit_bytes=20 * MIB),
        cost_estimate=pl.CostEstimate(
            flops=6 * rows * channels * channels, bytes_accessed=8 * rows * channels, transcendentals=0
        ),
        name="project_early",
    )(*pieces, norm_gain[None], *matrices[:3])


def attend_frames(pieces, early, n_early, gain, bias, weights, normed, projected, attended, mixed):
    w_query, w_key, w_value, w_out, w_time = weights
    groups, frames, _, channels = mixed.shape
    frames = frames - 2
    rows = frames * GROUP
    places = []
    at = 0
    for number, (piece, first) in enumerate(pieces):
        if number == n_early:
            at = 0
        for group, x in enumerate(groups_of(piece)):
            span = x.shape[0]
            count = span * GROUP
            mixed[group, pl.ds(first + 1, span)] = x
            begin = pl.multiple_of(group * rows + first * GROUP, count)
            if number < n_early:
                projected[:, pl.ds(begin, count)] = early[:, at : at + count]
            else:
                normed[at : at + count] = normalized(x, gain)
                places.append((begin, at, count))
            at += count
    for index, weight in enumerate((w_query, w_key, w_value)):
        result = jnp.dot(normed[...], weight[...], preferred_element_type=jnp.float32).astype(jnp.bfloat16)
        for begin, at, count in places:
            projected[index, pl.ds(begin, count)] = result[at : at + count]
    queries, key_proj, values = projected.at[0], projected.at[1], projected.at[2]
    height = rows // BLOCKS
    power = math.log2(math.e) / math.sqrt(channels)
    for group in range(groups):
        first = group * rows
        for block in range(BLOCKS):
            begin = block * height
            span = begin + height
            scores = lax.dot_general(
                queries[first + begin : first + span],
                key_proj[first : first + span],
                (((1,), (1,)), ((), ())),
                preferred_element_type=jnp.float32,
            )
            shares = []
            for low in range(0, height, SOFT_ROWS):
                part = scores[low : low + SOFT_ROWS] + bias[begin + low : begin + low + SOFT_ROWS, :span]
                raised = jnp.exp2((part - jnp.max(part, axis=-1, keepdims=True)) * power)
                scale = 1.0 / jnp.sum(raised, axis=-1, keepdims=True)
                shares.append((raised * scale).astype(jnp.bfloat16))
            attended[first + begin : first + span] = jnp.dot(
                jnp.concatenate(shares, axis=0), values[first : first + span], preferred_element_type=jnp.float32
            ).astype(jnp.bfloat16)
    out = jnp.dot(attended[...], w_out[...], preferred_element_type=jnp.float32).reshape(
        groups, frames, GROUP, channels
    )
    for group in range(groups):
        for first in range(0, frames, TILE):
            x = mixed[group, first + 1 : first + 1 + TILE] + out[group, first : first + TILE]
            mixed[group, first + 1 : first + 1 + TILE] = x
            if first == 0:
                mixed[group, 0] = x[0]
    taps = []
    for tap in range(3):
        parts = []
        for group in range(groups):
            view = mixed[group, tap - tap % 2 : tap - tap % 2 + frames].reshape(frames // 2, 2, GROUP, channels)
            parts.append(view[:, tap % 2].reshape(rows // 2, channels).astype(jnp.bfloat16))
        taps.append(jnp.dot(jnp.concatenate(parts, axis=0), w_time[tap], preferred_element_type=jnp.float32))
    summed = (taps[0] + taps[1]) + taps[2]
    return (summed / (1.0 + jnp.exp(-summed))).reshape(groups, frames // 2, GROUP, channels)


def attend_kernel(inward, hops, paired, n_early, n_in, *refs):
    gain, *weights = refs[n_in : n_in + 6]
    early = refs[n_in + 6] if n_early else None
    *results, done, bias, normed, projected, attended, mixed = refs[n_in + 6 + (n_early > 0) :]
    to_row = lax.broadcasted_iota(jnp.int32, bias.shape, 0)
    from_row = lax.broadcasted_iota(jnp.int32, bias.shape, 1)
    allowed = (from_row <= to_row) & (((from_row ^ to_row) & (GROUP - 1)) == 0)
    bias[...] = jnp.where(allowed, 0.0, -1e30)
    pieces = inward(refs[:n_in])
    made = attend_frames(pieces, early, n_early, gain[...], bias, weights, normed, projected, attended, mixed)
    done[...] = jnp.concatenate([made[g] for g in range(made.shape[0])], axis=1).astype(jnp.bfloat16)
    me = lax.axis_index("frm")
    for i, (hop, result) in enumerate(zip(hops, results)):
        span = result.shape[0]
        if paired:
            result[...] = done[pl.ds((me ^ hop) // 2 * span, span)]
        else:
            result[...] = done[pl.ds((me ^ hop) * span, span)]
            results[-1][i] = done[pl.ds((me ^ hop ^ 1) * span, span)]


def attend(inward, hops, paired, pieces, weights, frames, name, n_early=0, early=()):
    cols, channels = pieces[0].shape[-2:]
    rows = frames * cols
    made = frames // 2
    size = made // (2 * len(hops))
    shapes = [(2 * size if paired else size, cols, channels)] * len(hops)
    if not paired:
        shapes.append((len(hops), size, cols, channels))
    norm_gain, *matrices = weights
    return pl.pallas_call(
        functools.partial(attend_kernel, inward, hops, paired, n_early, len(pieces)),
        out_shape=[jax.ShapeDtypeStruct(shape, jnp.bfloat16) for shape in shapes],
        in_specs=[INSIDE] * (len(pieces) + 6 + len(early)),
        out_specs=[INSIDE] * len(shapes),
        scratch_shapes=[
            pltpu.VMEM((made, cols, channels), jnp.bfloat16),
            pltpu.VMEM((frames * GROUP, frames * GROUP), jnp.float32),
            pltpu.VMEM((rows - rows * n_early // (2 * len(hops)), channels), jnp.bfloat16),
            pltpu.VMEM((3, rows, channels), jnp.bfloat16),
            pltpu.VMEM((rows, channels), jnp.bfloat16),
            pltpu.VMEM((cols // GROUP, frames + 2, GROUP, channels), jnp.float32),
        ],
        compiler_params=pltpu.CompilerParams(vmem_limit_bytes=24 * MIB),
        cost_estimate=SMALL,
        name=name,
    )(*pieces, norm_gain[None], *matrices, *early)


def outer_rows(hops, pieces, taken):
    _, core = place()
    made = taken.shape[1]
    pairs = []
    for i, (hop, piece) in enumerate(zip(hops, pieces)):
        pairs += [(hop, piece.at[pl.ds(core * made, made)]), (hop + 1, taken.at[i])]
    return pairs


def inner_rows(hops, pieces, taken):
    *far, own = pieces
    pairs = [(hop + j, piece.at[j]) for hop, piece in zip(hops, far) for j in range(2)]
    return pairs + [(0, own), (1, taken.at[len(far)])]


def rim_kernel(hops, *refs):
    *pieces, taken, left, right = refs
    for k, piece in outer_rows(hops, pieces, taken):
        part = piece[...]
        left[k] = part[:, 0]
        right[k] = part[:, part.shape[1] - 1]


def rim(hops, pieces, taken):
    _, made, _, channels = taken.shape
    return pl.pallas_call(
        functools.partial(rim_kernel, hops),
        out_shape=[jax.ShapeDtypeStruct((2 * len(hops), made, channels), jnp.bfloat16)] * 2,
        in_specs=[INSIDE] * (len(pieces) + 1),
        out_specs=[INSIDE] * 2,
        compiler_params=pltpu.CompilerParams(vmem_limit_bytes=4 * MIB),
        name="rim",
    )(*pieces, taken)


def filter_kernel(hops, *refs):
    count = len(hops) + 1
    left, right, w_depth, result, outer, inner, out, sems = refs[2 * count :]
    me = lax.axis_index("frm")
    for k, piece in outer_rows(hops, refs[: count - 1], refs[count - 1]):
        outer[me ^ k] = piece[...]
    for k, piece in inner_rows(hops, refs[count : 2 * count - 1], refs[2 * count - 1]):
        inner[me ^ k] = piece[...]
    frames, height, cols, channels = out.shape
    edge = cols // 4
    lanes = 128

    copies = [pltpu.make_async_copy(out.at[frame], result.at[frame], sems.at[frame]) for frame in range(frames)]
    for frame in range(frames):
        for first in range(0, channels, lanes):
            part = pl.ds(first, lanes)
            taps = [[w_depth[a, b, part] for b in range(3)] for a in range(3)]

            def filtered(row):
                sides = outer[row, frame, :, part].astype(jnp.float32)
                between = inner[row, frame, :, part].astype(jnp.float32)
                mid = jnp.concatenate([sides[:edge], between, sides[edge:]], axis=0)
                spot = lax.broadcasted_iota(jnp.int32, mid.shape, 0)
                low = left[me ^ row, frame, part].astype(jnp.float32)[None]
                high = right[me ^ row, frame, part].astype(jnp.float32)[None]
                before = jnp.where(spot == 0, low, pltpu.roll(mid, 1, 0))
                after = jnp.where(spot == cols - 1, high, pltpu.roll(mid, cols - 1, 0))
                return [
                    before * taps[a][0][None] + mid * taps[a][1][None] + after * taps[a][2][None] for a in range(3)
                ]

            above = None
            here = filtered(0)
            for row in range(height):
                below = filtered(row + 1) if row + 1 < height else None
                total = here[1]
                if above is not None:
                    total = total + above[0]
                if below is not None:
                    total = total + below[2]
                out[frame, row, :, part] = total.astype(jnp.bfloat16)
                above, here = here, below
        copies[frame].start()
    for copy in copies:
        copy.wait()


def depth_filter(hops, outer, inner, left, right, w_depth):
    height, frames, channels = left.shape
    width = inner[-1].shape[2]
    cols = 2 * width
    size = frames * height * cols * channels
    return pl.pallas_call(
        functools.partial(filter_kernel, hops),
        out_shape=jax.ShapeDtypeStruct((frames, height, cols, channels), jnp.bfloat16),
        in_specs=[INSIDE] * (2 * len(hops) + 5),
        out_specs=pl.BlockSpec(memory_space=pl.ANY),
        scratch_shapes=[
            *[pltpu.VMEM((height, frames, width, channels), jnp.bfloat16)] * 2,
            pltpu.VMEM((frames, height, cols, channels), jnp.bfloat16),
            pltpu.SemaphoreType.DMA((frames,)),
        ],
        compiler_params=pltpu.CompilerParams(vmem_limit_bytes=10 * MIB),
        cost_estimate=SMALL,
        name="depth_filter",
    )(*outer, *inner, left, right, w_depth)


def local(video, norm_gain, w_query, w_key, w_value, w_out, w_time, w_depth):
    count = lax.axis_size("frm")
    chips = count // 2
    span, height, cols, channels = video.shape
    assert height == count and chips & (chips - 1) == 0 and chips > 1
    made = span // 2
    frames = span * count
    width = cols // 2
    weights = (norm_gain, w_query, w_key, w_value, w_out, w_time)

    def swap(block, k):
        return lax.ppermute(block, "frm", [(i, i ^ k) for i in range(count)]) if k else block

    far = [chips - 1, *([1] if chips > 2 else []), *range(chips - 2, 1, -1)]
    hops = [2 * k for k in [*far, 0]]
    pieces = cut(lambda me: ([me ^ k for k in hops], [me ^ k ^ 1 for k in hops]), chips, video)
    *outer, outer_stack = pieces[: chips + 1]
    *inner, inner_stack = pieces[chips + 1 :]

    def joined(ins, outs):
        *owns, other = ins
        pairs = []
        for i, own in enumerate(owns):
            pairs.append((own, outs[i].at[pl.ds(0, span)]))
            pairs.append((other.at[i], outs[i].at[pl.ds(span, span)]))
        return pairs

    def join(owns, other, name):
        return gather(joined, [*owns[:-1], other], [(2 * span, width, channels)] * len(far), name)

    outer_other = swap(outer_stack, 1)
    outer_far = join(outer, outer_other, "join_outer")
    *outer_far, inner_stack = lax.optimization_barrier((*outer_far, inner_stack))
    outer_far = [swap(piece, k) for k, piece in zip(hops, outer_far)]
    nearest = far.index(1)
    inner_other = swap(inner_stack, 1)
    inner_far = join(inner, inner_other, "join_inner")
    outer_far[0], *inner_far = lax.optimization_barrier((outer_far[0], *inner_far))
    inner_far = [swap(piece, k) for k, piece in zip(hops, inner_far)]

    late = list(range(2, len(far))) or [len(far) - 1]
    soon = [i for i in range(len(far)) if i not in late]
    n_early = 2 * len(soon) + 2

    def inward(pieces):
        me = lax.axis_index("frm")
        *pieces, own, other = pieces

        def halves(numbers):
            return [
                (pieces[i].at[pl.ds(j * span, span)], (me ^ hops[i] ^ j) * span) for i in numbers for j in range(2)
            ]

        return [(own, me * span), (other.at[len(far)], (me ^ 1) * span), *halves(soon), *halves(late)]

    def inward_soon(pieces):
        *pieces, own, other = pieces
        blocks = [pieces[i].at[pl.ds(j * span, span)] for i in range(len(soon)) for j in range(2)]
        return [(block, None) for block in [own, other.at[len(far)], *blocks]]

    outer = list(attend(inward, hops, True, [*outer_far, outer[-1], outer_other], weights, frames, "attend_outer"))
    near = [inner[-1], inner_other]
    early = project(inward_soon, n_early, [*[inner_far[i] for i in soon], *near], weights, span)
    outer[:2], early = lax.optimization_barrier((outer[:2], early))
    for i in range(2, len(far)):
        outer[i], inner_far[i] = lax.optimization_barrier((outer[i], inner_far[i]))
    outer = [swap(piece, k) for k, piece in zip(hops, outer)]
    *keep, give = attend(
        inward, hops, False, [*inner_far, *near], weights, frames, "attend_inner", n_early, [early]
    )

    outer[:2], give = lax.optimization_barrier((outer[:2], give))
    taken = swap(give, 1)

    def joined_back(ins, outs):
        *keep, taken = ins
        pairs = []
        for i, own in enumerate(keep):
            pairs += [(own, outs[i].at[0]), (taken.at[i], outs[i].at[1])]
        return pairs

    inner = gather(joined_back, [*keep[:-1], taken], [(2, made, width, channels)] * len(far), "join_back")
    inner = [swap(piece, k) for k, piece in zip(hops, inner)]

    def for_mate(ins, outs):
        _, core = place()
        return [(piece.at[pl.ds((1 - core) * made, made)], outs[0].at[i]) for i, piece in enumerate(ins)]

    (stack,) = gather(for_mate, outer, [(chips, made, width, channels)], "stack_back")
    halves = swap(stack, 1)
    low_side, high_side = rim(hops, outer, halves)
    low_side, high_side, inner[nearest] = lax.optimization_barrier((low_side, high_side, inner[nearest]))
    line = lax.axis_size("col")
    upward = [(i, i + 1) for i in range(line - 1)]
    left = lax.ppermute(high_side, "col", upward)
    right = lax.ppermute(low_side, "col", [(b, a) for a, b in upward])
    return depth_filter(hops, [*outer, halves], [*inner, keep[-1], taken], left, right, w_depth)


def solution(mesh):
    return jax.shard_map(
        local,
        mesh=mesh,
        in_specs=(P("frm", None, "col", None), P(), P(), P(), P(), P(), P(), P()),
        out_specs=P("frm", None, "col", None),
        check_vma=False,
    )
```

```python
import functools
import math

import jax
import jax.numpy as jnp
from jax import lax
from jax.experimental import pallas as pl
from jax.experimental.pallas import tpu as pltpu
from jax.sharding import PartitionSpec as P

epsilon = 1e-06
GROUP = 8
BLOCKS = 2
TILE = 8
SOFT_ROWS = 32
MIB = 1024 * 1024
SMALL = pl.CostEstimate(flops=1, bytes_accessed=1, transcendentals=0)
INSIDE = pl.BlockSpec(memory_space=pltpu.VMEM)


def place():
    me = lax.axis_index("frm")
    return me // 2, me % 2


def gather_kernel(pairs_of, n_in, *refs):
    for source, target in pairs_of(refs[:n_in], refs[n_in:]):
        target[...] = source[...]


def gather(pairs_of, arrays, shapes, name):
    size = sum(math.prod(shape) for shape in shapes)
    return pl.pallas_call(
        functools.partial(gather_kernel, pairs_of, len(arrays)),
        out_shape=[jax.ShapeDtypeStruct(shape, jnp.bfloat16) for shape in shapes],
        in_specs=[INSIDE] * len(arrays),
        out_specs=[INSIDE] * len(shapes),
        compiler_params=pltpu.CompilerParams(vmem_limit_bytes=6 * MIB),
        cost_estimate=SMALL,
        name=name,
    )(*arrays)


def cut_kernel(rows_of, video, *results):
    edge = video.shape[2] // 4
    half = len(results) // 2
    own, other = rows_of(lax.axis_index("frm"))
    for rim in (True, False):
        *singles, stack = results[:half] if rim else results[half:]
        targets = list(singles) + [stack.at[k] for k in range(stack.shape[0])]
        for row, target in zip(own + other, targets):
            values = video[:, row].astype(jnp.float32)
            if rim:
                values = jnp.concatenate([values[:, :edge], values[:, 3 * edge :]], axis=1)
            else:
                values = values[:, edge : 3 * edge]
            target[...] = values.astype(jnp.bfloat16)


def cut(rows_of, chips, video):
    span, height, cols, channels = video.shape
    shape = (span, cols // 2, channels)
    shapes = ([shape] * chips + [(chips, *shape)]) * 2
    return pl.pallas_call(
        functools.partial(cut_kernel, rows_of),
        out_shape=[jax.ShapeDtypeStruct(shape, jnp.bfloat16) for shape in shapes],
        in_specs=[INSIDE],
        out_specs=[INSIDE] * len(shapes),
        compiler_params=pltpu.CompilerParams(vmem_limit_bytes=12 * MIB),
        cost_estimate=SMALL,
        name="cut",
    )(video)


def groups_of(piece):
    wide = piece[...].astype(jnp.float32)
    return [wide[:, begin : begin + GROUP] for begin in range(0, wide.shape[1], GROUP)]


def normalized(x, gain):
    x = x.reshape(-1, x.shape[-1])
    x = x * lax.rsqrt(jnp.mean(x * x, axis=-1, keepdims=True) + epsilon) * gain
    return x.astype(jnp.bfloat16)


def project_kernel(inward, n_early, n_in, *refs):
    gain, w_query, w_key, w_value, out, normed = refs[n_in:]
    at = 0
    for piece, _ in inward(refs[:n_in])[:n_early]:
        for x in groups_of(piece):
            count = x.shape[0] * GROUP
            normed[at : at + count] = normalized(x, gain[...])
            at += count
    for index, weight in enumerate((w_query, w_key, w_value)):
        out[index] = jnp.dot(normed[...], weight[...], preferred_element_type=jnp.float32).astype(jnp.bfloat16)


def project(inward, n_early, pieces, weights, span):
    cols, channels = pieces[0].shape[-2:]
    rows = n_early * span * cols
    norm_gain, *matrices = weights
    return pl.pallas_call(
        functools.partial(project_kernel, inward, n_early, len(pieces)),
        out_shape=jax.ShapeDtypeStruct((3, rows, channels), jnp.bfloat16),
        in_specs=[INSIDE] * (len(pieces) + 4),
        out_specs=INSIDE,
        scratch_shapes=[pltpu.VMEM((rows, channels), jnp.bfloat16)],
        compiler_params=pltpu.CompilerParams(vmem_limit_bytes=20 * MIB),
        cost_estimate=pl.CostEstimate(
            flops=6 * rows * channels * channels, bytes_accessed=8 * rows * channels, transcendentals=0
        ),
        name="project_early",
    )(*pieces, norm_gain[None], *matrices[:3])


def attend_frames(pieces, early, n_early, gain, bias, weights, normed, projected, attended, mixed):
    w_query, w_key, w_value, w_out, w_time = weights
    groups, frames, _, channels = mixed.shape
    frames = frames - 2
    rows = frames * GROUP
    places = []
    at = 0
    for number, (piece, first) in enumerate(pieces):
        if number == n_early:
            at = 0
        for group, x in enumerate(groups_of(piece)):
            span = x.shape[0]
            count = span * GROUP
            mixed[group, pl.ds(first + 1, span)] = x
            begin = pl.multiple_of(group * rows + first * GROUP, count)
            if number < n_early:
                projected[:, pl.ds(begin, count)] = early[:, at : at + count]
            else:
                normed[at : at + count] = normalized(x, gain)
                places.append((begin, at, count))
            at += count
    for index, weight in enumerate((w_query, w_key, w_value)):
        result = jnp.dot(normed[...], weight[...], preferred_element_type=jnp.float32).astype(jnp.bfloat16)
        for begin, at, count in places:
            projected[index, pl.ds(begin, count)] = result[at : at + count]
    queries, key_proj, values = projected.at[0], projected.at[1], projected.at[2]
    height = rows // BLOCKS
    power = math.log2(math.e) / math.sqrt(channels)
    for group in range(groups):
        first = group * rows
        for block in range(BLOCKS):
            begin = block * height
            span = begin + height
            scores = lax.dot_general(
                queries[first + begin : first + span],
                key_proj[first : first + span],
                (((1,), (1,)), ((), ())),
                preferred_element_type=jnp.float32,
            )
            shares = []
            for low in range(0, height, SOFT_ROWS):
                part = scores[low : low + SOFT_ROWS] + bias[begin + low : begin + low + SOFT_ROWS, :span]
                raised = jnp.exp2((part - jnp.max(part, axis=-1, keepdims=True)) * power)
                scale = 1.0 / jnp.sum(raised, axis=-1, keepdims=True)
                shares.append((raised * scale).astype(jnp.bfloat16))
            attended[first + begin : first + span] = jnp.dot(
                jnp.concatenate(shares, axis=0), values[first : first + span], preferred_element_type=jnp.float32
            ).astype(jnp.bfloat16)
    out = jnp.dot(attended[...], w_out[...], preferred_element_type=jnp.float32).reshape(
        groups, frames, GROUP, channels
    )
    for group in range(groups):
        for first in range(0, frames, TILE):
            x = mixed[group, first + 1 : first + 1 + TILE] + out[group, first : first + TILE]
            mixed[group, first + 1 : first + 1 + TILE] = x
            if first == 0:
                mixed[group, 0] = x[0]
    taps = []
    for tap in range(3):
        parts = []
        for group in range(groups):
            view = mixed[group, tap - tap % 2 : tap - tap % 2 + frames].reshape(frames // 2, 2, GROUP, channels)
            parts.append(view[:, tap % 2].reshape(rows // 2, channels).astype(jnp.bfloat16))
        taps.append(jnp.dot(jnp.concatenate(parts, axis=0), w_time[tap], preferred_element_type=jnp.float32))
    summed = (taps[0] + taps[1]) + taps[2]
    return (summed / (1.0 + jnp.exp(-summed))).reshape(groups, frames // 2, GROUP, channels)


def attend_kernel(inward, hops, paired, n_early, n_in, *refs):
    gain, *weights = refs[n_in : n_in + 6]
    early = refs[n_in + 6] if n_early else None
    *results, done, bias, normed, projected, attended, mixed = refs[n_in + 6 + (n_early > 0) :]
    to_row = lax.broadcasted_iota(jnp.int32, bias.shape, 0)
    from_row = lax.broadcasted_iota(jnp.int32, bias.shape, 1)
    allowed = (from_row <= to_row) & (((from_row ^ to_row) & (GROUP - 1)) == 0)
    bias[...] = jnp.where(allowed, 0.0, -1e30)
    pieces = inward(refs[:n_in])
    made = attend_frames(pieces, early, n_early, gain[...], bias, weights, normed, projected, attended, mixed)
    done[...] = jnp.concatenate([made[g] for g in range(made.shape[0])], axis=1).astype(jnp.bfloat16)
    me = lax.axis_index("frm")
    for i, (hop, result) in enumerate(zip(hops, results)):
        span = result.shape[0]
        if paired:
            result[...] = done[pl.ds((me ^ hop) // 2 * span, span)]
        else:
            result[...] = done[pl.ds((me ^ hop) * span, span)]
            results[-1][i] = done[pl.ds((me ^ hop ^ 1) * span, span)]


def attend(inward, hops, paired, pieces, weights, frames, name, n_early=0, early=()):
    cols, channels = pieces[0].shape[-2:]
    rows = frames * cols
    made = frames // 2
    size = made // (2 * len(hops))
    shapes = [(2 * size if paired else size, cols, channels)] * len(hops)
    if not paired:
        shapes.append((len(hops), size, cols, channels))
    norm_gain, *matrices = weights
    return pl.pallas_call(
        functools.partial(attend_kernel, inward, hops, paired, n_early, len(pieces)),
        out_shape=[jax.ShapeDtypeStruct(shape, jnp.bfloat16) for shape in shapes],
        in_specs=[INSIDE] * (len(pieces) + 6 + len(early)),
        out_specs=[INSIDE] * len(shapes),
        scratch_shapes=[
            pltpu.VMEM((made, cols, channels), jnp.bfloat16),
            pltpu.VMEM((frames * GROUP, frames * GROUP), jnp.float32),
            pltpu.VMEM((rows - rows * n_early // (2 * len(hops)), channels), jnp.bfloat16),
            pltpu.VMEM((3, rows, channels), jnp.bfloat16),
            pltpu.VMEM((rows, channels), jnp.bfloat16),
            pltpu.VMEM((cols // GROUP, frames + 2, GROUP, channels), jnp.float32),
        ],
        compiler_params=pltpu.CompilerParams(vmem_limit_bytes=24 * MIB),
        cost_estimate=SMALL,
        name=name,
    )(*pieces, norm_gain[None], *matrices, *early)


def outer_rows(hops, pieces, taken):
    _, core = place()
    made = taken.shape[1]
    pairs = []
    for i, (hop, piece) in enumerate(zip(hops, pieces)):
        pairs += [(hop, piece.at[pl.ds(core * made, made)]), (hop + 1, taken.at[i])]
    return pairs


def inner_rows(hops, pieces, taken):
    *far, own = pieces
    pairs = [(hop + j, piece.at[j]) for hop, piece in zip(hops, far) for j in range(2)]
    return pairs + [(0, own), (1, taken.at[len(far)])]


def rim_kernel(hops, *refs):
    *pieces, taken, left, right = refs
    for k, piece in outer_rows(hops, pieces, taken):
        part = piece[...]
        left[k] = part[:, 0]
        right[k] = part[:, part.shape[1] - 1]


def rim(hops, pieces, taken):
    _, made, _, channels = taken.shape
    return pl.pallas_call(
        functools.partial(rim_kernel, hops),
        out_shape=[jax.ShapeDtypeStruct((2 * len(hops), made, channels), jnp.bfloat16)] * 2,
        in_specs=[INSIDE] * (len(pieces) + 1),
        out_specs=[INSIDE] * 2,
        compiler_params=pltpu.CompilerParams(vmem_limit_bytes=4 * MIB),
        name="rim",
    )(*pieces, taken)


def filter_kernel(hops, *refs):
    count = len(hops) + 1
    left, right, w_depth, result, outer, inner, out, sems = refs[2 * count :]
    me = lax.axis_index("frm")
    for k, piece in outer_rows(hops, refs[: count - 1], refs[count - 1]):
        outer[me ^ k] = piece[...]
    for k, piece in inner_rows(hops, refs[count : 2 * count - 1], refs[2 * count - 1]):
        inner[me ^ k] = piece[...]
    frames, height, cols, channels = out.shape
    edge = cols // 4
    lanes = 128

    copies = [pltpu.make_async_copy(out.at[frame], result.at[frame], sems.at[frame]) for frame in range(frames)]
    for frame in range(frames):
        for first in range(0, channels, lanes):
            part = pl.ds(first, lanes)
            taps = [[w_depth[a, b, part] for b in range(3)] for a in range(3)]

            def filtered(row):
                sides = outer[row, frame, :, part].astype(jnp.float32)
                between = inner[row, frame, :, part].astype(jnp.float32)
                mid = jnp.concatenate([sides[:edge], between, sides[edge:]], axis=0)
                spot = lax.broadcasted_iota(jnp.int32, mid.shape, 0)
                low = left[me ^ row, frame, part].astype(jnp.float32)[None]
                high = right[me ^ row, frame, part].astype(jnp.float32)[None]
                before = jnp.where(spot == 0, low, pltpu.roll(mid, 1, 0))
                after = jnp.where(spot == cols - 1, high, pltpu.roll(mid, cols - 1, 0))
                return [
                    before * taps[a][0][None] + mid * taps[a][1][None] + after * taps[a][2][None] for a in range(3)
                ]

            above = None
            here = filtered(0)
            for row in range(height):
                below = filtered(row + 1) if row + 1 < height else None
                total = here[1]
                if above is not None:
                    total = total + above[0]
                if below is not None:
                    total = total + below[2]
                out[frame, row, :, part] = total.astype(jnp.bfloat16)
                above, here = here, below
        copies[frame].start()
    for copy in copies:
        copy.wait()


def depth_filter(hops, outer, inner, left, right, w_depth):
    height, frames, channels = left.shape
    width = inner[-1].shape[2]
    cols = 2 * width
    size = frames * height * cols * channels
    return pl.pallas_call(
        functools.partial(filter_kernel, hops),
        out_shape=jax.ShapeDtypeStruct((frames, height, cols, channels), jnp.bfloat16),
        in_specs=[INSIDE] * (2 * len(hops) + 5),
        out_specs=pl.BlockSpec(memory_space=pl.ANY),
        scratch_shapes=[
            *[pltpu.VMEM((height, frames, width, channels), jnp.bfloat16)] * 2,
            pltpu.VMEM((frames, height, cols, channels), jnp.bfloat16),
            pltpu.SemaphoreType.DMA((frames,)),
        ],
        compiler_params=pltpu.CompilerParams(vmem_limit_bytes=10 * MIB),
        cost_estimate=SMALL,
        name="depth_filter",
    )(*outer, *inner, left, right, w_depth)


def local(video, norm_gain, w_query, w_key, w_value, w_out, w_time, w_depth):
    count = lax.axis_size("frm")
    chips = count // 2
    span, height, cols, channels = video.shape
    assert height == count and chips & (chips - 1) == 0 and chips > 1
    made = span // 2
    frames = span * count
    width = cols // 2
    weights = (norm_gain, w_query, w_key, w_value, w_out, w_time)

    def swap(block, k):
        return lax.ppermute(block, "frm", [(i, i ^ k) for i in range(count)]) if k else block

    far = [chips - 1, *([1] if chips > 2 else []), *range(chips - 2, 1, -1)]
    hops = [2 * k for k in [*far, 0]]
    pieces = cut(lambda me: ([me ^ k for k in hops], [me ^ k ^ 1 for k in hops]), chips, video)
    *outer, outer_stack = pieces[: chips + 1]
    *inner, inner_stack = pieces[chips + 1 :]

    def joined(ins, outs):
        *owns, other = ins
        pairs = []
        for i, own in enumerate(owns):
            pairs.append((own, outs[i].at[pl.ds(0, span)]))
            pairs.append((other.at[i], outs[i].at[pl.ds(span, span)]))
        return pairs

    def join(owns, other, name):
        return gather(joined, [*owns[:-1], other], [(2 * span, width, channels)] * len(far), name)

    outer_other = swap(outer_stack, 1)
    outer_far = join(outer, outer_other, "join_outer")
    *outer_far, inner_stack = lax.optimization_barrier((*outer_far, inner_stack))
    outer_far = [swap(piece, k) for k, piece in zip(hops, outer_far)]
    inner_other = swap(inner_stack, 1)
    inner_far = join(inner, inner_other, "join_inner")
    outer_far[0], *inner_far = lax.optimization_barrier((outer_far[0], *inner_far))
    inner_far = [swap(piece, k) for k, piece in zip(hops, inner_far)]

    late = list(range(2, len(far))) or [len(far) - 1]
    soon = [i for i in range(len(far)) if i not in late]
    n_early = 2 * len(soon) + 2

    def inward(pieces):
        me = lax.axis_index("frm")
        *pieces, own, other = pieces

        def halves(numbers):
            return [
                (pieces[i].at[pl.ds(j * span, span)], (me ^ hops[i] ^ j) * span) for i in numbers for j in range(2)
            ]

        return [(own, me * span), (other.at[len(far)], (me ^ 1) * span), *halves(soon), *halves(late)]

    def inward_soon(pieces):
        *pieces, own, other = pieces
        blocks = [pieces[i].at[pl.ds(j * span, span)] for i in range(len(soon)) for j in range(2)]
        return [(block, None) for block in [own, other.at[len(far)], *blocks]]

    outer = list(attend(inward, hops, True, [*outer_far, outer[-1], outer_other], weights, frames, "attend_outer"))
    near = [inner[-1], inner_other]
    early = project(inward_soon, n_early, [*[inner_far[i] for i in soon], *near], weights, span)
    outer[:2], early = lax.optimization_barrier((outer[:2], early))
    for i in range(2, len(far)):
        outer[i], inner_far[i] = lax.optimization_barrier((outer[i], inner_far[i]))
    outer = [swap(piece, k) for k, piece in zip(hops, outer)]
    *keep, give = attend(
        inward, hops, False, [*inner_far, *near], weights, frames, "attend_inner", n_early, [early]
    )

    outer[:2], give = lax.optimization_barrier((outer[:2], give))
    taken = swap(give, 1)

    def joined_back(ins, outs):
        *keep, taken = ins
        pairs = []
        for i, own in enumerate(keep):
            pairs += [(own, outs[i].at[0]), (taken.at[i], outs[i].at[1])]
        return pairs

    inner = gather(joined_back, [*keep[:-1], taken], [(2, made, width, channels)] * len(far), "join_back")
    inner = [swap(piece, k) for k, piece in zip(hops, inner)]

    def for_mate(ins, outs):
        _, core = place()
        return [(piece.at[pl.ds((1 - core) * made, made)], outs[0].at[i]) for i, piece in enumerate(ins)]

    (stack,) = gather(for_mate, outer, [(chips, made, width, channels)], "stack_back")
    halves = swap(stack, 1)
    low_side, high_side = rim(hops, outer, halves)
    line = lax.axis_size("col")
    upward = [(i, i + 1) for i in range(line - 1)]
    left = lax.ppermute(high_side, "col", upward)
    right = lax.ppermute(low_side, "col", [(b, a) for a, b in upward])
    return depth_filter(hops, [*outer, halves], [*inner, keep[-1], taken], left, right, w_depth)


def solution(mesh):
    return jax.shard_map(
        local,
        mesh=mesh,
        in_specs=(P("frm", None, "col", None), P(), P(), P(), P(), P(), P(), P()),
        out_specs=P("frm", None, "col", None),
        check_vma=False,
    )
```

```python
import functools
import math

import jax
import jax.numpy as jnp
from jax import lax
from jax.experimental import pallas as pl
from jax.experimental.pallas import tpu as pltpu
from jax.sharding import PartitionSpec as P

epsilon = 1e-06
GROUP = 8
BLOCKS = 2
TILE = 8
SOFT_ROWS = 32
MIB = 1024 * 1024
SMALL = pl.CostEstimate(flops=1, bytes_accessed=1, transcendentals=0)
INSIDE = pl.BlockSpec(memory_space=pltpu.VMEM)


def place():
    me = lax.axis_index("frm")
    return me // 2, me % 2


def gather_kernel(pairs_of, n_in, *refs):
    for source, target in pairs_of(refs[:n_in], refs[n_in:]):
        target[...] = source[...]


def gather(pairs_of, arrays, shapes, name):
    size = sum(math.prod(shape) for shape in shapes)
    return pl.pallas_call(
        functools.partial(gather_kernel, pairs_of, len(arrays)),
        out_shape=[jax.ShapeDtypeStruct(shape, jnp.bfloat16) for shape in shapes],
        in_specs=[INSIDE] * len(arrays),
        out_specs=[INSIDE] * len(shapes),
        compiler_params=pltpu.CompilerParams(vmem_limit_bytes=6 * MIB),
        cost_estimate=SMALL,
        name=name,
    )(*arrays)


def cut_kernel(rows_of, video, *results):
    edge = video.shape[2] // 4
    half = len(results) // 2
    own, other = rows_of(lax.axis_index("frm"))
    for rim in (True, False):
        *singles, stack = results[:half] if rim else results[half:]
        targets = list(singles) + [stack.at[k] for k in range(stack.shape[0])]
        for row, target in zip(own + other, targets):
            values = video[:, row].astype(jnp.float32)
            if rim:
                values = jnp.concatenate([values[:, :edge], values[:, 3 * edge :]], axis=1)
            else:
                values = values[:, edge : 3 * edge]
            target[...] = values.astype(jnp.bfloat16)


def cut(rows_of, chips, video):
    span, height, cols, channels = video.shape
    shape = (span, cols // 2, channels)
    shapes = ([shape] * chips + [(chips, *shape)]) * 2
    return pl.pallas_call(
        functools.partial(cut_kernel, rows_of),
        out_shape=[jax.ShapeDtypeStruct(shape, jnp.bfloat16) for shape in shapes],
        in_specs=[INSIDE],
        out_specs=[INSIDE] * len(shapes),
        compiler_params=pltpu.CompilerParams(vmem_limit_bytes=12 * MIB),
        cost_estimate=SMALL,
        name="cut",
    )(video)


def groups_of(piece):
    wide = piece[...].astype(jnp.float32)
    return [wide[:, begin : begin + GROUP] for begin in range(0, wide.shape[1], GROUP)]


def normalized(x, gain):
    x = x.reshape(-1, x.shape[-1])
    x = x * lax.rsqrt(jnp.mean(x * x, axis=-1, keepdims=True) + epsilon) * gain
    return x.astype(jnp.bfloat16)


def project_kernel(inward, n_early, n_in, *refs):
    gain, w_query, w_key, w_value, out, normed = refs[n_in:]
    at = 0
    for piece, _ in inward(refs[:n_in])[:n_early]:
        for x in groups_of(piece):
            count = x.shape[0] * GROUP
            normed[at : at + count] = normalized(x, gain[...])
            at += count
    for index, weight in enumerate((w_query, w_key, w_value)):
        out[index] = jnp.dot(normed[...], weight[...], preferred_element_type=jnp.float32).astype(jnp.bfloat16)


def project(inward, n_early, pieces, weights, span):
    cols, channels = pieces[0].shape[-2:]
    rows = n_early * span * cols
    norm_gain, *matrices = weights
    return pl.pallas_call(
        functools.partial(project_kernel, inward, n_early, len(pieces)),
        out_shape=jax.ShapeDtypeStruct((3, rows, channels), jnp.bfloat16),
        in_specs=[INSIDE] * (len(pieces) + 4),
        out_specs=INSIDE,
        scratch_shapes=[pltpu.VMEM((rows, channels), jnp.bfloat16)],
        compiler_params=pltpu.CompilerParams(vmem_limit_bytes=20 * MIB),
        cost_estimate=pl.CostEstimate(
            flops=6 * rows * channels * channels, bytes_accessed=8 * rows * channels, transcendentals=0
        ),
        name="project_early",
    )(*pieces, norm_gain[None], *matrices[:3])


def attend_frames(pieces, early, n_early, gain, bias, weights, normed, projected, attended, mixed):
    w_query, w_key, w_value, w_out, w_time = weights
    groups, frames, _, channels = mixed.shape
    frames = frames - 2
    rows = frames * GROUP
    places = []
    at = 0
    for number, (piece, first) in enumerate(pieces):
        if number == n_early:
            at = 0
        for group, x in enumerate(groups_of(piece)):
            span = x.shape[0]
            count = span * GROUP
            mixed[group, pl.ds(first + 1, span)] = x
            begin = pl.multiple_of(group * rows + first * GROUP, count)
            if number < n_early:
                projected[:, pl.ds(begin, count)] = early[:, at : at + count]
            else:
                normed[at : at + count] = normalized(x, gain)
                places.append((begin, at, count))
            at += count
    for index, weight in enumerate((w_query, w_key, w_value)):
        result = jnp.dot(normed[...], weight[...], preferred_element_type=jnp.float32).astype(jnp.bfloat16)
        for begin, at, count in places:
            projected[index, pl.ds(begin, count)] = result[at : at + count]
    queries, key_proj, values = projected.at[0], projected.at[1], projected.at[2]
    height = rows // BLOCKS
    power = math.log2(math.e) / math.sqrt(channels)
    for group in range(groups):
        first = group * rows
        for block in range(BLOCKS):
            begin = block * height
            span = begin + height
            scores = lax.dot_general(
                queries[first + begin : first + span],
                key_proj[first : first + span],
                (((1,), (1,)), ((), ())),
                preferred_element_type=jnp.float32,
            )
            shares = []
            for low in range(0, height, SOFT_ROWS):
                part = scores[low : low + SOFT_ROWS] + bias[begin + low : begin + low + SOFT_ROWS, :span]
                raised = jnp.exp2((part - jnp.max(part, axis=-1, keepdims=True)) * power)
                scale = 1.0 / jnp.sum(raised, axis=-1, keepdims=True)
                shares.append((raised * scale).astype(jnp.bfloat16))
            attended[first + begin : first + span] = jnp.dot(
                jnp.concatenate(shares, axis=0), values[first : first + span], preferred_element_type=jnp.float32
            ).astype(jnp.bfloat16)
    out = jnp.dot(attended[...], w_out[...], preferred_element_type=jnp.float32).reshape(
        groups, frames, GROUP, channels
    )
    for group in range(groups):
        for first in range(0, frames, TILE):
            x = mixed[group, first + 1 : first + 1 + TILE] + out[group, first : first + TILE]
            mixed[group, first + 1 : first + 1 + TILE] = x
            if first == 0:
                mixed[group, 0] = x[0]
    taps = []
    for tap in range(3):
        parts = []
        for group in range(groups):
            view = mixed[group, tap - tap % 2 : tap - tap % 2 + frames].reshape(frames // 2, 2, GROUP, channels)
            parts.append(view[:, tap % 2].reshape(rows // 2, channels).astype(jnp.bfloat16))
        taps.append(jnp.dot(jnp.concatenate(parts, axis=0), w_time[tap], preferred_element_type=jnp.float32))
    summed = (taps[0] + taps[1]) + taps[2]
    return (summed / (1.0 + jnp.exp(-summed))).reshape(groups, frames // 2, GROUP, channels)


def attend_kernel(inward, hops, paired, n_early, n_in, *refs):
    gain, *weights = refs[n_in : n_in + 6]
    early = refs[n_in + 6] if n_early else None
    *results, done, bias, normed, projected, attended, mixed = refs[n_in + 6 + (n_early > 0) :]
    to_row = lax.broadcasted_iota(jnp.int32, bias.shape, 0)
    from_row = lax.broadcasted_iota(jnp.int32, bias.shape, 1)
    allowed = (from_row <= to_row) & (((from_row ^ to_row) & (GROUP - 1)) == 0)
    bias[...] = jnp.where(allowed, 0.0, -1e30)
    pieces = inward(refs[:n_in])
    made = attend_frames(pieces, early, n_early, gain[...], bias, weights, normed, projected, attended, mixed)
    done[...] = jnp.concatenate([made[g] for g in range(made.shape[0])], axis=1).astype(jnp.bfloat16)
    me = lax.axis_index("frm")
    for i, (hop, result) in enumerate(zip(hops, results)):
        span = result.shape[0]
        if paired:
            result[...] = done[pl.ds((me ^ hop) // 2 * span, span)]
        else:
            result[...] = done[pl.ds((me ^ hop) * span, span)]
            results[-1][i] = done[pl.ds((me ^ hop ^ 1) * span, span)]


def attend(inward, hops, paired, pieces, weights, frames, name, n_early=0, early=()):
    cols, channels = pieces[0].shape[-2:]
    rows = frames * cols
    made = frames // 2
    size = made // (2 * len(hops))
    shapes = [(2 * size if paired else size, cols, channels)] * len(hops)
    if not paired:
        shapes.append((len(hops), size, cols, channels))
    norm_gain, *matrices = weights
    return pl.pallas_call(
        functools.partial(attend_kernel, inward, hops, paired, n_early, len(pieces)),
        out_shape=[jax.ShapeDtypeStruct(shape, jnp.bfloat16) for shape in shapes],
        in_specs=[INSIDE] * (len(pieces) + 6 + len(early)),
        out_specs=[INSIDE] * len(shapes),
        scratch_shapes=[
            pltpu.VMEM((made, cols, channels), jnp.bfloat16),
            pltpu.VMEM((frames * GROUP, frames * GROUP), jnp.float32),
            pltpu.VMEM((rows - rows * n_early // (2 * len(hops)), channels), jnp.bfloat16),
            pltpu.VMEM((3, rows, channels), jnp.bfloat16),
            pltpu.VMEM((rows, channels), jnp.bfloat16),
            pltpu.VMEM((cols // GROUP, frames + 2, GROUP, channels), jnp.float32),
        ],
        compiler_params=pltpu.CompilerParams(vmem_limit_bytes=24 * MIB),
        cost_estimate=SMALL,
        name=name,
    )(*pieces, norm_gain[None], *matrices, *early)


def outer_rows(hops, pieces, taken):
    _, core = place()
    made = taken.shape[1]
    pairs = []
    for i, (hop, piece) in enumerate(zip(hops, pieces)):
        pairs += [(hop, piece.at[pl.ds(core * made, made)]), (hop + 1, taken.at[i])]
    return pairs


def inner_rows(hops, pieces, taken):
    *far, own = pieces
    pairs = [(hop + j, piece.at[j]) for hop, piece in zip(hops, far) for j in range(2)]
    return pairs + [(0, own), (1, taken.at[len(far)])]


def rim_kernel(hops, *refs):
    *pieces, taken, left, right = refs
    for k, piece in outer_rows(hops, pieces, taken):
        part = piece[...]
        left[k] = part[:, 0]
        right[k] = part[:, part.shape[1] - 1]


def rim(hops, pieces, taken):
    _, made, _, channels = taken.shape
    return pl.pallas_call(
        functools.partial(rim_kernel, hops),
        out_shape=[jax.ShapeDtypeStruct((2 * len(hops), made, channels), jnp.bfloat16)] * 2,
        in_specs=[INSIDE] * (len(pieces) + 1),
        out_specs=[INSIDE] * 2,
        compiler_params=pltpu.CompilerParams(vmem_limit_bytes=4 * MIB),
        name="rim",
    )(*pieces, taken)


def filter_kernel(hops, *refs):
    count = len(hops) + 1
    left, right, w_depth, result, outer, inner, out, sems = refs[2 * count :]
    me = lax.axis_index("frm")
    for k, piece in outer_rows(hops, refs[: count - 1], refs[count - 1]):
        outer[me ^ k] = piece[...]
    for k, piece in inner_rows(hops, refs[count : 2 * count - 1], refs[2 * count - 1]):
        inner[me ^ k] = piece[...]
    frames, height, cols, channels = out.shape
    edge = cols // 4
    lanes = 128

    copies = [pltpu.make_async_copy(out.at[frame], result.at[frame], sems.at[frame]) for frame in range(frames)]
    for frame in range(frames):
        for first in range(0, channels, lanes):
            part = pl.ds(first, lanes)
            taps = [[w_depth[a, b, part] for b in range(3)] for a in range(3)]

            def filtered(row):
                sides = outer[row, frame, :, part].astype(jnp.float32)
                between = inner[row, frame, :, part].astype(jnp.float32)
                mid = jnp.concatenate([sides[:edge], between, sides[edge:]], axis=0)
                spot = lax.broadcasted_iota(jnp.int32, mid.shape, 0)
                low = left[me ^ row, frame, part].astype(jnp.float32)[None]
                high = right[me ^ row, frame, part].astype(jnp.float32)[None]
                before = jnp.where(spot == 0, low, pltpu.roll(mid, 1, 0))
                after = jnp.where(spot == cols - 1, high, pltpu.roll(mid, cols - 1, 0))
                return [
                    before * taps[a][0][None] + mid * taps[a][1][None] + after * taps[a][2][None] for a in range(3)
                ]

            above = None
            here = filtered(0)
            for row in range(height):
                below = filtered(row + 1) if row + 1 < height else None
                total = here[1]
                if above is not None:
                    total = total + above[0]
                if below is not None:
                    total = total + below[2]
                out[frame, row, :, part] = total.astype(jnp.bfloat16)
                above, here = here, below
        copies[frame].start()
    for copy in copies:
        copy.wait()


def depth_filter(hops, outer, inner, left, right, w_depth):
    height, frames, channels = left.shape
    width = inner[-1].shape[2]
    cols = 2 * width
    size = frames * height * cols * channels
    return pl.pallas_call(
        functools.partial(filter_kernel, hops),
        out_shape=jax.ShapeDtypeStruct((frames, height, cols, channels), jnp.bfloat16),
        in_specs=[INSIDE] * (2 * len(hops) + 5),
        out_specs=pl.BlockSpec(memory_space=pl.ANY),
        scratch_shapes=[
            *[pltpu.VMEM((height, frames, width, channels), jnp.bfloat16)] * 2,
            pltpu.VMEM((frames, height, cols, channels), jnp.bfloat16),
            pltpu.SemaphoreType.DMA((frames,)),
        ],
        compiler_params=pltpu.CompilerParams(vmem_limit_bytes=10 * MIB),
        cost_estimate=SMALL,
        name="depth_filter",
    )(*outer, *inner, left, right, w_depth)


def local(video, norm_gain, w_query, w_key, w_value, w_out, w_time, w_depth):
    count = lax.axis_size("frm")
    chips = count // 2
    span, height, cols, channels = video.shape
    assert height == count and chips & (chips - 1) == 0 and chips > 1
    made = span // 2
    frames = span * count
    width = cols // 2
    weights = (norm_gain, w_query, w_key, w_value, w_out, w_time)

    def swap(block, k):
        return lax.ppermute(block, "frm", [(i, i ^ k) for i in range(count)]) if k else block

    far = [chips - 1, *([1] if chips > 2 else []), *range(chips - 2, 1, -1)]
    hops = [2 * k for k in [*far, 0]]
    pieces = cut(lambda me: ([me ^ k for k in hops], [me ^ k ^ 1 for k in hops]), chips, video)
    *outer, outer_stack = pieces[: chips + 1]
    *inner, inner_stack = pieces[chips + 1 :]

    def joined(ins, outs):
        *owns, other = ins
        pairs = []
        for i, own in enumerate(owns):
            pairs.append((own, outs[i].at[pl.ds(0, span)]))
            pairs.append((other.at[i], outs[i].at[pl.ds(span, span)]))
        return pairs

    def join(owns, other, name):
        return gather(joined, [*owns[:-1], other], [(2 * span, width, channels)] * len(far), name)

    outer_other = swap(outer_stack, 1)
    outer_far = join(outer, outer_other, "join_outer")
    *outer_far, inner_stack = lax.optimization_barrier((*outer_far, inner_stack))
    outer_far = [swap(piece, k) for k, piece in zip(hops, outer_far)]
    inner_other = swap(inner_stack, 1)
    inner_far = join(inner, inner_other, "join_inner")
    outer_far[0], *inner_far = lax.optimization_barrier((outer_far[0], *inner_far))
    inner_far = [swap(piece, k) for k, piece in zip(hops, inner_far)]

    late = list(range(2, len(far))) or [len(far) - 1]
    soon = [i for i in range(len(far)) if i not in late]
    n_early = 2 * len(soon) + 2

    def inward(pieces):
        me = lax.axis_index("frm")
        *pieces, own, other = pieces

        def halves(numbers):
            return [
                (pieces[i].at[pl.ds(j * span, span)], (me ^ hops[i] ^ j) * span) for i in numbers for j in range(2)
            ]

        return [(own, me * span), (other.at[len(far)], (me ^ 1) * span), *halves(soon), *halves(late)]

    def inward_soon(pieces):
        *pieces, own, other = pieces
        blocks = [pieces[i].at[pl.ds(j * span, span)] for i in range(len(soon)) for j in range(2)]
        return [(block, None) for block in [own, other.at[len(far)], *blocks]]

    outer = list(attend(inward, hops, True, [*outer_far, outer[-1], outer_other], weights, frames, "attend_outer"))
    near = [inner[-1], inner_other]
    early = project(inward_soon, n_early, [*[inner_far[i] for i in soon], *near], weights, span)
    outer, early = lax.optimization_barrier((outer, early))
    outer = [swap(piece, k) for k, piece in zip(hops, outer)]
    *keep, give = attend(
        inward, hops, False, [*inner_far, *near], weights, frames, "attend_inner", n_early, [early]
    )

    outer[:2], give = lax.optimization_barrier((outer[:2], give))
    taken = swap(give, 1)

    def joined_back(ins, outs):
        *keep, taken = ins
        pairs = []
        for i, own in enumerate(keep):
            pairs += [(own, outs[i].at[0]), (taken.at[i], outs[i].at[1])]
        return pairs

    inner = gather(joined_back, [*keep[:-1], taken], [(2, made, width, channels)] * len(far), "join_back")
    inner = [swap(piece, k) for k, piece in zip(hops, inner)]

    def for_mate(ins, outs):
        _, core = place()
        return [(piece.at[pl.ds((1 - core) * made, made)], outs[0].at[i]) for i, piece in enumerate(ins)]

    (stack,) = gather(for_mate, outer, [(chips, made, width, channels)], "stack_back")
    halves = swap(stack, 1)
    low_side, high_side = rim(hops, outer, halves)
    line = lax.axis_size("col")
    upward = [(i, i + 1) for i in range(line - 1)]
    left = lax.ppermute(high_side, "col", upward)
    right = lax.ppermute(low_side, "col", [(b, a) for a, b in upward])
    return depth_filter(hops, [*outer, halves], [*inner, keep[-1], taken], left, right, w_depth)


def solution(mesh):
    return jax.shard_map(
        local,
        mesh=mesh,
        in_specs=(P("frm", None, "col", None), P(), P(), P(), P(), P(), P(), P()),
        out_specs=P("frm", None, "col", None),
        check_vma=False,
    )
```

```python
import functools
import math

import jax
import jax.numpy as jnp
from jax import lax
from jax.experimental import pallas as pl
from jax.experimental.pallas import tpu as pltpu
from jax.sharding import PartitionSpec as P

epsilon = 1e-06
GROUP = 8
BLOCKS = 2
TILE = 8
SOFT_ROWS = 32
MIB = 1024 * 1024
SMALL = pl.CostEstimate(flops=1, bytes_accessed=1, transcendentals=0)
INSIDE = pl.BlockSpec(memory_space=pltpu.VMEM)


def place():
    me = lax.axis_index("frm")
    return me // 2, me % 2


def gather_kernel(pairs_of, n_in, *refs):
    for source, target in pairs_of(refs[:n_in], refs[n_in:]):
        target[...] = source[...]


def gather(pairs_of, arrays, shapes, name):
    size = sum(math.prod(shape) for shape in shapes)
    return pl.pallas_call(
        functools.partial(gather_kernel, pairs_of, len(arrays)),
        out_shape=[jax.ShapeDtypeStruct(shape, jnp.bfloat16) for shape in shapes],
        in_specs=[INSIDE] * len(arrays),
        out_specs=[INSIDE] * len(shapes),
        compiler_params=pltpu.CompilerParams(vmem_limit_bytes=6 * MIB),
        cost_estimate=SMALL,
        name=name,
    )(*arrays)


def cut_kernel(rows_of, video, *results):
    edge = video.shape[2] // 4
    half = len(results) // 2
    own, other = rows_of(lax.axis_index("frm"))
    for rim in (True, False):
        *singles, stack = results[:half] if rim else results[half:]
        targets = list(singles) + [stack.at[k] for k in range(stack.shape[0])]
        for row, target in zip(own + other, targets):
            values = video[:, row].astype(jnp.float32)
            if rim:
                values = jnp.concatenate([values[:, :edge], values[:, 3 * edge :]], axis=1)
            else:
                values = values[:, edge : 3 * edge]
            target[...] = values.astype(jnp.bfloat16)


def cut(rows_of, chips, video):
    span, height, cols, channels = video.shape
    shape = (span, cols // 2, channels)
    shapes = ([shape] * chips + [(chips, *shape)]) * 2
    return pl.pallas_call(
        functools.partial(cut_kernel, rows_of),
        out_shape=[jax.ShapeDtypeStruct(shape, jnp.bfloat16) for shape in shapes],
        in_specs=[INSIDE],
        out_specs=[INSIDE] * len(shapes),
        compiler_params=pltpu.CompilerParams(vmem_limit_bytes=12 * MIB),
        cost_estimate=SMALL,
        name="cut",
    )(video)


def groups_of(piece):
    wide = piece[...].astype(jnp.float32)
    return [wide[:, begin : begin + GROUP] for begin in range(0, wide.shape[1], GROUP)]


def normalized(x, gain):
    x = x.reshape(-1, x.shape[-1])
    x = x * lax.rsqrt(jnp.mean(x * x, axis=-1, keepdims=True) + epsilon) * gain
    return x.astype(jnp.bfloat16)


def project_kernel(inward, n_early, n_in, *refs):
    gain, w_query, w_key, w_value, out, normed = refs[n_in:]
    at = 0
    for piece, _ in inward(refs[:n_in])[:n_early]:
        for x in groups_of(piece):
            count = x.shape[0] * GROUP
            normed[at : at + count] = normalized(x, gain[...])
            at += count
    for index, weight in enumerate((w_query, w_key, w_value)):
        out[index] = jnp.dot(normed[...], weight[...], preferred_element_type=jnp.float32).astype(jnp.bfloat16)


def project(inward, n_early, pieces, weights, span):
    cols, channels = pieces[0].shape[-2:]
    rows = n_early * span * cols
    norm_gain, *matrices = weights
    return pl.pallas_call(
        functools.partial(project_kernel, inward, n_early, len(pieces)),
        out_shape=jax.ShapeDtypeStruct((3, rows, channels), jnp.bfloat16),
        in_specs=[INSIDE] * (len(pieces) + 4),
        out_specs=INSIDE,
        scratch_shapes=[pltpu.VMEM((rows, channels), jnp.bfloat16)],
        compiler_params=pltpu.CompilerParams(vmem_limit_bytes=20 * MIB),
        cost_estimate=pl.CostEstimate(
            flops=6 * rows * channels * channels, bytes_accessed=8 * rows * channels, transcendentals=0
        ),
        name="project_early",
    )(*pieces, norm_gain[None], *matrices[:3])


def attend_frames(pieces, early, n_early, gain, bias, weights, normed, projected, attended, mixed):
    w_query, w_key, w_value, w_out, w_time = weights
    groups, frames, _, channels = mixed.shape
    frames = frames - 2
    rows = frames * GROUP
    places = []
    at = 0
    for number, (piece, first) in enumerate(pieces):
        if number == n_early:
            at = 0
        for group, x in enumerate(groups_of(piece)):
            span = x.shape[0]
            count = span * GROUP
            mixed[group, pl.ds(first + 1, span)] = x
            begin = pl.multiple_of(group * rows + first * GROUP, count)
            if number < n_early:
                projected[:, pl.ds(begin, count)] = early[:, at : at + count]
            else:
                normed[at : at + count] = normalized(x, gain)
                places.append((begin, at, count))
            at += count
    for index, weight in enumerate((w_query, w_key, w_value)):
        result = jnp.dot(normed[...], weight[...], preferred_element_type=jnp.float32).astype(jnp.bfloat16)
        for begin, at, count in places:
            projected[index, pl.ds(begin, count)] = result[at : at + count]
    queries, key_proj, values = projected.at[0], projected.at[1], projected.at[2]
    height = rows // BLOCKS
    power = math.log2(math.e) / math.sqrt(channels)
    for group in range(groups):
        first = group * rows
        for block in range(BLOCKS):
            begin = block * height
            span = begin + height
            scores = lax.dot_general(
                queries[first + begin : first + span],
                key_proj[first : first + span],
                (((1,), (1,)), ((), ())),
                preferred_element_type=jnp.float32,
            )
            shares = []
            for low in range(0, height, SOFT_ROWS):
                part = scores[low : low + SOFT_ROWS] + bias[begin + low : begin + low + SOFT_ROWS, :span]
                raised = jnp.exp2((part - jnp.max(part, axis=-1, keepdims=True)) * power)
                scale = 1.0 / jnp.sum(raised, axis=-1, keepdims=True)
                shares.append((raised * scale).astype(jnp.bfloat16))
            attended[first + begin : first + span] = jnp.dot(
                jnp.concatenate(shares, axis=0), values[first : first + span], preferred_element_type=jnp.float32
            ).astype(jnp.bfloat16)
    out = jnp.dot(attended[...], w_out[...], preferred_element_type=jnp.float32).reshape(
        groups, frames, GROUP, channels
    )
    for group in range(groups):
        for first in range(0, frames, TILE):
            x = mixed[group, first + 1 : first + 1 + TILE] + out[group, first : first + TILE]
            mixed[group, first + 1 : first + 1 + TILE] = x
            if first == 0:
                mixed[group, 0] = x[0]
    taps = []
    for tap in range(3):
        parts = []
        for group in range(groups):
            view = mixed[group, tap - tap % 2 : tap - tap % 2 + frames].reshape(frames // 2, 2, GROUP, channels)
            parts.append(view[:, tap % 2].reshape(rows // 2, channels).astype(jnp.bfloat16))
        taps.append(jnp.dot(jnp.concatenate(parts, axis=0), w_time[tap], preferred_element_type=jnp.float32))
    summed = (taps[0] + taps[1]) + taps[2]
    return (summed / (1.0 + jnp.exp(-summed))).reshape(groups, frames // 2, GROUP, channels)


def attend_kernel(inward, hops, paired, n_early, n_in, *refs):
    gain, *weights = refs[n_in : n_in + 6]
    early = refs[n_in + 6] if n_early else None
    *results, done, bias, normed, projected, attended, mixed = refs[n_in + 6 + (n_early > 0) :]
    to_row = lax.broadcasted_iota(jnp.int32, bias.shape, 0)
    from_row = lax.broadcasted_iota(jnp.int32, bias.shape, 1)
    allowed = (from_row <= to_row) & (((from_row ^ to_row) & (GROUP - 1)) == 0)
    bias[...] = jnp.where(allowed, 0.0, -1e30)
    pieces = inward(refs[:n_in])
    made = attend_frames(pieces, early, n_early, gain[...], bias, weights, normed, projected, attended, mixed)
    done[...] = jnp.concatenate([made[g] for g in range(made.shape[0])], axis=1).astype(jnp.bfloat16)
    me = lax.axis_index("frm")
    for i, (hop, result) in enumerate(zip(hops, results)):
        span = result.shape[0]
        if paired:
            result[...] = done[pl.ds((me ^ hop) // 2 * span, span)]
        else:
            result[...] = done[pl.ds((me ^ hop) * span, span)]
            results[-1][i] = done[pl.ds((me ^ hop ^ 1) * span, span)]


def attend(inward, hops, paired, pieces, weights, frames, name, n_early=0, early=()):
    cols, channels = pieces[0].shape[-2:]
    rows = frames * cols
    made = frames // 2
    size = made // (2 * len(hops))
    shapes = [(2 * size if paired else size, cols, channels)] * len(hops)
    if not paired:
        shapes.append((len(hops), size, cols, channels))
    norm_gain, *matrices = weights
    return pl.pallas_call(
        functools.partial(attend_kernel, inward, hops, paired, n_early, len(pieces)),
        out_shape=[jax.ShapeDtypeStruct(shape, jnp.bfloat16) for shape in shapes],
        in_specs=[INSIDE] * (len(pieces) + 6 + len(early)),
        out_specs=[INSIDE] * len(shapes),
        scratch_shapes=[
            pltpu.VMEM((made, cols, channels), jnp.bfloat16),
            pltpu.VMEM((frames * GROUP, frames * GROUP), jnp.float32),
            pltpu.VMEM((rows - rows * n_early // (2 * len(hops)), channels), jnp.bfloat16),
            pltpu.VMEM((3, rows, channels), jnp.bfloat16),
            pltpu.VMEM((rows, channels), jnp.bfloat16),
            pltpu.VMEM((cols // GROUP, frames + 2, GROUP, channels), jnp.float32),
        ],
        compiler_params=pltpu.CompilerParams(vmem_limit_bytes=24 * MIB),
        cost_estimate=SMALL,
        name=name,
    )(*pieces, norm_gain[None], *matrices, *early)


def outer_rows(hops, pieces, taken):
    _, core = place()
    made = taken.shape[1]
    pairs = []
    for i, (hop, piece) in enumerate(zip(hops, pieces)):
        pairs += [(hop, piece.at[pl.ds(core * made, made)]), (hop + 1, taken.at[i])]
    return pairs


def inner_rows(hops, pieces, taken):
    *far, own = pieces
    pairs = [(hop + j, piece.at[j]) for hop, piece in zip(hops, far) for j in range(2)]
    return pairs + [(0, own), (1, taken.at[len(far)])]


def rim_kernel(hops, *refs):
    *pieces, taken, left, right = refs
    for k, piece in outer_rows(hops, pieces, taken):
        part = piece[...]
        left[k] = part[:, 0]
        right[k] = part[:, part.shape[1] - 1]


def rim(hops, pieces, taken):
    _, made, _, channels = taken.shape
    return pl.pallas_call(
        functools.partial(rim_kernel, hops),
        out_shape=[jax.ShapeDtypeStruct((2 * len(hops), made, channels), jnp.bfloat16)] * 2,
        in_specs=[INSIDE] * (len(pieces) + 1),
        out_specs=[INSIDE] * 2,
        compiler_params=pltpu.CompilerParams(vmem_limit_bytes=4 * MIB),
        name="rim",
    )(*pieces, taken)


def filter_kernel(hops, back, *refs):
    count = len(hops) + 1
    left, right, w_depth, result, outer, inner, out, sems = refs[2 * count :]
    me = lax.axis_index("frm")
    for k, piece in outer_rows(hops, refs[: count - 1], refs[count - 1]):
        outer[me ^ k] = piece[...]
    for k, piece in inner_rows(back, refs[count : 2 * count - 1], refs[2 * count - 1]):
        inner[me ^ k] = piece[...]
    frames, height, cols, channels = out.shape
    edge = cols // 4
    lanes = 128

    copies = [pltpu.make_async_copy(out.at[frame], result.at[frame], sems.at[frame]) for frame in range(frames)]
    for frame in range(frames):
        for first in range(0, channels, lanes):
            part = pl.ds(first, lanes)
            taps = [[w_depth[a, b, part] for b in range(3)] for a in range(3)]

            def filtered(row):
                sides = outer[row, frame, :, part].astype(jnp.float32)
                between = inner[row, frame, :, part].astype(jnp.float32)
                mid = jnp.concatenate([sides[:edge], between, sides[edge:]], axis=0)
                spot = lax.broadcasted_iota(jnp.int32, mid.shape, 0)
                low = left[me ^ row, frame, part].astype(jnp.float32)[None]
                high = right[me ^ row, frame, part].astype(jnp.float32)[None]
                before = jnp.where(spot == 0, low, pltpu.roll(mid, 1, 0))
                after = jnp.where(spot == cols - 1, high, pltpu.roll(mid, cols - 1, 0))
                return [
                    before * taps[a][0][None] + mid * taps[a][1][None] + after * taps[a][2][None] for a in range(3)
                ]

            above = None
            here = filtered(0)
            for row in range(height):
                below = filtered(row + 1) if row + 1 < height else None
                total = here[1]
                if above is not None:
                    total = total + above[0]
                if below is not None:
                    total = total + below[2]
                out[frame, row, :, part] = total.astype(jnp.bfloat16)
                above, here = here, below
        copies[frame].start()
    for copy in copies:
        copy.wait()


def depth_filter(hops, back, outer, inner, left, right, w_depth):
    height, frames, channels = left.shape
    width = inner[-1].shape[2]
    cols = 2 * width
    size = frames * height * cols * channels
    return pl.pallas_call(
        functools.partial(filter_kernel, hops, back),
        out_shape=jax.ShapeDtypeStruct((frames, height, cols, channels), jnp.bfloat16),
        in_specs=[INSIDE] * (2 * len(hops) + 5),
        out_specs=pl.BlockSpec(memory_space=pl.ANY),
        scratch_shapes=[
            *[pltpu.VMEM((height, frames, width, channels), jnp.bfloat16)] * 2,
            pltpu.VMEM((frames, height, cols, channels), jnp.bfloat16),
            pltpu.SemaphoreType.DMA((frames,)),
        ],
        compiler_params=pltpu.CompilerParams(vmem_limit_bytes=10 * MIB),
        cost_estimate=SMALL,
        name="depth_filter",
    )(*outer, *inner, left, right, w_depth)


def local(video, norm_gain, w_query, w_key, w_value, w_out, w_time, w_depth):
    count = lax.axis_size("frm")
    chips = count // 2
    span, height, cols, channels = video.shape
    assert height == count and chips & (chips - 1) == 0 and chips > 1
    made = span // 2
    frames = span * count
    width = cols // 2
    weights = (norm_gain, w_query, w_key, w_value, w_out, w_time)

    def swap(block, k):
        return lax.ppermute(block, "frm", [(i, i ^ k) for i in range(count)]) if k else block

    far = [chips - 1, *([1] if chips > 2 else []), *range(chips - 2, 1, -1)]
    hops = [2 * k for k in [*far, 0]]
    pieces = cut(lambda me: ([me ^ k for k in hops], [me ^ k ^ 1 for k in hops]), chips, video)
    *outer, outer_stack = pieces[: chips + 1]
    *inner, inner_stack = pieces[chips + 1 :]

    def joined(ins, outs):
        *owns, other = ins
        pairs = []
        for i, own in enumerate(owns):
            pairs.append((own, outs[i].at[pl.ds(0, span)]))
            pairs.append((other.at[i], outs[i].at[pl.ds(span, span)]))
        return pairs

    def join(owns, other, name):
        return gather(joined, [*owns[:-1], other], [(2 * span, width, channels)] * len(far), name)

    outer_other = swap(outer_stack, 1)
    outer_far = join(outer, outer_other, "join_outer")
    *outer_far, inner_stack = lax.optimization_barrier((*outer_far, inner_stack))
    outer_far = [swap(piece, k) for k, piece in zip(hops, outer_far)]
    inner_other = swap(inner_stack, 1)
    inner_far = join(inner, inner_other, "join_inner")
    outer_far[0], *inner_far = lax.optimization_barrier((outer_far[0], *inner_far))
    inner_far = [swap(piece, k) for k, piece in zip(hops, inner_far)]

    late = list(range(2, len(far))) or [len(far) - 1]
    soon = [i for i in range(len(far)) if i not in late]
    n_early = 2 * len(soon) + 2

    def inward(pieces):
        me = lax.axis_index("frm")
        *pieces, own, other = pieces

        def halves(numbers):
            return [
                (pieces[i].at[pl.ds(j * span, span)], (me ^ hops[i] ^ j) * span) for i in numbers for j in range(2)
            ]

        return [(own, me * span), (other.at[len(far)], (me ^ 1) * span), *halves(soon), *halves(late)]

    def inward_soon(pieces):
        *pieces, own, other = pieces
        blocks = [pieces[i].at[pl.ds(j * span, span)] for i in range(len(soon)) for j in range(2)]
        return [(block, None) for block in [own, other.at[len(far)], *blocks]]

    outer = list(attend(inward, hops, True, [*outer_far, outer[-1], outer_other], weights, frames, "attend_outer"))
    near = [inner[-1], inner_other]
    early = project(inward_soon, n_early, [*[inner_far[i] for i in soon], *near], weights, span)
    outer[:2], early = lax.optimization_barrier((outer[:2], early))
    for i in range(2, len(far)):
        outer[i], inner_far[i] = lax.optimization_barrier((outer[i], inner_far[i]))
    outer = [swap(piece, k) for k, piece in zip(hops, outer)]
    *keep, give = attend(
        inward, hops, False, [*inner_far, *near], weights, frames, "attend_inner", n_early, [early]
    )

    outer[:2], give = lax.optimization_barrier((outer[:2], give))
    taken = swap(give, 1)

    def joined_back(ins, outs):
        *keep, taken = ins
        pairs = []
        for i, own in enumerate(keep):
            pairs += [(own, outs[i].at[0]), (taken.at[i], outs[i].at[1])]
        return pairs

    inner = gather(joined_back, [*keep[:-1], taken], [(2, made, width, channels)] * len(far), "join_back")
    turn = sorted(range(len(far)), key=lambda i: far[i] == 1)
    back = [hops[i] for i in turn] + [0]
    inner = [swap(inner[i], hops[i]) for i in turn]

    def for_mate(ins, outs):
        _, core = place()
        return [(piece.at[pl.ds((1 - core) * made, made)], outs[0].at[i]) for i, piece in enumerate(ins)]

    (stack,) = gather(for_mate, outer, [(chips, made, width, channels)], "stack_back")
    halves = swap(stack, 1)
    low_side, high_side = rim(hops, outer, halves)
    line = lax.axis_size("col")
    upward = [(i, i + 1) for i in range(line - 1)]
    left = lax.ppermute(high_side, "col", upward)
    right = lax.ppermute(low_side, "col", [(b, a) for a, b in upward])
    return depth_filter(hops, back, [*outer, halves], [*inner, keep[-1], taken], left, right, w_depth)


def solution(mesh):
    return jax.shard_map(
        local,
        mesh=mesh,
        in_specs=(P("frm", None, "col", None), P(), P(), P(), P(), P(), P(), P()),
        out_specs=P("frm", None, "col", None),
        check_vma=False,
    )
```
